32 devices in a mesh: member: 4 (over x, core), lat: 8 (over z, y).
Axes of the slice: x: 2, y: 2, z: 4, core: 2. Of those that a mesh axis runs over, the one named last changes fastest.
Arguments:
- velocity: bfloat16 [8, 8, 1024, 2048], P('member', None, 'lat'), may hold values from -6 to 6
- tracer: bfloat16 [8, 8, 1024, 2048], P('member', None, 'lat'), may hold values from -6 to 6
- wave_slots: int32 [704], replicated, may hold values from 0 to 703, each once
- parents: int32 [8], replicated, may hold values from 0 to 7, as said below
- noise: bfloat16 [704, 8, 2, 8, 683], P('lat', 'member'), may hold values from -4 to 4
Outputs:
- child_spectra: bfloat16 [704, 8, 2, 8, 683], P('lat', 'member')
- child_fourier: bfloat16 [704, 8, 2, 8, 1024], P('lat', 'member')
The draws below stay inside these ranges and needn't reach their ends.
Inputs may be any that keep to these rules, and one draw needn't show every extreme that they name: `wave_slots`: each number below 683 stands in exactly one slot; a slot holding 683 or more is empty. `parents`: the parent of child i lies within 2 of i, and some child's parent is exactly 2 above it.
All inputs are finite; a program needn't handle non-finite values.
Results may differ from the reference program's by a relative error of at most 0.008.
Values may be sent and summed in bfloat16 or wider, within the bound.
No kernel may reach another device: no remote copies, remote signals or barrier semaphores. Data moves between devices by JAX's collectives and lax.ppermute only.
A program may use at most 128 MiB of HBM per device.

```python
import math
import jax
import jax.numpy as jnp
from jax import lax

NLAT = 1024
NLON = 2048
TRUNC = 683
FIELDS = 8
SPREAD = 2
MEM_DEV = 2
MEMBERS = 8
MPAD = 704


def draw_parents(key, part):
    index = jnp.arange(MEMBERS, dtype=jnp.int32)
    position = index % MEM_DEV
    offsets = jax.random.randint(jax.random.fold_in(key, 11), (MEMBERS,), -SPREAD, SPREAD + 1)
    below = jax.random.randint(jax.random.fold_in(key, 12), (MEMBERS,), -SPREAD, 0)
    above = jax.random.randint(jax.random.fold_in(key, 13), (MEMBERS,), 1, SPREAD + 1)
    first_child = (position == 0) & (index >= MEM_DEV)
    last_child = (position == MEM_DEV - 1) & (index < MEMBERS - MEM_DEV)
    offsets = jnp.where(first_child, below, offsets)
    offsets = jnp.where(last_child, above, offsets)
    offsets = jnp.where(index == MEM_DEV - 1, SPREAD, offsets)
    return jnp.clip(index + offsets, 0, MEMBERS - 1).astype(jnp.int32)


def steps_of(key, shape, shards, least, top_value):
    factor_of = 1.0
    for axis_at, parts in shards:
        draws = jax.random.uniform(jax.random.fold_in(jax.random.fold_in(key, 6), axis_at), (parts,), jnp.float32, least / len(shards), top_value / len(shards))
        factor_of = factor_of * jnp.repeat(jnp.exp(draws), shape[axis_at] // parts).reshape((-1,) + (1,) * (len(shape) - 1 - axis_at))
    return factor_of


def normal_values(key, shape, scale, bound, cuts=(), held_as=jnp.bfloat16):
    values = jax.random.normal(key, shape, jnp.float32) * scale
    if len(cuts) > 0:
        values = steps_of(key, shape, cuts, -0.22, 0.18) * values
    return jnp.clip(values, min=-bound, max=bound).astype(held_as)


def setup_inputs(seed: int = 0) -> dict:
    key_list = jax.random.split(jax.random.key(seed), 6)
    return {
        "velocity": normal_values(key_list[0], (MEMBERS, FIELDS, NLAT, NLON), 1.0, 6.0, ((0, 4), (2, 8))),
        "tracer": normal_values(key_list[1], (MEMBERS, FIELDS, NLAT, NLON), 1.0, 6.0, ((0, 4), (2, 8))),
        "wave_slots": jax.random.permutation(key_list[2], MPAD).astype(jnp.int32),
        "parents": draw_parents(jax.random.fold_in(key_list[5], 71), 0),
        "noise": normal_values(key_list[4], (MPAD, MEMBERS, 2, FIELDS, TRUNC), 0.5, 4.0, ((0, 8), (1, 4))),
    }


def zonal_table(wavenumbers):
    longitude = jnp.arange(NLON, dtype=jnp.int32)
    active = (wavenumbers < TRUNC).astype(jnp.float32)
    phase = wavenumbers[:, None] * longitude[None, :] % NLON
    angle = phase.astype(jnp.float32) * (2.0 * math.pi / NLON)
    weight = active[:, None] / math.sqrt(NLON)
    table = jnp.stack([jnp.cos(angle) * weight, -jnp.sin(angle) * weight], axis=1)
    return table.astype(jnp.bfloat16)

def meridional_table(wavenumbers):
    degree = jnp.arange(TRUNC, dtype=jnp.int32)
    latitude = jnp.arange(NLAT, dtype=jnp.int32)
    phase = degree[:, None] * (2 * latitude + 1)[None, :] % (4 * NLAT)
    angle = phase.astype(jnp.float32) * (math.pi / (2 * NLAT))
    factor = math.sqrt(2.0 / NLAT)
    even_table = (jnp.cos(angle) * factor).astype(jnp.bfloat16)
    odd_table = (jnp.sin(angle) * factor).astype(jnp.bfloat16)
    active = (degree[None, :] >= wavenumbers[:, None]) & (wavenumbers[:, None] < TRUNC)
    is_odd = (wavenumbers % 2 == 1)[:, None, None]
    table = jnp.where(is_odd, odd_table[None], even_table[None])
    return jnp.where(active[:, :, None], table, jnp.zeros((), jnp.bfloat16))

def reference(velocity, tracer, wave_slots, parents, noise):
    members = velocity.shape[0]
    product = (velocity.astype(jnp.float32) * tracer.astype(jnp.float32)).astype(jnp.bfloat16)
    table = zonal_table(wave_slots).reshape(-1, NLON)
    flat = product.reshape(-1, NLON)
    fourier = lax.dot_general(table, flat, (((1,), (1,)), ((), ())), preferred_element_type=jnp.float32)
    fourier = fourier.astype(jnp.bfloat16).reshape(MPAD, 2, members, FIELDS, NLAT)
    fourier = jnp.transpose(fourier, (0, 2, 1, 3, 4))
    degree = jnp.arange(TRUNC, dtype=jnp.int32)

    def per_slot(entries):
        wavenumber, coefficients, perturbation = entries
        basis = meridional_table(wavenumber[None])[0]
        spectra = jnp.dot(coefficients.reshape(-1, NLAT), basis.T, preferred_element_type=jnp.float32)
        spectra = spectra.astype(jnp.bfloat16).reshape(members, 2, FIELDS, TRUNC)
        parent_rows = spectra[parents]
        active = ((degree >= wavenumber) & (wavenumber < TRUNC)).astype(jnp.float32)
        children = (parent_rows.astype(jnp.float32) + perturbation.astype(jnp.float32) * active).astype(jnp.bfloat16)
        returned = jnp.dot(children.reshape(-1, TRUNC), basis, preferred_element_type=jnp.float32)
        return (children, returned.astype(jnp.bfloat16).reshape(members, 2, FIELDS, NLAT))
    child_spectra, child_fourier = lax.map(per_slot, (wave_slots, fourier, noise))
    return (child_spectra, child_fourier)
```

```python
import functools
import math

import jax
import jax.numpy as jnp
from jax import lax
from jax.experimental import pallas as pl
from jax.experimental.pallas import tpu as pltpu
from jax.sharding import PartitionSpec as P

SPREAD = 2
VMEM_BYTES = 48 * 1024 * 1024
LANES = 128


def zonal_factors(wavenumbers, longitudes, truncation):
    coarse = jnp.arange(longitudes // LANES, dtype=jnp.int32) * LANES
    fine = jnp.arange(LANES, dtype=jnp.int32)
    weight = (wavenumbers < truncation).astype(jnp.float32) / math.sqrt(longitudes)

    def angles(points):
        phase = wavenumbers[:, None] * points[None, :] % longitudes
        return phase.astype(jnp.float32) * (2.0 * math.pi / longitudes)

    coarse_angle, fine_angle = angles(coarse), angles(fine)
    return (
        jnp.cos(coarse_angle) * weight[:, None],
        jnp.sin(coarse_angle) * weight[:, None],
        jnp.cos(fine_angle),
        jnp.sin(fine_angle),
    )


def meridional_tables(truncation, latitudes):
    degree = jnp.arange(truncation, dtype=jnp.int32)
    latitude = jnp.arange(latitudes, dtype=jnp.int32)
    phase = degree[:, None] * (2 * latitude + 1)[None, :] % (4 * latitudes)
    angle = phase.astype(jnp.float32) * (math.pi / (2 * latitudes))
    factor = math.sqrt(2.0 / latitudes)
    even_table = (jnp.cos(angle) * factor).astype(jnp.bfloat16)
    odd_table = (jnp.sin(angle) * factor).astype(jnp.bfloat16)
    return even_table, odd_table


def zonal_kernel(
    fields_step, fields, cos_c, sin_c, cos_f, sin_f, velocity, tracer, out, table, total
):
    step = pl.program_id(0)
    rows = cos_f.shape[0]
    lat_local, longitudes = velocity.shape[2:]
    out_rows = out.shape[1]

    @pl.when(step == 0)
    def _():
        cos_b, sin_b = cos_f[...], sin_f[...]
        for at in range(longitudes // LANES):
            cos_a, sin_a = cos_c[:, at : at + 1], sin_c[:, at : at + 1]
            columns = slice(at * LANES, (at + 1) * LANES)
            table[:rows, columns] = (cos_a * cos_b - sin_a * sin_b).astype(table.dtype)
            table[rows:, columns] = (-sin_a * cos_b - cos_a * sin_b).astype(table.dtype)

    product = velocity[...].astype(jnp.float32) * tracer[...].astype(jnp.float32)
    product = product.astype(jnp.bfloat16).reshape(fields_step * lat_local, longitudes)
    sums = lax.dot_general(
        table[...], product, (((1,), (1,)), ((), ())), preferred_element_type=jnp.float32
    )
    steps_per_member = fields // fields_step
    member = step // steps_per_member
    first_field = step % steps_per_member * fields_step
    for part in range(2):
        for field in range(fields_step):
            row = (member * 2 + part) * fields + first_field + field
            total[pl.ds(row, rows, stride=out_rows), :] = sums[
                part * rows : (part + 1) * rows, field * lat_local : (field + 1) * lat_local
            ]

    @pl.when(step == pl.num_programs(0) - 1)
    def _():
        out[...] = total[...].reshape(out.shape).astype(out.dtype)


def zonal_transform(factors, velocity, tracer):
    mem_local, fields, lat_local, longitudes = velocity.shape
    rows = factors[0].shape[0]
    fields_step = min(fields, max(1, 256 // lat_local))
    steps = fields // fields_step
    out_rows = mem_local * 2 * fields
    whole = lambda step: (0, 0)
    grid_block = pl.BlockSpec(
        (1, fields_step, lat_local, longitudes), lambda step: (step // steps, step % steps, 0, 0)
    )
    flops = 2 * 2 * rows * longitudes * mem_local * fields * lat_local
    moved = 2 * velocity.size * 2 + rows * out_rows * lat_local * 2
    return pl.pallas_call(
        functools.partial(zonal_kernel, fields_step, fields),
        grid=(mem_local * steps,),
        in_specs=[pl.BlockSpec(f.shape, whole) for f in factors] + [grid_block, grid_block],
        out_specs=pl.BlockSpec((rows, out_rows, lat_local), lambda step: (0, 0, 0)),
        out_shape=jax.ShapeDtypeStruct((rows, out_rows, lat_local), jnp.bfloat16),
        scratch_shapes=[
            pltpu.VMEM((2 * rows, longitudes), jnp.bfloat16),
            pltpu.VMEM((rows * out_rows, lat_local), jnp.float32),
        ],
        compiler_params=pltpu.CompilerParams(vmem_limit_bytes=VMEM_BYTES),
        cost_estimate=pl.CostEstimate(flops=flops, bytes_accessed=moved, transcendentals=0),
        name="zonal",
    )(*factors, velocity, tracer)


def forward_kernel(first, block, waves, received, even, odd, out):
    truncation = even.shape[0]
    step = pl.program_id(0)
    per_slot = received.shape[1] // block
    rows = jnp.concatenate([received[g] for g in range(received.shape[0])], axis=-1)
    contract = (((1,), (1,)), ((), ()))
    by_even = lax.dot_general(rows, even[...], contract, preferred_element_type=jnp.float32)
    by_odd = lax.dot_general(rows, odd[...], contract, preferred_element_type=jnp.float32)
    degree = lax.broadcasted_iota(jnp.int32, (per_slot, truncation), 1)
    for slot in range(block):
        wave = waves[first + step * block + slot]
        least = jnp.where(wave < truncation, wave, truncation)
        here = slice(slot * per_slot, (slot + 1) * per_slot)
        chosen = jnp.where(wave % 2 == 1, by_odd[here], by_even[here])
        chosen = jnp.where(degree >= least, chosen, 0.0)
        out[slot] = chosen.astype(out.dtype).reshape(out.shape[1:])


def forward_transform(waves, first, block, received, even, odd, mem_local):
    groups, all_rows, lat_local = received.shape
    truncation, latitudes = even.shape
    slots = all_rows // (waves[1] * mem_local)
    out_shape = (slots, mem_local, waves[1], truncation)
    per_block = block * mem_local * waves[1]
    table = pl.BlockSpec(even.shape, lambda step, w: (0, 0))
    return pl.pallas_call(
        functools.partial(forward_kernel, first, block),
        grid_spec=pltpu.PrefetchScalarGridSpec(
            num_scalar_prefetch=1,
            grid=(slots // block,),
            in_specs=[
                pl.BlockSpec((groups, per_block, lat_local), lambda step, w: (0, step, 0)),
                table,
                table,
            ],
            out_specs=pl.BlockSpec((block,) + out_shape[1:], lambda step, w: (step, 0, 0, 0)),
        ),
        out_shape=jax.ShapeDtypeStruct(out_shape, jnp.bfloat16),
        compiler_params=pltpu.CompilerParams(vmem_limit_bytes=VMEM_BYTES),
        cost_estimate=pl.CostEstimate(
            flops=4 * all_rows * truncation * latitudes,
            bytes_accessed=2 * (received.size + 2 * even.size + all_rows * truncation),
            transcendentals=0,
        ),
        name="forward",
    )(waves[0], received, even, odd)


def inverse_kernel(first, block, waves, offsets, low, own, high, noise, even, odd, *rest):
    spectra_out, fourier_out = rest[-2:]
    truncation, latitudes = even.shape
    step = pl.program_id(0)
    mem_local, parts, fields = noise.shape[1:4]
    degree = lax.broadcasted_iota(jnp.int32, (fields, truncation), 1)
    sources = [low[:, m] for m in range(low.shape[1])]
    sources += [own[:, m] for m in range(own.shape[1])]
    sources += [high[:, m] for m in range(high.shape[1])]
    even_rows, odd_rows = [], []
    parents = []
    for child in range(mem_local):
        parent = sources[0]
        for at in range(1, len(sources)):
            parent = jnp.where(offsets[child] == at, sources[at], parent)
        parents.append(parent)
    for slot in range(block):
        wave = waves[first + step * block + slot]
        least = jnp.where(wave < truncation, wave, truncation)
        is_odd = wave % 2 == 1
        active = degree >= least
        for child in range(mem_local):
            parent = parents[child][slot].astype(jnp.float32)
            parent = parent.reshape(parts, fields, truncation)
            added = jnp.where(active[None], noise[slot, child].astype(jnp.float32), 0.0)
            total = parent + added
            spectra_out[slot, child] = total.astype(spectra_out.dtype)
            rows = total.reshape(parts * fields, truncation)
            even_rows.append(jnp.where(is_odd, 0.0, rows).astype(jnp.bfloat16))
            odd_rows.append(jnp.where(is_odd, rows, 0.0).astype(jnp.bfloat16))
    result = jnp.dot(
        jnp.concatenate(even_rows, axis=0), even[...], preferred_element_type=jnp.float32
    )
    result += jnp.dot(
        jnp.concatenate(odd_rows, axis=0), odd[...], preferred_element_type=jnp.float32
    )
    fourier_out[...] = result.reshape(fourier_out.shape).astype(fourier_out.dtype)


def inverse_transform(waves, offsets, first, block, low, own, high, noise, even, odd, outs):
    slots_all, mem_local, parts, fields, truncation = noise.shape
    latitudes = even.shape[1]
    slots = own.shape[0]
    at = first // block
    near = lambda step, w, o: (step, 0, 0, 0)
    far = lambda step, w, o: (at + step, 0, 0, 0, 0)
    table = pl.BlockSpec(even.shape, lambda step, w, o: (0, 0))
    noise_block = pl.BlockSpec((block,) + noise.shape[1:], far)
    fourier_shape = noise.shape[:4] + (latitudes,)
    fourier_block = pl.BlockSpec((block,) + fourier_shape[1:], far)
    operands = [low, own, high, noise, even, odd]
    in_specs = [pl.BlockSpec((block,) + a.shape[1:], near) for a in operands[:3]]
    in_specs += [noise_block, table, table]
    aliases = {}
    if outs is not None:
        aliases = {8: 0, 9: 1}
        operands += list(outs)
        in_specs += [pl.BlockSpec(memory_space=pl.ANY)] * 2
    rows = slots * mem_local * parts * fields
    return pl.pallas_call(
        functools.partial(inverse_kernel, first, block),
        grid_spec=pltpu.PrefetchScalarGridSpec(
            num_scalar_prefetch=2,
            grid=(slots // block,),
            in_specs=in_specs,
            out_specs=[noise_block, fourier_block],
        ),
        out_shape=[
            jax.ShapeDtypeStruct(noise.shape, jnp.bfloat16),
            jax.ShapeDtypeStruct(fourier_shape, jnp.bfloat16),
        ],
        input_output_aliases=aliases,
        compiler_params=pltpu.CompilerParams(vmem_limit_bytes=VMEM_BYTES),
        cost_estimate=pl.CostEstimate(
            flops=4 * rows * truncation * latitudes,
            bytes_accessed=2 * rows * (5 * truncation + latitudes) + 4 * even.size,
            transcendentals=0,
        ),
        name="inverse",
    )(waves, offsets, *operands)


def chunk_bounds(slots_here, block):
    blocks = slots_here // block
    count = min(4, blocks)
    edges = [blocks * at // count * block for at in range(count + 1)]
    return list(zip(edges[:-1], edges[1:]))


def per_device(velocity, tracer, wave_slots, parents, noise):
    lat_count = lax.axis_size("lat")
    lat_index = lax.axis_index("lat")
    mem_count = lax.axis_size("member")
    group_index = lax.axis_index("member")
    mem_local, fields, lat_local, longitudes = velocity.shape
    slots_here, truncation = noise.shape[0], noise.shape[-1]
    block = math.gcd(slots_here, 8)
    per_slot = mem_local * 2 * fields
    latitudes = lat_count * lat_local
    own_waves = lax.dynamic_slice_in_dim(wave_slots, lat_index * slots_here, slots_here)
    first_member = group_index * mem_local
    own_parents = lax.dynamic_slice_in_dim(parents, first_member, mem_local)
    offsets = own_parents - first_member + SPREAD
    even, odd = meridional_tables(truncation, latitudes)
    upward = [(i, i + 1) for i in range(mem_count - 1)]
    downward = [(target, source) for source, target in upward]
    slot_grid = wave_slots.reshape(lat_count, slots_here)
    outs = None
    for start, stop in chunk_bounds(slots_here, block):
        slots = stop - start
        factors = zonal_factors(slot_grid[:, start:stop].reshape(-1), longitudes, truncation)
        outgoing = zonal_transform(factors, velocity, tracer)
        outgoing = outgoing.reshape(lat_count, slots * per_slot, lat_local)
        received = lax.all_to_all(outgoing, "lat", split_axis=0, concat_axis=0, tiled=True)
        if lat_local % LANES != 0:
            received = jnp.swapaxes(received, 0, 1).reshape(1, slots * per_slot, latitudes)
        own = forward_transform(
            (own_waves, 2 * fields), start, block, received, even, odd, mem_local
        )
        low = lax.ppermute(own[:, mem_local - SPREAD :], "member", upward)
        high = lax.ppermute(own[:, :SPREAD], "member", downward)
        outs = inverse_transform(
            own_waves, offsets, start, block, low, own, high, noise, even, odd, outs
        )
    return tuple(outs)


def solution(mesh):
    in_specs = (
        P("member", None, "lat", None),
        P("member", None, "lat", None),
        P(),
        P(),
        P("lat", "member", None, None, None),
    )
    out_specs = (P("lat", "member", None, None, None), P("lat", "member", None, None, None))
    return jax.shard_map(
        per_device, mesh=mesh, in_specs=in_specs, out_specs=out_specs, check_vma=False
    )
```

```python
import functools
import math

import jax
import jax.numpy as jnp
from jax import lax
from jax.experimental import pallas as pl
from jax.experimental.pallas import tpu as pltpu
from jax.sharding import PartitionSpec as P

SPREAD = 2
VMEM_BYTES = 48 * 1024 * 1024
LANES = 128
TOKEN = (8, 128)


def zonal_factors(wavenumbers, longitudes, truncation):
    coarse = jnp.arange(longitudes // LANES, dtype=jnp.int32) * LANES
    fine = jnp.arange(LANES, dtype=jnp.int32)
    weight = (wavenumbers < truncation).astype(jnp.float32) / math.sqrt(longitudes)

    def angles(points):
        phase = wavenumbers[:, None] * points[None, :] % longitudes
        return phase.astype(jnp.float32) * (2.0 * math.pi / longitudes)

    coarse_angle, fine_angle = angles(coarse), angles(fine)
    return (
        jnp.cos(coarse_angle) * weight[:, None],
        jnp.sin(coarse_angle) * weight[:, None],
        jnp.cos(fine_angle),
        jnp.sin(fine_angle),
    )


def meridional_factors(truncation, latitudes, starts, width):
    degree = jnp.arange(truncation, dtype=jnp.int32)

    def angles(points):
        phase = degree[:, None] * points[None, :] % (4 * latitudes)
        return phase.astype(jnp.float32) * (math.pi / (2 * latitudes))

    coarse = angles(2 * starts)
    fine = angles(2 * jnp.arange(width, dtype=jnp.int32) + 1)
    factor = math.sqrt(2.0 / latitudes)
    return jnp.cos(coarse) * factor, jnp.sin(coarse) * factor, jnp.cos(fine), jnp.sin(fine)


def tables_kernel(cos_c, sin_c, cos_f, sin_f, even, odd):
    width = cos_f.shape[1]
    cos_b, sin_b = cos_f[...], sin_f[...]
    for at in range(cos_c.shape[1]):
        cos_a, sin_a = cos_c[:, at : at + 1], sin_c[:, at : at + 1]
        columns = slice(at * width, (at + 1) * width)
        even[:, columns] = (cos_a * cos_b - sin_a * sin_b).astype(even.dtype)
        odd[:, columns] = (sin_a * cos_b + cos_a * sin_b).astype(odd.dtype)


def meridional_tables(truncation, latitudes, starts, width):
    factors = meridional_factors(truncation, latitudes, starts, width)
    shape = jax.ShapeDtypeStruct((truncation, starts.shape[0] * width), jnp.bfloat16)
    return pl.pallas_call(
        tables_kernel,
        out_shape=[shape, shape],
        compiler_params=pltpu.CompilerParams(vmem_limit_bytes=VMEM_BYTES),
        cost_estimate=pl.CostEstimate(
            flops=6 * truncation * latitudes, bytes_accessed=4 * truncation * latitudes,
            transcendentals=0,
        ),
        name="tables",
    )(*factors)


def zonal_kernel(
    fields_step, fields, tokens, cos_c, sin_c, cos_f, sin_f, velocity, tracer, *rest
):
    outs, (table, total) = rest[tokens:-2], rest[-2:]
    step = pl.program_id(0)
    rows = cos_f.shape[0]
    lat_local, longitudes = velocity.shape[2:]
    out_rows = outs[0].shape[1]

    @pl.when(step == 0)
    def _():
        cos_b, sin_b = cos_f[...], sin_f[...]
        for at in range(longitudes // LANES):
            cos_a, sin_a = cos_c[:, at : at + 1], sin_c[:, at : at + 1]
            columns = slice(at * LANES, (at + 1) * LANES)
            table[:rows, columns] = (cos_a * cos_b - sin_a * sin_b).astype(table.dtype)
            table[rows:, columns] = (-sin_a * cos_b - cos_a * sin_b).astype(table.dtype)

    product = velocity[...].astype(jnp.float32) * tracer[...].astype(jnp.float32)
    product = product.astype(jnp.bfloat16).reshape(fields_step * lat_local, longitudes)
    sums = lax.dot_general(
        table[...], product, (((1,), (1,)), ((), ())), preferred_element_type=jnp.float32
    )
    steps_per_member = fields // fields_step
    member = step // steps_per_member
    first_field = step % steps_per_member * fields_step
    for part in range(2):
        for field in range(fields_step):
            row = (member * 2 + part) * fields + first_field + field
            total[pl.ds(row, rows, stride=out_rows), :] = sums[
                part * rows : (part + 1) * rows, field * lat_local : (field + 1) * lat_local
            ]

    @pl.when(step == pl.num_programs(0) - 1)
    def _():
        for at, out in enumerate(outs):
            size = out.shape[0] * out_rows
            part = total[at * size : (at + 1) * size, :]
            out[...] = part.reshape(out.shape).astype(out.dtype)


def zonal_transform(factors, velocity, tracer, pieces, tokens):
    mem_local, fields, lat_local, longitudes = velocity.shape
    rows = factors[0].shape[0]
    fields_step = min(fields, max(1, 512 // lat_local))
    steps = fields // fields_step
    out_rows = mem_local * 2 * fields
    piece = (rows // pieces, out_rows, lat_local)
    whole = lambda step: (0, 0)
    grid_block = pl.BlockSpec(
        (1, fields_step, lat_local, longitudes), lambda step: (step // steps, step % steps, 0, 0)
    )
    flops = 2 * 2 * rows * longitudes * mem_local * fields * lat_local
    moved = 2 * velocity.size * 2 + rows * out_rows * lat_local * 2
    return pl.pallas_call(
        functools.partial(zonal_kernel, fields_step, fields, len(tokens)),
        grid=(mem_local * steps,),
        in_specs=[pl.BlockSpec(f.shape, whole) for f in factors]
        + [grid_block, grid_block]
        + [pl.BlockSpec(memory_space=pl.ANY)] * len(tokens),
        out_specs=[pl.BlockSpec(piece, lambda step: (0, 0, 0))] * pieces,
        out_shape=[jax.ShapeDtypeStruct(piece, jnp.bfloat16)] * pieces,
        scratch_shapes=[
            pltpu.VMEM((2 * rows, longitudes), jnp.bfloat16),
            pltpu.VMEM((rows * out_rows, lat_local), jnp.float32),
        ],
        compiler_params=pltpu.CompilerParams(vmem_limit_bytes=VMEM_BYTES),
        cost_estimate=pl.CostEstimate(flops=flops, bytes_accessed=moved, transcendentals=0),
        name="zonal",
    )(*factors, velocity, tracer, *tokens)


def forward_kernel(first, block, waves, *refs):
    received, (even, odd, out, token) = refs[:-4], refs[-4:]
    truncation = even.shape[0]
    step = pl.program_id(0)
    per_slot = received[0].shape[0] // block
    rows = jnp.concatenate([piece[...] for piece in received], axis=-1)
    contract = (((1,), (1,)), ((), ()))
    by_even = lax.dot_general(rows, even[...], contract, preferred_element_type=jnp.float32)
    by_odd = lax.dot_general(rows, odd[...], contract, preferred_element_type=jnp.float32)
    degree = lax.broadcasted_iota(jnp.int32, (per_slot, truncation), 1)
    for slot in range(block):
        wave = waves[first + step * block + slot]
        least = jnp.where(wave < truncation, wave, truncation)
        here = slice(slot * per_slot, (slot + 1) * per_slot)
        chosen = jnp.where(wave % 2 == 1, by_odd[here], by_even[here])
        chosen = jnp.where(degree >= least, chosen, 0.0)
        out[slot] = chosen.astype(out.dtype).reshape(out.shape[1:])
    token[...] = jnp.zeros_like(token)


def forward_transform(waves, first, block, received, even, odd, mem_local):
    all_rows, lat_local = received[0].shape
    truncation, latitudes = even.shape
    slots = all_rows // (waves[1] * mem_local)
    out_shape = (slots, mem_local, waves[1], truncation)
    per_block = block * mem_local * waves[1]
    table = pl.BlockSpec(even.shape, lambda step, w: (0, 0))
    return pl.pallas_call(
        functools.partial(forward_kernel, first, block),
        grid_spec=pltpu.PrefetchScalarGridSpec(
            num_scalar_prefetch=1,
            grid=(slots // block,),
            in_specs=[pl.BlockSpec((per_block, lat_local), lambda step, w: (step, 0))]
            * len(received)
            + [table, table],
            out_specs=[
                pl.BlockSpec((block,) + out_shape[1:], lambda step, w: (step, 0, 0, 0)),
                pl.BlockSpec(TOKEN, lambda step, w: (0, 0)),
            ],
        ),
        out_shape=[
            jax.ShapeDtypeStruct(out_shape, jnp.bfloat16),
            jax.ShapeDtypeStruct(TOKEN, jnp.float32),
        ],
        compiler_params=pltpu.CompilerParams(vmem_limit_bytes=VMEM_BYTES),
        cost_estimate=pl.CostEstimate(
            flops=4 * all_rows * truncation * latitudes,
            bytes_accessed=2 * (all_rows * latitudes + 2 * even.size + all_rows * truncation),
            transcendentals=0,
        ),
        name="forward",
    )(waves[0], *received, even, odd)


def inverse_kernel(first, block, waves, offsets, low, own, high, noise, even, odd, *rest):
    spectra_out, fourier_out, token = rest[-3:]
    token[...] = jnp.zeros_like(token)
    truncation, latitudes = even.shape
    step = pl.program_id(0)
    mem_local, parts, fields = noise.shape[1:4]
    degree = lax.broadcasted_iota(jnp.int32, (fields, truncation), 1)
    sources = [low[:, m] for m in range(low.shape[1])]
    sources += [own[:, m] for m in range(own.shape[1])]
    sources += [high[:, m] for m in range(high.shape[1])]
    even_rows, odd_rows = [], []
    parents = []
    for child in range(mem_local):
        parent = sources[0]
        for at in range(1, len(sources)):
            parent = jnp.where(offsets[child] == at, sources[at], parent)
        parents.append(parent)
    for slot in range(block):
        wave = waves[first + step * block + slot]
        least = jnp.where(wave < truncation, wave, truncation)
        is_odd = wave % 2 == 1
        active = degree >= least
        for child in range(mem_local):
            parent = parents[child][slot].astype(jnp.float32)
            parent = parent.reshape(parts, fields, truncation)
            added = jnp.where(active[None], noise[slot, child].astype(jnp.float32), 0.0)
            total = parent + added
            spectra_out[slot, child] = total.astype(spectra_out.dtype)
            rows = total.reshape(parts * fields, truncation)
            even_rows.append(jnp.where(is_odd, 0.0, rows).astype(jnp.bfloat16))
            odd_rows.append(jnp.where(is_odd, rows, 0.0).astype(jnp.bfloat16))
    result = jnp.dot(
        jnp.concatenate(even_rows, axis=0), even[...], preferred_element_type=jnp.float32
    )
    result += jnp.dot(
        jnp.concatenate(odd_rows, axis=0), odd[...], preferred_element_type=jnp.float32
    )
    fourier_out[...] = result.reshape(fourier_out.shape).astype(fourier_out.dtype)


def inverse_transform(waves, offsets, first, block, low, own, high, noise, even, odd, outs):
    slots_all, mem_local, parts, fields, truncation = noise.shape
    latitudes = even.shape[1]
    slots = own.shape[0]
    at = first // block
    near = lambda step, w, o: (step, 0, 0, 0)
    far = lambda step, w, o: (at + step, 0, 0, 0, 0)
    table = pl.BlockSpec(even.shape, lambda step, w, o: (0, 0))
    noise_block = pl.BlockSpec((block,) + noise.shape[1:], far)
    fourier_shape = noise.shape[:4] + (latitudes,)
    fourier_block = pl.BlockSpec((block,) + fourier_shape[1:], far)
    operands = [low, own, high, noise, even, odd]
    in_specs = [pl.BlockSpec((block,) + a.shape[1:], near) for a in operands[:3]]
    in_specs += [noise_block, table, table]
    aliases = {}
    if outs is not None:
        aliases = {8: 0, 9: 1}
        operands += list(outs)
        in_specs += [pl.BlockSpec(memory_space=pl.ANY)] * 2
    rows = slots * mem_local * parts * fields
    return pl.pallas_call(
        functools.partial(inverse_kernel, first, block),
        grid_spec=pltpu.PrefetchScalarGridSpec(
            num_scalar_prefetch=2,
            grid=(slots // block,),
            in_specs=in_specs,
            out_specs=[
                noise_block,
                fourier_block,
                pl.BlockSpec(TOKEN, lambda step, w, o: (0, 0)),
            ],
        ),
        out_shape=[
            jax.ShapeDtypeStruct(noise.shape, jnp.bfloat16),
            jax.ShapeDtypeStruct(fourier_shape, jnp.bfloat16),
            jax.ShapeDtypeStruct(TOKEN, jnp.float32),
        ],
        input_output_aliases=aliases,
        compiler_params=pltpu.CompilerParams(vmem_limit_bytes=VMEM_BYTES),
        cost_estimate=pl.CostEstimate(
            flops=4 * rows * truncation * latitudes,
            bytes_accessed=2 * rows * (5 * truncation + latitudes) + 4 * even.size,
            transcendentals=0,
        ),
        name="inverse",
    )(waves, offsets, *operands)


def chunk_bounds(slots_here, block):
    blocks = slots_here // block
    edges = [0, 2, 5, 8, 10, 11]
    if blocks < edges[-1]:
        edges = list(range(blocks + 1))
    edges[-1] = blocks
    edges = [edge * block for edge in edges]
    return list(zip(edges[:-1], edges[1:]))


def per_device(velocity, tracer, wave_slots, parents, noise):
    lat_count = lax.axis_size("lat")
    lat_index = lax.axis_index("lat")
    mem_count = lax.axis_size("member")
    group_index = lax.axis_index("member")
    mem_local, fields, lat_local, longitudes = velocity.shape
    slots_here, truncation = noise.shape[0], noise.shape[-1]
    block = math.gcd(slots_here, 8)
    per_slot = mem_local * 2 * fields
    latitudes = lat_count * lat_local
    own_waves = lax.dynamic_slice_in_dim(wave_slots, lat_index * slots_here, slots_here)
    first_member = group_index * mem_local
    own_parents = lax.dynamic_slice_in_dim(parents, first_member, mem_local)
    offsets = own_parents - first_member + SPREAD
    upward = [(i, i + 1) for i in range(mem_count - 1)]
    downward = [(target, source) for source, target in upward]
    partners = jnp.arange(lat_count, dtype=jnp.int32) ^ lat_index
    slot_grid = wave_slots.reshape(lat_count, slots_here)[partners]
    bounds = chunk_bounds(slots_here, block)
    count = len(bounds)
    inner = min(lat_local, LANES)
    order = jnp.arange(latitudes // inner, dtype=jnp.int32) * inner
    swapped = (partners[:, None] * lat_local + jnp.arange(0, lat_local, inner)[None, :]).reshape(-1)
    received, own, edges, tokens = {}, {}, {}, {}
    outs = None

    def send(at):
        start, stop = bounds[at]
        waves = slot_grid[:, start:stop].reshape(-1)
        factors = zonal_factors(waves, longitudes, truncation)
        after = [tokens[key] for key in (("f", at - 2), ("i", at - 3)) if key in tokens]
        pieces = zonal_transform(factors, velocity, tracer, lat_count, after)
        pieces = [piece.reshape(-1, lat_local) for piece in pieces]
        moved = [pieces[0]] + [None] * (lat_count - 1)
        for k in reversed(range(1, lat_count)):
            moved[k] = lax.ppermute(pieces[k], "lat", [(i, i ^ k) for i in range(lat_count)])
        if lat_local % LANES != 0:
            moved = [jnp.concatenate(moved, axis=-1)]
        received[at] = moved

    def forward(at):
        start, _ = bounds[at]
        spectra, tokens["f", at] = forward_transform(
            (own_waves, 2 * fields), start, block, received[at], even_swapped, odd_swapped, mem_local
        )
        low = lax.ppermute(spectra[:, mem_local - SPREAD :], "member", upward)
        high = lax.ppermute(spectra[:, :SPREAD], "member", downward)
        own[at] = (low, spectra, high)

    def inverse(at, outs):
        start, _ = bounds[at]
        *outs, tokens["i", at] = inverse_transform(
            own_waves, offsets, start, block, *own[at], noise, even, odd, outs
        )
        return outs

    send(0)
    even_swapped, odd_swapped = meridional_tables(truncation, latitudes, swapped, inner)
    even, odd = meridional_tables(truncation, latitudes, order, inner)
    if count > 1:
        send(1)
    for at in range(count):
        forward(at)
        if at >= 1:
            outs = inverse(at - 1, outs)
        if at + 2 < count:
            send(at + 2)
    outs = inverse(count - 1, outs)
    return tuple(outs)


def solution(mesh):
    in_specs = (
        P("member", None, "lat", None),
        P("member", None, "lat", None),
        P(),
        P(),
        P("lat", "member", None, None, None),
    )
    out_specs = (P("lat", "member", None, None, None), P("lat", "member", None, None, None))
    return jax.shard_map(
        per_device, mesh=mesh, in_specs=in_specs, out_specs=out_specs, check_vma=False
    )
```

```python
import functools
import math

import jax
import jax.numpy as jnp
from jax import lax
from jax.experimental import pallas as pl
from jax.experimental.pallas import tpu as pltpu
from jax.sharding import PartitionSpec as P

SPREAD = 2
VMEM_BYTES = 48 * 1024 * 1024
LANES = 128
TOKEN = (8, 128)


def zonal_factors(wavenumbers, longitudes, truncation):
    coarse = jnp.arange(longitudes // LANES, dtype=jnp.int32) * LANES
    fine = jnp.arange(LANES, dtype=jnp.int32)
    weight = (wavenumbers < truncation).astype(jnp.float32) / math.sqrt(longitudes)

    def angles(points):
        phase = wavenumbers[:, None] * points[None, :] % longitudes
        return phase.astype(jnp.float32) * (2.0 * math.pi / longitudes)

    coarse_angle, fine_angle = angles(coarse), angles(fine)
    return (
        jnp.cos(coarse_angle) * weight[:, None],
        jnp.sin(coarse_angle) * weight[:, None],
        jnp.cos(fine_angle),
        jnp.sin(fine_angle),
    )


def meridional_factors(truncation, latitudes, starts, width):
    degree = jnp.arange(truncation, dtype=jnp.int32)

    def angles(points):
        phase = degree[:, None] * points[None, :] % (4 * latitudes)
        return phase.astype(jnp.float32) * (math.pi / (2 * latitudes))

    coarse = angles(2 * starts)
    fine = angles(2 * jnp.arange(width, dtype=jnp.int32) + 1)
    factor = math.sqrt(2.0 / latitudes)
    return jnp.cos(coarse) * factor, jnp.sin(coarse) * factor, jnp.cos(fine), jnp.sin(fine)


def tables_kernel(cos_c, sin_c, cos_f, sin_f, even, odd):
    width = cos_f.shape[1]
    cos_b, sin_b = cos_f[...], sin_f[...]
    for at in range(cos_c.shape[1]):
        cos_a, sin_a = cos_c[:, at : at + 1], sin_c[:, at : at + 1]
        columns = slice(at * width, (at + 1) * width)
        even[:, columns] = (cos_a * cos_b - sin_a * sin_b).astype(even.dtype)
        odd[:, columns] = (sin_a * cos_b + cos_a * sin_b).astype(odd.dtype)


def meridional_tables(truncation, latitudes, starts, width):
    factors = meridional_factors(truncation, latitudes, starts, width)
    shape = jax.ShapeDtypeStruct((truncation, starts.shape[0] * width), jnp.bfloat16)
    return pl.pallas_call(
        tables_kernel,
        out_shape=[shape, shape],
        compiler_params=pltpu.CompilerParams(vmem_limit_bytes=VMEM_BYTES),
        cost_estimate=pl.CostEstimate(
            flops=6 * truncation * latitudes, bytes_accessed=4 * truncation * latitudes,
            transcendentals=0,
        ),
        name="tables",
    )(*factors)


def zonal_kernel(
    fields_step, fields, tokens, cos_c, sin_c, cos_f, sin_f, velocity, tracer, *rest
):
    out, table, total = rest[tokens:]
    step = pl.program_id(0)
    rows = cos_f.shape[0]
    lat_local, longitudes = velocity.shape[2:]
    out_rows = out.shape[1]

    @pl.when(step == 0)
    def _():
        cos_b, sin_b = cos_f[...], sin_f[...]
        for at in range(longitudes // LANES):
            cos_a, sin_a = cos_c[:, at : at + 1], sin_c[:, at : at + 1]
            columns = slice(at * LANES, (at + 1) * LANES)
            table[:rows, columns] = (cos_a * cos_b - sin_a * sin_b).astype(table.dtype)
            table[rows:, columns] = (-sin_a * cos_b - cos_a * sin_b).astype(table.dtype)

    product = velocity[...].astype(jnp.float32) * tracer[...].astype(jnp.float32)
    product = product.astype(jnp.bfloat16).reshape(fields_step * lat_local, longitudes)
    sums = lax.dot_general(
        table[...], product, (((1,), (1,)), ((), ())), preferred_element_type=jnp.float32
    )
    steps_per_member = fields // fields_step
    member = step // steps_per_member
    first_field = step % steps_per_member * fields_step
    for part in range(2):
        for field in range(fields_step):
            row = (member * 2 + part) * fields + first_field + field
            total[pl.ds(row, rows, stride=out_rows), :] = sums[
                part * rows : (part + 1) * rows, field * lat_local : (field + 1) * lat_local
            ]

    @pl.when(step == pl.num_programs(0) - 1)
    def _():
        out[...] = total[...].reshape(out.shape).astype(out.dtype)


def zonal_transform(factors, velocity, tracer, tokens):
    mem_local, fields, lat_local, longitudes = velocity.shape
    rows = factors[0].shape[0]
    fields_step = min(fields, max(1, 512 // lat_local))
    steps = fields // fields_step
    out_rows = mem_local * 2 * fields
    whole = lambda step: (0, 0)
    grid_block = pl.BlockSpec(
        (1, fields_step, lat_local, longitudes), lambda step: (step // steps, step % steps, 0, 0)
    )
    flops = 2 * 2 * rows * longitudes * mem_local * fields * lat_local
    moved = 2 * velocity.size * 2 + rows * out_rows * lat_local * 2
    return pl.pallas_call(
        functools.partial(zonal_kernel, fields_step, fields, len(tokens)),
        grid=(mem_local * steps,),
        in_specs=[pl.BlockSpec(f.shape, whole) for f in factors]
        + [grid_block, grid_block]
        + [pl.BlockSpec(memory_space=pl.ANY)] * len(tokens),
        out_specs=pl.BlockSpec((rows, out_rows, lat_local), lambda step: (0, 0, 0)),
        out_shape=jax.ShapeDtypeStruct((rows, out_rows, lat_local), jnp.bfloat16),
        scratch_shapes=[
            pltpu.VMEM((2 * rows, longitudes), jnp.bfloat16),
            pltpu.VMEM((rows * out_rows, lat_local), jnp.float32),
        ],
        compiler_params=pltpu.CompilerParams(vmem_limit_bytes=VMEM_BYTES),
        cost_estimate=pl.CostEstimate(flops=flops, bytes_accessed=moved, transcendentals=0),
        name="zonal",
    )(*factors, velocity, tracer, *tokens)


def forward_kernel(first, block, waves, received, even, odd, out, token):
    truncation = even.shape[0]
    step = pl.program_id(0)
    per_slot = received.shape[1] // block
    rows = jnp.concatenate([received[g] for g in range(received.shape[0])], axis=-1)
    contract = (((1,), (1,)), ((), ()))
    by_even = lax.dot_general(rows, even[...], contract, preferred_element_type=jnp.float32)
    by_odd = lax.dot_general(rows, odd[...], contract, preferred_element_type=jnp.float32)
    degree = lax.broadcasted_iota(jnp.int32, (per_slot, truncation), 1)
    for slot in range(block):
        wave = waves[first + step * block + slot]
        least = jnp.where(wave < truncation, wave, truncation)
        here = slice(slot * per_slot, (slot + 1) * per_slot)
        chosen = jnp.where(wave % 2 == 1, by_odd[here], by_even[here])
        chosen = jnp.where(degree >= least, chosen, 0.0)
        out[slot] = chosen.astype(out.dtype).reshape(out.shape[1:])
    token[...] = jnp.zeros_like(token)


def forward_transform(waves, first, block, received, even, odd, mem_local):
    groups, all_rows, lat_local = received.shape
    truncation, latitudes = even.shape
    slots = all_rows // (waves[1] * mem_local)
    out_shape = (slots, mem_local, waves[1], truncation)
    per_block = block * mem_local * waves[1]
    table = pl.BlockSpec(even.shape, lambda step, w: (0, 0))
    return pl.pallas_call(
        functools.partial(forward_kernel, first, block),
        grid_spec=pltpu.PrefetchScalarGridSpec(
            num_scalar_prefetch=1,
            grid=(slots // block,),
            in_specs=[
                pl.BlockSpec((groups, per_block, lat_local), lambda step, w: (0, step, 0)),
                table,
                table,
            ],
            out_specs=[
                pl.BlockSpec((block,) + out_shape[1:], lambda step, w: (step, 0, 0, 0)),
                pl.BlockSpec(TOKEN, lambda step, w: (0, 0)),
            ],
        ),
        out_shape=[
            jax.ShapeDtypeStruct(out_shape, jnp.bfloat16),
            jax.ShapeDtypeStruct(TOKEN, jnp.float32),
        ],
        compiler_params=pltpu.CompilerParams(vmem_limit_bytes=VMEM_BYTES),
        cost_estimate=pl.CostEstimate(
            flops=4 * all_rows * truncation * latitudes,
            bytes_accessed=2 * (all_rows * latitudes + 2 * even.size + all_rows * truncation),
            transcendentals=0,
        ),
        name="forward",
    )(waves[0], received, even, odd)


def inverse_kernel(first, block, waves, offsets, low, own, high, noise, even, odd, *rest):
    spectra_out, fourier_out, token = rest[-3:]
    token[...] = jnp.zeros_like(token)
    truncation, latitudes = even.shape
    step = pl.program_id(0)
    mem_local, parts, fields = noise.shape[1:4]
    degree = lax.broadcasted_iota(jnp.int32, (fields, truncation), 1)
    sources = [low[:, m] for m in range(low.shape[1])]
    sources += [own[:, m] for m in range(own.shape[1])]
    sources += [high[:, m] for m in range(high.shape[1])]
    even_rows, odd_rows = [], []
    parents = []
    for child in range(mem_local):
        parent = sources[0]
        for at in range(1, len(sources)):
            parent = jnp.where(offsets[child] == at, sources[at], parent)
        parents.append(parent)
    for slot in range(block):
        wave = waves[first + step * block + slot]
        least = jnp.where(wave < truncation, wave, truncation)
        is_odd = wave % 2 == 1
        active = degree >= least
        for child in range(mem_local):
            parent = parents[child][slot].astype(jnp.float32)
            parent = parent.reshape(parts, fields, truncation)
            added = jnp.where(active[None], noise[slot, child].astype(jnp.float32), 0.0)
            total = parent + added
            spectra_out[slot, child] = total.astype(spectra_out.dtype)
            rows = total.reshape(parts * fields, truncation)
            even_rows.append(jnp.where(is_odd, 0.0, rows).astype(jnp.bfloat16))
            odd_rows.append(jnp.where(is_odd, rows, 0.0).astype(jnp.bfloat16))
    result = jnp.dot(
        jnp.concatenate(even_rows, axis=0), even[...], preferred_element_type=jnp.float32
    )
    result += jnp.dot(
        jnp.concatenate(odd_rows, axis=0), odd[...], preferred_element_type=jnp.float32
    )
    fourier_out[...] = result.reshape(fourier_out.shape).astype(fourier_out.dtype)


def inverse_transform(waves, offsets, first, block, low, own, high, noise, even, odd, outs):
    slots_all, mem_local, parts, fields, truncation = noise.shape
    latitudes = even.shape[1]
    slots = own.shape[0]
    at = first // block
    near = lambda step, w, o: (step, 0, 0, 0)
    far = lambda step, w, o: (at + step, 0, 0, 0, 0)
    table = pl.BlockSpec(even.shape, lambda step, w, o: (0, 0))
    noise_block = pl.BlockSpec((block,) + noise.shape[1:], far)
    fourier_shape = noise.shape[:4] + (latitudes,)
    fourier_block = pl.BlockSpec((block,) + fourier_shape[1:], far)
    operands = [low, own, high, noise, even, odd]
    in_specs = [pl.BlockSpec((block,) + a.shape[1:], near) for a in operands[:3]]
    in_specs += [noise_block, table, table]
    aliases = {}
    if outs is not None:
        aliases = {8: 0, 9: 1}
        operands += list(outs)
        in_specs += [pl.BlockSpec(memory_space=pl.ANY)] * 2
    rows = slots * mem_local * parts * fields
    return pl.pallas_call(
        functools.partial(inverse_kernel, first, block),
        grid_spec=pltpu.PrefetchScalarGridSpec(
            num_scalar_prefetch=2,
            grid=(slots // block,),
            in_specs=in_specs,
            out_specs=[
                noise_block,
                fourier_block,
                pl.BlockSpec(TOKEN, lambda step, w, o: (0, 0)),
            ],
        ),
        out_shape=[
            jax.ShapeDtypeStruct(noise.shape, jnp.bfloat16),
            jax.ShapeDtypeStruct(fourier_shape, jnp.bfloat16),
            jax.ShapeDtypeStruct(TOKEN, jnp.float32),
        ],
        input_output_aliases=aliases,
        compiler_params=pltpu.CompilerParams(vmem_limit_bytes=VMEM_BYTES),
        cost_estimate=pl.CostEstimate(
            flops=4 * rows * truncation * latitudes,
            bytes_accessed=2 * rows * (5 * truncation + latitudes) + 4 * even.size,
            transcendentals=0,
        ),
        name="inverse",
    )(waves, offsets, *operands)


def chunk_bounds(slots_here, block):
    blocks = slots_here // block
    edges = [0, 2, 6, 9, 11]
    if blocks < edges[-1]:
        edges = list(range(blocks + 1))
    edges[-1] = blocks
    edges = [edge * block for edge in edges]
    return list(zip(edges[:-1], edges[1:]))


def per_device(velocity, tracer, wave_slots, parents, noise):
    lat_count = lax.axis_size("lat")
    lat_index = lax.axis_index("lat")
    mem_count = lax.axis_size("member")
    group_index = lax.axis_index("member")
    mem_local, fields, lat_local, longitudes = velocity.shape
    slots_here, truncation = noise.shape[0], noise.shape[-1]
    block = math.gcd(slots_here, 8)
    per_slot = mem_local * 2 * fields
    latitudes = lat_count * lat_local
    own_waves = lax.dynamic_slice_in_dim(wave_slots, lat_index * slots_here, slots_here)
    first_member = group_index * mem_local
    own_parents = lax.dynamic_slice_in_dim(parents, first_member, mem_local)
    offsets = own_parents - first_member + SPREAD
    upward = [(i, i + 1) for i in range(mem_count - 1)]
    downward = [(target, source) for source, target in upward]
    slot_grid = wave_slots.reshape(lat_count, slots_here)
    bounds = chunk_bounds(slots_here, block)
    count = len(bounds)
    inner = min(lat_local, LANES)
    starts = jnp.arange(latitudes // inner, dtype=jnp.int32) * inner
    received, own, tokens = {}, {}, {}
    outs = None

    def send(at):
        start, stop = bounds[at]
        waves = slot_grid[:, start:stop].reshape(-1)
        factors = zonal_factors(waves, longitudes, truncation)
        after = [tokens[key] for key in (("f", at - 2), ("i", at - 3)) if key in tokens]
        outgoing = zonal_transform(factors, velocity, tracer, after)
        rows = (stop - start) * per_slot
        outgoing = outgoing.reshape(lat_count, rows, lat_local)
        moved = lax.all_to_all(outgoing, "lat", split_axis=0, concat_axis=0, tiled=True)
        if lat_local % LANES != 0:
            moved = jnp.swapaxes(moved, 0, 1).reshape(1, rows, latitudes)
        received[at] = moved

    def forward(at):
        start, _ = bounds[at]
        spectra, tokens["f", at] = forward_transform(
            (own_waves, 2 * fields), start, block, received[at], even, odd, mem_local
        )
        low = lax.ppermute(spectra[:, mem_local - SPREAD :], "member", upward)
        high = lax.ppermute(spectra[:, :SPREAD], "member", downward)
        own[at] = (low, spectra, high)

    def inverse(at, outs):
        start, _ = bounds[at]
        *outs, tokens["i", at] = inverse_transform(
            own_waves, offsets, start, block, *own[at], noise, even, odd, outs
        )
        return outs

    send(0)
    even, odd = meridional_tables(truncation, latitudes, starts, inner)
    if count > 1:
        send(1)
    for at in range(count):
        forward(at)
        if at >= 1:
            outs = inverse(at - 1, outs)
        if at + 2 < count:
            send(at + 2)
    outs = inverse(count - 1, outs)
    return tuple(outs)


def solution(mesh):
    in_specs = (
        P("member", None, "lat", None),
        P("member", None, "lat", None),
        P(),
        P(),
        P("lat", "member", None, None, None),
    )
    out_specs = (P("lat", "member", None, None, None), P("lat", "member", None, None, None))
    return jax.shard_map(
        per_device, mesh=mesh, in_specs=in_specs, out_specs=out_specs, check_vma=False
    )
```

```python
import functools
import math

import jax
import jax.numpy as jnp
from jax import lax
from jax.experimental import pallas as pl
from jax.experimental.pallas import tpu as pltpu
from jax.sharding import PartitionSpec as P

SPREAD = 2
VMEM_BYTES = 48 * 1024 * 1024
LANES = 128
TOKEN = (8, 128)


def zonal_factors(wavenumbers, longitudes, truncation):
    coarse = jnp.arange(longitudes // LANES, dtype=jnp.int32) * LANES
    fine = jnp.arange(LANES, dtype=jnp.int32)
    weight = (wavenumbers < truncation).astype(jnp.float32) / math.sqrt(longitudes)

    def angles(points):
        phase = wavenumbers[:, None] * points[None, :] % longitudes
        return phase.astype(jnp.float32) * (2.0 * math.pi / longitudes)

    coarse_angle, fine_angle = angles(coarse), angles(fine)
    return (
        jnp.cos(coarse_angle) * weight[:, None],
        jnp.sin(coarse_angle) * weight[:, None],
        jnp.cos(fine_angle),
        jnp.sin(fine_angle),
    )


def meridional_factors(truncation, latitudes, starts, width):
    degree = jnp.arange(truncation, dtype=jnp.int32)

    def angles(points):
        phase = degree[:, None] * points[None, :] % (4 * latitudes)
        return phase.astype(jnp.float32) * (math.pi / (2 * latitudes))

    coarse = angles(2 * starts)
    fine = angles(2 * jnp.arange(width, dtype=jnp.int32) + 1)
    factor = math.sqrt(2.0 / latitudes)
    return jnp.cos(coarse) * factor, jnp.sin(coarse) * factor, jnp.cos(fine), jnp.sin(fine)


def tables_kernel(cos_c, sin_c, cos_f, sin_f, even, odd):
    width = cos_f.shape[1]
    cos_b, sin_b = cos_f[...], sin_f[...]
    for at in range(cos_c.shape[1]):
        cos_a, sin_a = cos_c[:, at : at + 1], sin_c[:, at : at + 1]
        columns = slice(at * width, (at + 1) * width)
        even[:, columns] = (cos_a * cos_b - sin_a * sin_b).astype(even.dtype)
        odd[:, columns] = (sin_a * cos_b + cos_a * sin_b).astype(odd.dtype)


def meridional_tables(truncation, latitudes, starts, width):
    factors = meridional_factors(truncation, latitudes, starts, width)
    shape = jax.ShapeDtypeStruct((truncation, starts.shape[0] * width), jnp.bfloat16)
    return pl.pallas_call(
        tables_kernel,
        out_shape=[shape, shape],
        compiler_params=pltpu.CompilerParams(vmem_limit_bytes=VMEM_BYTES),
        cost_estimate=pl.CostEstimate(
            flops=6 * truncation * latitudes, bytes_accessed=4 * truncation * latitudes,
            transcendentals=0,
        ),
        name="tables",
    )(*factors)


def zonal_kernel(
    fields_step, fields, tokens, cos_c, sin_c, cos_f, sin_f, velocity, tracer, *rest
):
    out, table, total = rest[tokens:]
    step = pl.program_id(0)
    rows = cos_f.shape[0]
    lat_local, longitudes = velocity.shape[2:]
    out_rows = out.shape[1]

    @pl.when(step == 0)
    def _():
        cos_b, sin_b = cos_f[...], sin_f[...]
        for at in range(longitudes // LANES):
            cos_a, sin_a = cos_c[:, at : at + 1], sin_c[:, at : at + 1]
            columns = slice(at * LANES, (at + 1) * LANES)
            table[:rows, columns] = (cos_a * cos_b - sin_a * sin_b).astype(table.dtype)
            table[rows:, columns] = (-sin_a * cos_b - cos_a * sin_b).astype(table.dtype)

    product = velocity[...].astype(jnp.float32) * tracer[...].astype(jnp.float32)
    product = product.astype(jnp.bfloat16).reshape(fields_step * lat_local, longitudes)
    sums = lax.dot_general(
        table[...], product, (((1,), (1,)), ((), ())), preferred_element_type=jnp.float32
    )
    steps_per_member = fields // fields_step
    member = step // steps_per_member
    first_field = step % steps_per_member * fields_step
    for part in range(2):
        for field in range(fields_step):
            row = (member * 2 + part) * fields + first_field + field
            total[pl.ds(row, rows, stride=out_rows), :] = sums[
                part * rows : (part + 1) * rows, field * lat_local : (field + 1) * lat_local
            ]

    @pl.when(step == pl.num_programs(0) - 1)
    def _():
        out[...] = total[...].reshape(out.shape).astype(out.dtype)


def zonal_transform(factors, velocity, tracer, tokens):
    mem_local, fields, lat_local, longitudes = velocity.shape
    rows = factors[0].shape[0]
    fields_step = min(fields, max(1, 512 // lat_local))
    steps = fields // fields_step
    out_rows = mem_local * 2 * fields
    whole = lambda step: (0, 0)
    grid_block = pl.BlockSpec(
        (1, fields_step, lat_local, longitudes), lambda step: (step // steps, step % steps, 0, 0)
    )
    flops = 2 * 2 * rows * longitudes * mem_local * fields * lat_local
    moved = 2 * velocity.size * 2 + rows * out_rows * lat_local * 2
    return pl.pallas_call(
        functools.partial(zonal_kernel, fields_step, fields, len(tokens)),
        grid=(mem_local * steps,),
        in_specs=[pl.BlockSpec(f.shape, whole) for f in factors]
        + [grid_block, grid_block]
        + [pl.BlockSpec(memory_space=pl.ANY)] * len(tokens),
        out_specs=pl.BlockSpec((rows, out_rows, lat_local), lambda step: (0, 0, 0)),
        out_shape=jax.ShapeDtypeStruct((rows, out_rows, lat_local), jnp.bfloat16),
        scratch_shapes=[
            pltpu.VMEM((2 * rows, longitudes), jnp.bfloat16),
            pltpu.VMEM((rows * out_rows, lat_local), jnp.float32),
        ],
        compiler_params=pltpu.CompilerParams(vmem_limit_bytes=VMEM_BYTES),
        cost_estimate=pl.CostEstimate(flops=flops, bytes_accessed=moved, transcendentals=0),
        name="zonal",
    )(*factors, velocity, tracer, *tokens)


def forward_kernel(first, block, waves, received, even, odd, *rest):
    out, token = rest[-2:]
    truncation = even.shape[0]
    step = pl.program_id(0)
    per_slot = received.shape[1] // block
    rows = jnp.concatenate([received[g] for g in range(received.shape[0])], axis=-1)
    contract = (((1,), (1,)), ((), ()))
    by_even = lax.dot_general(rows, even[...], contract, preferred_element_type=jnp.float32)
    by_odd = lax.dot_general(rows, odd[...], contract, preferred_element_type=jnp.float32)
    degree = lax.broadcasted_iota(jnp.int32, (per_slot, truncation), 1)
    for slot in range(block):
        wave = waves[first + step * block + slot]
        least = jnp.where(wave < truncation, wave, truncation)
        here = slice(slot * per_slot, (slot + 1) * per_slot)
        chosen = jnp.where(wave % 2 == 1, by_odd[here], by_even[here])
        chosen = jnp.where(degree >= least, chosen, 0.0)
        out[slot] = chosen.astype(out.dtype).reshape(out.shape[1:])
    token[...] = jnp.zeros_like(token)


def forward_transform(waves, first, block, received, even, odd, mem_local, tokens):
    groups, all_rows, lat_local = received.shape
    truncation, latitudes = even.shape
    slots = all_rows // (waves[1] * mem_local)
    out_shape = (slots, mem_local, waves[1], truncation)
    per_block = block * mem_local * waves[1]
    table = pl.BlockSpec(even.shape, lambda step, w: (0, 0))
    return pl.pallas_call(
        functools.partial(forward_kernel, first, block),
        grid_spec=pltpu.PrefetchScalarGridSpec(
            num_scalar_prefetch=1,
            grid=(slots // block,),
            in_specs=[
                pl.BlockSpec((groups, per_block, lat_local), lambda step, w: (0, step, 0)),
                table,
                table,
            ]
            + [pl.BlockSpec(memory_space=pl.ANY)] * len(tokens),
            out_specs=[
                pl.BlockSpec((block,) + out_shape[1:], lambda step, w: (step, 0, 0, 0)),
                pl.BlockSpec(TOKEN, lambda step, w: (0, 0)),
            ],
        ),
        out_shape=[
            jax.ShapeDtypeStruct(out_shape, jnp.bfloat16),
            jax.ShapeDtypeStruct(TOKEN, jnp.float32),
        ],
        compiler_params=pltpu.CompilerParams(vmem_limit_bytes=VMEM_BYTES),
        cost_estimate=pl.CostEstimate(
            flops=4 * all_rows * truncation * latitudes,
            bytes_accessed=2 * (all_rows * latitudes + 2 * even.size + all_rows * truncation),
            transcendentals=0,
        ),
        name="forward",
    )(waves[0], received, even, odd, *tokens)


def inverse_kernel(first, block, waves, offsets, low, own, high, noise, even, odd, *rest):
    spectra_out, fourier_out, token = rest[-3:]
    token[...] = jnp.zeros_like(token)
    truncation, latitudes = even.shape
    step = pl.program_id(0)
    mem_local, parts, fields = noise.shape[1:4]
    degree = lax.broadcasted_iota(jnp.int32, (fields, truncation), 1)
    sources = [low[:, m] for m in range(low.shape[1])]
    sources += [own[:, m] for m in range(own.shape[1])]
    sources += [high[:, m] for m in range(high.shape[1])]
    even_rows, odd_rows = [], []
    parents = []
    for child in range(mem_local):
        parent = sources[0]
        for at in range(1, len(sources)):
            parent = jnp.where(offsets[child] == at, sources[at], parent)
        parents.append(parent)
    for slot in range(block):
        wave = waves[first + step * block + slot]
        least = jnp.where(wave < truncation, wave, truncation)
        is_odd = wave % 2 == 1
        active = degree >= least
        for child in range(mem_local):
            parent = parents[child][slot].astype(jnp.float32)
            parent = parent.reshape(parts, fields, truncation)
            added = jnp.where(active[None], noise[slot, child].astype(jnp.float32), 0.0)
            total = parent + added
            spectra_out[slot, child] = total.astype(spectra_out.dtype)
            rows = total.reshape(parts * fields, truncation)
            even_rows.append(jnp.where(is_odd, 0.0, rows).astype(jnp.bfloat16))
            odd_rows.append(jnp.where(is_odd, rows, 0.0).astype(jnp.bfloat16))
    result = jnp.dot(
        jnp.concatenate(even_rows, axis=0), even[...], preferred_element_type=jnp.float32
    )
    result += jnp.dot(
        jnp.concatenate(odd_rows, axis=0), odd[...], preferred_element_type=jnp.float32
    )
    fourier_out[...] = result.reshape(fourier_out.shape).astype(fourier_out.dtype)


def inverse_transform(waves, offsets, first, block, low, own, high, noise, even, odd, outs):
    slots_all, mem_local, parts, fields, truncation = noise.shape
    latitudes = even.shape[1]
    slots = own.shape[0]
    at = first // block
    near = lambda step, w, o: (step, 0, 0, 0)
    far = lambda step, w, o: (at + step, 0, 0, 0, 0)
    table = pl.BlockSpec(even.shape, lambda step, w, o: (0, 0))
    noise_block = pl.BlockSpec((block,) + noise.shape[1:], far)
    fourier_shape = noise.shape[:4] + (latitudes,)
    fourier_block = pl.BlockSpec((block,) + fourier_shape[1:], far)
    operands = [low, own, high, noise, even, odd]
    in_specs = [pl.BlockSpec((block,) + a.shape[1:], near) for a in operands[:3]]
    in_specs += [noise_block, table, table]
    aliases = {}
    if outs is not None:
        aliases = {8: 0, 9: 1}
        operands += list(outs)
        in_specs += [pl.BlockSpec(memory_space=pl.ANY)] * 2
    rows = slots * mem_local * parts * fields
    return pl.pallas_call(
        functools.partial(inverse_kernel, first, block),
        grid_spec=pltpu.PrefetchScalarGridSpec(
            num_scalar_prefetch=2,
            grid=(slots // block,),
            in_specs=in_specs,
            out_specs=[
                noise_block,
                fourier_block,
                pl.BlockSpec(TOKEN, lambda step, w, o: (0, 0)),
            ],
        ),
        out_shape=[
            jax.ShapeDtypeStruct(noise.shape, jnp.bfloat16),
            jax.ShapeDtypeStruct(fourier_shape, jnp.bfloat16),
            jax.ShapeDtypeStruct(TOKEN, jnp.float32),
        ],
        input_output_aliases=aliases,
        compiler_params=pltpu.CompilerParams(vmem_limit_bytes=VMEM_BYTES),
        cost_estimate=pl.CostEstimate(
            flops=4 * rows * truncation * latitudes,
            bytes_accessed=2 * rows * (5 * truncation + latitudes) + 4 * even.size,
            transcendentals=0,
        ),
        name="inverse",
    )(waves, offsets, *operands)


def chunk_bounds(slots_here, block):
    blocks = slots_here // block
    edges = [0, 3, 7, 10, 11]
    if blocks < edges[-1]:
        edges = list(range(blocks + 1))
    edges[-1] = blocks
    edges = [edge * block for edge in edges]
    return list(zip(edges[:-1], edges[1:]))


def per_device(velocity, tracer, wave_slots, parents, noise):
    lat_count = lax.axis_size("lat")
    lat_index = lax.axis_index("lat")
    mem_count = lax.axis_size("member")
    group_index = lax.axis_index("member")
    mem_local, fields, lat_local, longitudes = velocity.shape
    slots_here, truncation = noise.shape[0], noise.shape[-1]
    block = math.gcd(slots_here, 8)
    per_slot = mem_local * 2 * fields
    latitudes = lat_count * lat_local
    own_waves = lax.dynamic_slice_in_dim(wave_slots, lat_index * slots_here, slots_here)
    first_member = group_index * mem_local
    own_parents = lax.dynamic_slice_in_dim(parents, first_member, mem_local)
    offsets = own_parents - first_member + SPREAD
    upward = [(i, i + 1) for i in range(mem_count - 1)]
    downward = [(target, source) for source, target in upward]
    slot_grid = wave_slots.reshape(lat_count, slots_here)
    bounds = chunk_bounds(slots_here, block)
    count = len(bounds)
    inner = min(lat_local, LANES)
    starts = jnp.arange(latitudes // inner, dtype=jnp.int32) * inner
    received, own, tokens = {}, {}, {}
    outs = None

    def send(at):
        start, stop = bounds[at]
        waves = slot_grid[:, start:stop].reshape(-1)
        factors = zonal_factors(waves, longitudes, truncation)
        after = [tokens["f", at - 2]] if at >= 2 else []
        outgoing = zonal_transform(factors, velocity, tracer, after)
        rows = (stop - start) * per_slot
        outgoing = outgoing.reshape(lat_count, rows, lat_local)
        moved = lax.all_to_all(outgoing, "lat", split_axis=0, concat_axis=0, tiled=True)
        if lat_local % LANES != 0:
            moved = jnp.swapaxes(moved, 0, 1).reshape(1, rows, latitudes)
        received[at] = moved

    def forward(at):
        start, _ = bounds[at]
        after = [tokens["i", at - 2]] if at >= 2 else []
        spectra, tokens["f", at] = forward_transform(
            (own_waves, 2 * fields), start, block, received[at], even, odd, mem_local, after
        )
        low = lax.ppermute(spectra[:, mem_local - SPREAD :], "member", upward)
        high = lax.ppermute(spectra[:, :SPREAD], "member", downward)
        own[at] = (low, spectra, high)

    def inverse(at, outs):
        start, _ = bounds[at]
        *outs, tokens["i", at] = inverse_transform(
            own_waves, offsets, start, block, *own[at], noise, even, odd, outs
        )
        return outs

    send(0)
    even, odd = meridional_tables(truncation, latitudes, starts, inner)
    if count > 1:
        send(1)
    for at in range(count):
        forward(at)
        if at >= 1:
            outs = inverse(at - 1, outs)
        if at + 2 < count:
            send(at + 2)
    outs = inverse(count - 1, outs)
    return tuple(outs)


def solution(mesh):
    in_specs = (
        P("member", None, "lat", None),
        P("member", None, "lat", None),
        P(),
        P(),
        P("lat", "member", None, None, None),
    )
    out_specs = (P("lat", "member", None, None, None), P("lat", "member", None, None, None))
    return jax.shard_map(
        per_device, mesh=mesh, in_specs=in_specs, out_specs=out_specs, check_vma=False
    )
```

```python
import functools
import math

import jax
import jax.numpy as jnp
from jax import lax
from jax.experimental import pallas as pl
from jax.experimental.pallas import tpu as pltpu
from jax.sharding import PartitionSpec as P

SPREAD = 2
VMEM_BYTES = 48 * 1024 * 1024
LANES = 128
TOKEN = (8, 128)


def zonal_factors(wavenumbers, longitudes, truncation):
    coarse = jnp.arange(longitudes // LANES, dtype=jnp.int32) * LANES
    fine = jnp.arange(LANES, dtype=jnp.int32)
    weight = (wavenumbers < truncation).astype(jnp.float32) / math.sqrt(longitudes)

    def angles(points):
        phase = wavenumbers[:, None] * points[None, :] % longitudes
        return phase.astype(jnp.float32) * (2.0 * math.pi / longitudes)

    coarse_angle, fine_angle = angles(coarse), angles(fine)
    return (
        jnp.cos(coarse_angle) * weight[:, None],
        jnp.sin(coarse_angle) * weight[:, None],
        jnp.cos(fine_angle),
        jnp.sin(fine_angle),
    )


def meridional_factors(truncation, latitudes, starts, width):
    degree = jnp.arange(truncation, dtype=jnp.int32)

    def angles(points):
        phase = degree[:, None] * points[None, :] % (4 * latitudes)
        return phase.astype(jnp.float32) * (math.pi / (2 * latitudes))

    coarse = angles(2 * starts)
    fine = angles(2 * jnp.arange(width, dtype=jnp.int32) + 1)
    factor = math.sqrt(2.0 / latitudes)
    return jnp.cos(coarse) * factor, jnp.sin(coarse) * factor, jnp.cos(fine), jnp.sin(fine)


def tables_kernel(cos_c, sin_c, cos_f, sin_f, even, odd):
    width = cos_f.shape[1]
    cos_b, sin_b = cos_f[...], sin_f[...]
    for at in range(cos_c.shape[1]):
        cos_a, sin_a = cos_c[:, at : at + 1], sin_c[:, at : at + 1]
        columns = slice(at * width, (at + 1) * width)
        even[:, columns] = (cos_a * cos_b - sin_a * sin_b).astype(even.dtype)
        odd[:, columns] = (sin_a * cos_b + cos_a * sin_b).astype(odd.dtype)


def meridional_tables(truncation, latitudes, starts, width):
    factors = meridional_factors(truncation, latitudes, starts, width)
    shape = jax.ShapeDtypeStruct((truncation, starts.shape[0] * width), jnp.bfloat16)
    return pl.pallas_call(
        tables_kernel,
        out_shape=[shape, shape],
        compiler_params=pltpu.CompilerParams(vmem_limit_bytes=VMEM_BYTES),
        cost_estimate=pl.CostEstimate(
            flops=6 * truncation * latitudes, bytes_accessed=4 * truncation * latitudes,
            transcendentals=0,
        ),
        name="tables",
    )(*factors)


def zonal_kernel(
    fields_step, fields, tokens, cos_c, sin_c, cos_f, sin_f, velocity, tracer, *rest
):
    *outs, token, table, total = rest[tokens:]
    token[...] = jnp.zeros_like(token)
    step = pl.program_id(0)
    rows = cos_f.shape[0]
    lat_local, longitudes = velocity.shape[2:]
    out_rows = outs[0].shape[1]

    @pl.when(step == 0)
    def _():
        cos_b, sin_b = cos_f[...], sin_f[...]
        for at in range(longitudes // LANES):
            cos_a, sin_a = cos_c[:, at : at + 1], sin_c[:, at : at + 1]
            columns = slice(at * LANES, (at + 1) * LANES)
            table[:rows, columns] = (cos_a * cos_b - sin_a * sin_b).astype(table.dtype)
            table[rows:, columns] = (-sin_a * cos_b - cos_a * sin_b).astype(table.dtype)

    product = velocity[...].astype(jnp.float32) * tracer[...].astype(jnp.float32)
    product = product.astype(jnp.bfloat16).reshape(fields_step * lat_local, longitudes)
    sums = lax.dot_general(
        table[...], product, (((1,), (1,)), ((), ())), preferred_element_type=jnp.float32
    )
    steps_per_member = fields // fields_step
    member = step // steps_per_member
    first_field = step % steps_per_member * fields_step
    for part in range(2):
        for field in range(fields_step):
            row = (member * 2 + part) * fields + first_field + field
            total[pl.ds(row, rows, stride=out_rows), :] = sums[
                part * rows : (part + 1) * rows, field * lat_local : (field + 1) * lat_local
            ]

    @pl.when(step == pl.num_programs(0) - 1)
    def _():
        size = outs[0].shape[0] * out_rows
        for at, out in enumerate(outs):
            part = total[at * size : (at + 1) * size, :]
            out[...] = part.reshape(out.shape).astype(out.dtype)


def zonal_transform(factors, velocity, tracer, pieces, tokens):
    mem_local, fields, lat_local, longitudes = velocity.shape
    rows = factors[0].shape[0]
    fields_step = min(fields, max(1, 512 // lat_local))
    steps = fields // fields_step
    out_rows = mem_local * 2 * fields
    piece = (rows // pieces, out_rows, lat_local)
    whole = lambda step: (0, 0)
    grid_block = pl.BlockSpec(
        (1, fields_step, lat_local, longitudes), lambda step: (step // steps, step % steps, 0, 0)
    )
    flops = 2 * 2 * rows * longitudes * mem_local * fields * lat_local
    moved = 2 * velocity.size * 2 + rows * out_rows * lat_local * 2
    return pl.pallas_call(
        functools.partial(zonal_kernel, fields_step, fields, len(tokens)),
        grid=(mem_local * steps,),
        in_specs=[pl.BlockSpec(f.shape, whole) for f in factors]
        + [grid_block, grid_block]
        + [pl.BlockSpec(memory_space=pl.ANY)] * len(tokens),
        out_specs=[pl.BlockSpec(piece, lambda step: (0, 0, 0))] * pieces
        + [pl.BlockSpec(TOKEN, lambda step: (0, 0))],
        out_shape=[jax.ShapeDtypeStruct(piece, jnp.bfloat16)] * pieces
        + [jax.ShapeDtypeStruct(TOKEN, jnp.float32)],
        scratch_shapes=[
            pltpu.VMEM((2 * rows, longitudes), jnp.bfloat16),
            pltpu.VMEM((rows * out_rows, lat_local), jnp.float32),
        ],
        compiler_params=pltpu.CompilerParams(vmem_limit_bytes=VMEM_BYTES),
        cost_estimate=pl.CostEstimate(flops=flops, bytes_accessed=moved, transcendentals=0),
        name="zonal",
    )(*factors, velocity, tracer, *tokens)


def forward_kernel(first, block, pieces, waves, *refs):
    received, (even, odd), (out, token) = refs[:pieces], refs[pieces : pieces + 2], refs[-2:]
    truncation = even.shape[0]
    step = pl.program_id(0)
    per_slot = received[0].shape[1] // block
    rows = [piece[g] for piece in received for g in range(piece.shape[0])]
    rows = jnp.concatenate(rows, axis=-1)
    contract = (((1,), (1,)), ((), ()))
    by_even = lax.dot_general(rows, even[...], contract, preferred_element_type=jnp.float32)
    by_odd = lax.dot_general(rows, odd[...], contract, preferred_element_type=jnp.float32)
    degree = lax.broadcasted_iota(jnp.int32, (per_slot, truncation), 1)
    for slot in range(block):
        wave = waves[first + step * block + slot]
        least = jnp.where(wave < truncation, wave, truncation)
        here = slice(slot * per_slot, (slot + 1) * per_slot)
        chosen = jnp.where(wave % 2 == 1, by_odd[here], by_even[here])
        chosen = jnp.where(degree >= least, chosen, 0.0)
        out[slot] = chosen.astype(out.dtype).reshape(out.shape[1:])
    token[...] = jnp.zeros_like(token)


def forward_transform(waves, first, block, received, even, odd, mem_local, tokens):
    groups, all_rows, lat_local = received[0].shape
    truncation, latitudes = even.shape
    slots = all_rows // (waves[1] * mem_local)
    out_shape = (slots, mem_local, waves[1], truncation)
    per_block = block * mem_local * waves[1]
    table = pl.BlockSpec(even.shape, lambda step, w: (0, 0))
    return pl.pallas_call(
        functools.partial(forward_kernel, first, block, len(received)),
        grid_spec=pltpu.PrefetchScalarGridSpec(
            num_scalar_prefetch=1,
            grid=(slots // block,),
            in_specs=[
                pl.BlockSpec((groups, per_block, lat_local), lambda step, w: (0, step, 0))
            ]
            * len(received)
            + [table, table]
            + [pl.BlockSpec(memory_space=pl.ANY)] * len(tokens),
            out_specs=[
                pl.BlockSpec((block,) + out_shape[1:], lambda step, w: (step, 0, 0, 0)),
                pl.BlockSpec(TOKEN, lambda step, w: (0, 0)),
            ],
        ),
        out_shape=[
            jax.ShapeDtypeStruct(out_shape, jnp.bfloat16),
            jax.ShapeDtypeStruct(TOKEN, jnp.float32),
        ],
        compiler_params=pltpu.CompilerParams(vmem_limit_bytes=VMEM_BYTES),
        cost_estimate=pl.CostEstimate(
            flops=4 * all_rows * truncation * latitudes,
            bytes_accessed=2 * (all_rows * latitudes + 2 * even.size + all_rows * truncation),
            transcendentals=0,
        ),
        name="forward",
    )(waves[0], *received, even, odd, *tokens)


def inverse_kernel(first, block, waves, offsets, low, own, high, noise, even, odd, *rest):
    spectra_out, fourier_out, token = rest[-3:]
    token[...] = jnp.zeros_like(token)
    truncation, latitudes = even.shape
    step = pl.program_id(0)
    mem_local, parts, fields = noise.shape[1:4]
    degree = lax.broadcasted_iota(jnp.int32, (fields, truncation), 1)
    sources = [low[:, m] for m in range(low.shape[1])]
    sources += [own[:, m] for m in range(own.shape[1])]
    sources += [high[:, m] for m in range(high.shape[1])]
    even_rows, odd_rows = [], []
    parents = []
    for child in range(mem_local):
        parent = sources[0]
        for at in range(1, len(sources)):
            parent = jnp.where(offsets[child] == at, sources[at], parent)
        parents.append(parent)
    for slot in range(block):
        wave = waves[first + step * block + slot]
        least = jnp.where(wave < truncation, wave, truncation)
        is_odd = wave % 2 == 1
        active = degree >= least
        for child in range(mem_local):
            parent = parents[child][slot].astype(jnp.float32)
            parent = parent.reshape(parts, fields, truncation)
            added = jnp.where(active[None], noise[slot, child].astype(jnp.float32), 0.0)
            total = parent + added
            spectra_out[slot, child] = total.astype(spectra_out.dtype)
            rows = total.reshape(parts * fields, truncation)
            even_rows.append(jnp.where(is_odd, 0.0, rows).astype(jnp.bfloat16))
            odd_rows.append(jnp.where(is_odd, rows, 0.0).astype(jnp.bfloat16))
    result = jnp.dot(
        jnp.concatenate(even_rows, axis=0), even[...], preferred_element_type=jnp.float32
    )
    result += jnp.dot(
        jnp.concatenate(odd_rows, axis=0), odd[...], preferred_element_type=jnp.float32
    )
    fourier_out[...] = result.reshape(fourier_out.shape).astype(fourier_out.dtype)


def inverse_transform(waves, offsets, first, block, low, own, high, noise, even, odd, outs):
    slots_all, mem_local, parts, fields, truncation = noise.shape
    latitudes = even.shape[1]
    slots = own.shape[0]
    at = first // block
    near = lambda step, w, o: (step, 0, 0, 0)
    far = lambda step, w, o: (at + step, 0, 0, 0, 0)
    table = pl.BlockSpec(even.shape, lambda step, w, o: (0, 0))
    noise_block = pl.BlockSpec((block,) + noise.shape[1:], far)
    fourier_shape = noise.shape[:4] + (latitudes,)
    fourier_block = pl.BlockSpec((block,) + fourier_shape[1:], far)
    operands = [low, own, high, noise, even, odd]
    in_specs = [pl.BlockSpec((block,) + a.shape[1:], near) for a in operands[:3]]
    in_specs += [noise_block, table, table]
    aliases = {}
    if outs is not None:
        aliases = {8: 0, 9: 1}
        operands += list(outs)
        in_specs += [pl.BlockSpec(memory_space=pl.ANY)] * 2
    rows = slots * mem_local * parts * fields
    return pl.pallas_call(
        functools.partial(inverse_kernel, first, block),
        grid_spec=pltpu.PrefetchScalarGridSpec(
            num_scalar_prefetch=2,
            grid=(slots // block,),
            in_specs=in_specs,
            out_specs=[
                noise_block,
                fourier_block,
                pl.BlockSpec(TOKEN, lambda step, w, o: (0, 0)),
            ],
        ),
        out_shape=[
            jax.ShapeDtypeStruct(noise.shape, jnp.bfloat16),
            jax.ShapeDtypeStruct(fourier_shape, jnp.bfloat16),
            jax.ShapeDtypeStruct(TOKEN, jnp.float32),
        ],
        input_output_aliases=aliases,
        compiler_params=pltpu.CompilerParams(vmem_limit_bytes=VMEM_BYTES),
        cost_estimate=pl.CostEstimate(
            flops=4 * rows * truncation * latitudes,
            bytes_accessed=2 * rows * (5 * truncation + latitudes) + 4 * even.size,
            transcendentals=0,
        ),
        name="inverse",
    )(waves, offsets, *operands)


def chunk_bounds(slots_here, block):
    blocks = slots_here // block
    shares = (2, 5, 3)
    edges = [0]
    for share in shares:
        edges.append(min(blocks, edges[-1] + max(1, blocks * share // 11)))
    edges.append(blocks)
    edges = [edge * block for edge in edges]
    return [(start, stop) for start, stop in zip(edges[:-1], edges[1:]) if stop > start]


def per_device(velocity, tracer, wave_slots, parents, noise):
    lat_count = lax.axis_size("lat")
    lat_index = lax.axis_index("lat")
    mem_count = lax.axis_size("member")
    group_index = lax.axis_index("member")
    mem_local, fields, lat_local, longitudes = velocity.shape
    slots_here, truncation = noise.shape[0], noise.shape[-1]
    block = math.gcd(slots_here, 8)
    per_slot = mem_local * 2 * fields
    latitudes = lat_count * lat_local
    own_waves = lax.dynamic_slice_in_dim(wave_slots, lat_index * slots_here, slots_here)
    first_member = group_index * mem_local
    own_parents = lax.dynamic_slice_in_dim(parents, first_member, mem_local)
    offsets = own_parents - first_member + SPREAD
    upward = [(i, i + 1) for i in range(mem_count - 1)]
    downward = [(target, source) for source, target in upward]
    slot_grid = wave_slots.reshape(lat_count, slots_here)
    bounds = chunk_bounds(slots_here, block)
    count = len(bounds)
    inner = min(lat_local, LANES)
    partners = jnp.arange(lat_count, dtype=jnp.int32) ^ lat_index
    lanes_at = jnp.arange(0, lat_local, inner, dtype=jnp.int32)[None, :]

    def tables_of(devices):
        starts = (devices[:, None] * lat_local + lanes_at).reshape(-1)
        return meridional_tables(truncation, latitudes, starts, inner)

    received, own, tokens = {}, {}, {}
    outs = None

    def joined(pieces):
        if lat_local % LANES == 0:
            return pieces
        pieces = jnp.concatenate(pieces, axis=0)
        return [jnp.swapaxes(pieces, 0, 1).reshape(1, -1, latitudes)]

    def transform(at, grid, pieces, after):
        start, stop = bounds[at]
        factors = zonal_factors(grid[:, start:stop].reshape(-1), longitudes, truncation)
        after = [tokens[key] for key in after]
        *pieces, tokens["z", at] = zonal_transform(factors, velocity, tracer, pieces, after)
        return [piece.reshape(-1, (stop - start) * per_slot, lat_local) for piece in pieces]

    def send(at, *after):
        (outgoing,) = transform(at, slot_grid, 1, after)
        moved = lax.all_to_all(outgoing, "lat", split_axis=0, concat_axis=0, tiled=True)
        received[at] = joined([moved])

    def send_by_permutes(at, *after):
        moved = transform(at, slot_grid[partners], lat_count, after)
        for k in reversed(range(1, lat_count)):
            moved[k] = lax.ppermute(moved[k], "lat", [(i, i ^ k) for i in range(lat_count)])
        received[at] = joined(moved)

    def forward(at, tables, *after):
        start, _ = bounds[at]
        spectra, tokens["f", at] = forward_transform(
            (own_waves, 2 * fields),
            start,
            block,
            received[at],
            *tables,
            mem_local,
            [tokens[key] for key in after],
        )
        low = lax.ppermute(spectra[:, mem_local - SPREAD :], "member", upward)
        high = lax.ppermute(spectra[:, :SPREAD], "member", downward)
        own[at] = (low, spectra, high)

    def inverse(at, outs):
        start, _ = bounds[at]
        *outs, tokens["i", at] = inverse_transform(
            own_waves, offsets, start, block, *own[at], noise, *tables, outs
        )
        return outs

    send(1)
    send_by_permutes(0)
    swapped = tables_of(partners)
    tables = tables_of(jnp.arange(lat_count, dtype=jnp.int32))
    send(2, ("z", 0))
    forward(1, tables)
    forward(0, swapped, ("f", 1))
    outs = inverse(1, outs)
    if count > 3:
        send(3, ("f", 0))
    forward(2, tables)
    outs = inverse(0, outs)
    if count > 3:
        forward(3, tables, ("i", 0))
    outs = inverse(2, outs)
    if count > 3:
        outs = inverse(3, outs)
    return tuple(outs)


def solution(mesh):
    in_specs = (
        P("member", None, "lat", None),
        P("member", None, "lat", None),
        P(),
        P(),
        P("lat", "member", None, None, None),
    )
    out_specs = (P("lat", "member", None, None, None), P("lat", "member", None, None, None))
    return jax.shard_map(
        per_device, mesh=mesh, in_specs=in_specs, out_specs=out_specs, check_vma=False
    )
```

```python
import functools
import math

import jax
import jax.numpy as jnp
from jax import lax
from jax.experimental import pallas as pl
from jax.experimental.pallas import tpu as pltpu
from jax.sharding import PartitionSpec as P

SPREAD = 2
VMEM_BYTES = 48 * 1024 * 1024
LANES = 128
TOKEN = (8, 128)


def zonal_factors(wavenumbers, longitudes, truncation):
    coarse = jnp.arange(longitudes // LANES, dtype=jnp.int32) * LANES
    fine = jnp.arange(LANES, dtype=jnp.int32)
    weight = (wavenumbers < truncation).astype(jnp.float32) / math.sqrt(longitudes)

    def angles(points):
        phase = wavenumbers[:, None] * points[None, :] % longitudes
        return phase.astype(jnp.float32) * (2.0 * math.pi / longitudes)

    coarse_angle, fine_angle = angles(coarse), angles(fine)
    return (
        jnp.cos(coarse_angle) * weight[:, None],
        jnp.sin(coarse_angle) * weight[:, None],
        jnp.cos(fine_angle),
        jnp.sin(fine_angle),
    )


def meridional_factors(truncation, latitudes, starts, width):
    degree = jnp.arange(truncation, dtype=jnp.int32)

    def angles(points):
        phase = degree[:, None] * points[None, :] % (4 * latitudes)
        return phase.astype(jnp.float32) * (math.pi / (2 * latitudes))

    coarse = angles(2 * starts)
    fine = angles(2 * jnp.arange(width, dtype=jnp.int32) + 1)
    factor = math.sqrt(2.0 / latitudes)
    return jnp.cos(coarse) * factor, jnp.sin(coarse) * factor, jnp.cos(fine), jnp.sin(fine)


def tables_kernel(cos_c, sin_c, cos_f, sin_f, even, odd):
    width = cos_f.shape[1]
    cos_b, sin_b = cos_f[...], sin_f[...]
    for at in range(cos_c.shape[1]):
        cos_a, sin_a = cos_c[:, at : at + 1], sin_c[:, at : at + 1]
        columns = slice(at * width, (at + 1) * width)
        even[:, columns] = (cos_a * cos_b - sin_a * sin_b).astype(even.dtype)
        odd[:, columns] = (sin_a * cos_b + cos_a * sin_b).astype(odd.dtype)


def meridional_tables(truncation, latitudes, starts, width):
    factors = meridional_factors(truncation, latitudes, starts, width)
    shape = jax.ShapeDtypeStruct((truncation, starts.shape[0] * width), jnp.bfloat16)
    return pl.pallas_call(
        tables_kernel,
        out_shape=[shape, shape],
        compiler_params=pltpu.CompilerParams(vmem_limit_bytes=VMEM_BYTES),
        cost_estimate=pl.CostEstimate(
            flops=6 * truncation * latitudes, bytes_accessed=4 * truncation * latitudes,
            transcendentals=0,
        ),
        name="tables",
    )(*factors)


def zonal_kernel(
    fields_step, fields, tokens, cos_c, sin_c, cos_f, sin_f, velocity, tracer, *rest
):
    out, table, total = rest[tokens:]
    step = pl.program_id(0)
    rows = cos_f.shape[0]
    lat_local, longitudes = velocity.shape[2:]
    out_rows = out.shape[1]

    @pl.when(step == 0)
    def _():
        cos_b, sin_b = cos_f[...], sin_f[...]
        for at in range(longitudes // LANES):
            cos_a, sin_a = cos_c[:, at : at + 1], sin_c[:, at : at + 1]
            columns = slice(at * LANES, (at + 1) * LANES)
            table[:rows, columns] = (cos_a * cos_b - sin_a * sin_b).astype(table.dtype)
            table[rows:, columns] = (-sin_a * cos_b - cos_a * sin_b).astype(table.dtype)

    product = velocity[...].astype(jnp.float32) * tracer[...].astype(jnp.float32)
    product = product.astype(jnp.bfloat16).reshape(fields_step * lat_local, longitudes)
    sums = lax.dot_general(
        table[...], product, (((1,), (1,)), ((), ())), preferred_element_type=jnp.float32
    )
    steps_per_member = fields // fields_step
    member = step // steps_per_member
    first_field = step % steps_per_member * fields_step
    for part in range(2):
        for field in range(fields_step):
            row = (member * 2 + part) * fields + first_field + field
            total[pl.ds(row, rows, stride=out_rows), :] = sums[
                part * rows : (part + 1) * rows, field * lat_local : (field + 1) * lat_local
            ]

    @pl.when(step == pl.num_programs(0) - 1)
    def _():
        out[...] = total[...].reshape(out.shape).astype(out.dtype)


def zonal_transform(factors, velocity, tracer, tokens):
    mem_local, fields, lat_local, longitudes = velocity.shape
    rows = factors[0].shape[0]
    fields_step = min(fields, max(1, 512 // lat_local))
    steps = fields // fields_step
    out_rows = mem_local * 2 * fields
    whole = lambda step: (0, 0)
    grid_block = pl.BlockSpec(
        (1, fields_step, lat_local, longitudes), lambda step: (step // steps, step % steps, 0, 0)
    )
    flops = 2 * 2 * rows * longitudes * mem_local * fields * lat_local
    moved = 2 * velocity.size * 2 + rows * out_rows * lat_local * 2
    return pl.pallas_call(
        functools.partial(zonal_kernel, fields_step, fields, len(tokens)),
        grid=(mem_local * steps,),
        in_specs=[pl.BlockSpec(f.shape, whole) for f in factors]
        + [grid_block, grid_block]
        + [pl.BlockSpec(memory_space=pl.ANY)] * len(tokens),
        out_specs=pl.BlockSpec((rows, out_rows, lat_local), lambda step: (0, 0, 0)),
        out_shape=jax.ShapeDtypeStruct((rows, out_rows, lat_local), jnp.bfloat16),
        scratch_shapes=[
            pltpu.VMEM((2 * rows, longitudes), jnp.bfloat16),
            pltpu.VMEM((rows * out_rows, lat_local), jnp.float32),
        ],
        compiler_params=pltpu.CompilerParams(vmem_limit_bytes=VMEM_BYTES),
        cost_estimate=pl.CostEstimate(flops=flops, bytes_accessed=moved, transcendentals=0),
        name="zonal",
    )(*factors, velocity, tracer, *tokens)


def forward_kernel(first, block, waves, received, even, odd, *rest):
    out, token = rest[-2:]
    truncation = even.shape[0]
    step = pl.program_id(0)
    per_slot = received.shape[1] // block
    rows = jnp.concatenate([received[g] for g in range(received.shape[0])], axis=-1)
    contract = (((1,), (1,)), ((), ()))
    by_even = lax.dot_general(rows, even[...], contract, preferred_element_type=jnp.float32)
    by_odd = lax.dot_general(rows, odd[...], contract, preferred_element_type=jnp.float32)
    degree = lax.broadcasted_iota(jnp.int32, (per_slot, truncation), 1)
    for slot in range(block):
        wave = waves[first + step * block + slot]
        least = jnp.where(wave < truncation, wave, truncation)
        here = slice(slot * per_slot, (slot + 1) * per_slot)
        chosen = jnp.where(wave % 2 == 1, by_odd[here], by_even[here])
        chosen = jnp.where(degree >= least, chosen, 0.0)
        out[slot] = chosen.astype(out.dtype).reshape(out.shape[1:])
    token[...] = jnp.zeros_like(token)


def forward_transform(waves, first, block, received, even, odd, mem_local, tokens):
    groups, all_rows, lat_local = received.shape
    truncation, latitudes = even.shape
    slots = all_rows // (waves[1] * mem_local)
    out_shape = (slots, mem_local, waves[1], truncation)
    per_block = block * mem_local * waves[1]
    table = pl.BlockSpec(even.shape, lambda step, w: (0, 0))
    return pl.pallas_call(
        functools.partial(forward_kernel, first, block),
        grid_spec=pltpu.PrefetchScalarGridSpec(
            num_scalar_prefetch=1,
            grid=(slots // block,),
            in_specs=[
                pl.BlockSpec((groups, per_block, lat_local), lambda step, w: (0, step, 0)),
                table,
                table,
            ]
            + [pl.BlockSpec(memory_space=pl.ANY)] * len(tokens),
            out_specs=[
                pl.BlockSpec((block,) + out_shape[1:], lambda step, w: (step, 0, 0, 0)),
                pl.BlockSpec(TOKEN, lambda step, w: (0, 0)),
            ],
        ),
        out_shape=[
            jax.ShapeDtypeStruct(out_shape, jnp.bfloat16),
            jax.ShapeDtypeStruct(TOKEN, jnp.float32),
        ],
        compiler_params=pltpu.CompilerParams(vmem_limit_bytes=VMEM_BYTES),
        cost_estimate=pl.CostEstimate(
            flops=4 * all_rows * truncation * latitudes,
            bytes_accessed=2 * (all_rows * latitudes + 2 * even.size + all_rows * truncation),
            transcendentals=0,
        ),
        name="forward",
    )(waves[0], received, even, odd, *tokens)


def inverse_kernel(first, block, waves, offsets, low, own, high, noise, even, odd, *rest):
    spectra_out, fourier_out, token = rest[-3:]
    token[...] = jnp.zeros_like(token)
    truncation, latitudes = even.shape
    step = pl.program_id(0)
    mem_local, parts, fields = noise.shape[1:4]
    degree = lax.broadcasted_iota(jnp.int32, (fields, truncation), 1)
    sources = [low[:, m] for m in range(low.shape[1])]
    sources += [own[:, m] for m in range(own.shape[1])]
    sources += [high[:, m] for m in range(high.shape[1])]
    even_rows, odd_rows = [], []
    parents = []
    for child in range(mem_local):
        parent = sources[0]
        for at in range(1, len(sources)):
            parent = jnp.where(offsets[child] == at, sources[at], parent)
        parents.append(parent)
    for slot in range(block):
        wave = waves[first + step * block + slot]
        least = jnp.where(wave < truncation, wave, truncation)
        is_odd = wave % 2 == 1
        active = degree >= least
        for child in range(mem_local):
            parent = parents[child][slot].astype(jnp.float32)
            parent = parent.reshape(parts, fields, truncation)
            added = jnp.where(active[None], noise[slot, child].astype(jnp.float32), 0.0)
            total = parent + added
            spectra_out[slot, child] = total.astype(spectra_out.dtype)
            rows = total.reshape(parts * fields, truncation)
            even_rows.append(jnp.where(is_odd, 0.0, rows).astype(jnp.bfloat16))
            odd_rows.append(jnp.where(is_odd, rows, 0.0).astype(jnp.bfloat16))
    result = jnp.dot(
        jnp.concatenate(even_rows, axis=0), even[...], preferred_element_type=jnp.float32
    )
    result += jnp.dot(
        jnp.concatenate(odd_rows, axis=0), odd[...], preferred_element_type=jnp.float32
    )
    fourier_out[...] = result.reshape(fourier_out.shape).astype(fourier_out.dtype)


def inverse_transform(waves, offsets, first, block, low, own, high, noise, even, odd, outs):
    slots_all, mem_local, parts, fields, truncation = noise.shape
    latitudes = even.shape[1]
    slots = own.shape[0]
    at = first // block
    near = lambda step, w, o: (step, 0, 0, 0)
    far = lambda step, w, o: (at + step, 0, 0, 0, 0)
    table = pl.BlockSpec(even.shape, lambda step, w, o: (0, 0))
    noise_block = pl.BlockSpec((block,) + noise.shape[1:], far)
    fourier_shape = noise.shape[:4] + (latitudes,)
    fourier_block = pl.BlockSpec((block,) + fourier_shape[1:], far)
    operands = [low, own, high, noise, even, odd]
    in_specs = [pl.BlockSpec((block,) + a.shape[1:], near) for a in operands[:3]]
    in_specs += [noise_block, table, table]
    aliases = {}
    if outs is not None:
        aliases = {8: 0, 9: 1}
        operands += list(outs)
        in_specs += [pl.BlockSpec(memory_space=pl.ANY)] * 2
    rows = slots * mem_local * parts * fields
    return pl.pallas_call(
        functools.partial(inverse_kernel, first, block),
        grid_spec=pltpu.PrefetchScalarGridSpec(
            num_scalar_prefetch=2,
            grid=(slots // block,),
            in_specs=in_specs,
            out_specs=[
                noise_block,
                fourier_block,
                pl.BlockSpec(TOKEN, lambda step, w, o: (0, 0)),
            ],
        ),
        out_shape=[
            jax.ShapeDtypeStruct(noise.shape, jnp.bfloat16),
            jax.ShapeDtypeStruct(fourier_shape, jnp.bfloat16),
            jax.ShapeDtypeStruct(TOKEN, jnp.float32),
        ],
        input_output_aliases=aliases,
        compiler_params=pltpu.CompilerParams(vmem_limit_bytes=VMEM_BYTES),
        cost_estimate=pl.CostEstimate(
            flops=4 * rows * truncation * latitudes,
            bytes_accessed=2 * rows * (5 * truncation + latitudes) + 4 * even.size,
            transcendentals=0,
        ),
        name="inverse",
    )(waves, offsets, *operands)


def copy_kernel(members, pieces, offsets, low, own, high, out, sems):
    rows_total, rows = out.shape[0], out.shape[1] // members
    size = rows_total // pieces
    sources = [(ref, at) for ref in (low, own, high) for at in range(ref.shape[1] // rows)]

    def copy(child, piece, source):
        ref, at = source
        part = pl.ds(piece * size, size)
        return pltpu.make_async_copy(
            ref.at[part, pl.ds(at * rows, rows)],
            out.at[part, pl.ds(child * rows, rows)],
            sems.at[child, piece],
        )

    for child in range(members):
        for index, source in enumerate(sources):

            @pl.when(offsets[child] == index)
            def _():
                for piece in range(pieces):
                    copy(child, piece, source).start()

    for child in range(members):
        for piece in range(pieces):
            copy(child, piece, sources[0]).wait()


def copy_parents(offsets, low, own, high):
    members = offsets.shape[0]
    pieces = math.gcd(own.shape[0], 4)
    anywhere = pl.BlockSpec(memory_space=pl.ANY)
    return pl.pallas_call(
        functools.partial(copy_kernel, members, pieces),
        in_specs=[pl.BlockSpec(memory_space=pltpu.SMEM)] + [anywhere] * 3,
        out_specs=anywhere,
        out_shape=jax.ShapeDtypeStruct(own.shape, own.dtype),
        scratch_shapes=[pltpu.SemaphoreType.DMA((members, pieces))],
        cost_estimate=pl.CostEstimate(flops=0, bytes_accessed=4 * own.size, transcendentals=0),
        name="parents",
    )(offsets, low, own, high)


def finish_kernel(first, block, waves, received, noise, even, odd, *rest):
    spectra_out, fourier_out = rest[-2:]
    truncation = even.shape[0]
    mem_local, parts, fields = noise.shape[1:4]
    step = pl.program_id(0)
    per_slot = received.shape[1] // block
    rows = jnp.concatenate([received[g] for g in range(received.shape[0])], axis=-1)
    contract = (((1,), (1,)), ((), ()))
    by_even = lax.dot_general(rows, even[...], contract, preferred_element_type=jnp.float32)
    by_odd = lax.dot_general(rows, odd[...], contract, preferred_element_type=jnp.float32)
    degree = lax.broadcasted_iota(jnp.int32, (per_slot, truncation), 1)
    even_rows, odd_rows = [], []
    for slot in range(block):
        wave = waves[first + step * block + slot]
        least = jnp.where(wave < truncation, wave, truncation)
        is_odd = wave % 2 == 1
        active = degree >= least
        here = slice(slot * per_slot, (slot + 1) * per_slot)
        spectra = jnp.where(is_odd, by_odd[here], by_even[here])
        spectra = spectra.astype(jnp.bfloat16).astype(jnp.float32)
        added = noise[slot].astype(jnp.float32).reshape(per_slot, truncation)
        child = jnp.where(active, spectra + added, 0.0)
        spectra_out[slot] = child.reshape(noise.shape[1:]).astype(spectra_out.dtype)
        even_rows.append(jnp.where(is_odd, 0.0, child).astype(jnp.bfloat16))
        odd_rows.append(jnp.where(is_odd, child, 0.0).astype(jnp.bfloat16))
    result = jnp.dot(
        jnp.concatenate(even_rows, axis=0), even[...], preferred_element_type=jnp.float32
    )
    result += jnp.dot(
        jnp.concatenate(odd_rows, axis=0), odd[...], preferred_element_type=jnp.float32
    )
    fourier_out[...] = result.reshape(fourier_out.shape).astype(fourier_out.dtype)


def finish_transform(waves, first, block, received, noise, even, odd, outs):
    slots_all, mem_local, parts, fields, truncation = noise.shape
    latitudes = even.shape[1]
    groups, all_rows, lat_local = received.shape
    per_slot = mem_local * parts * fields
    at = first // block
    far = lambda step, w: (at + step, 0, 0, 0, 0)
    table = pl.BlockSpec(even.shape, lambda step, w: (0, 0))
    noise_block = pl.BlockSpec((block,) + noise.shape[1:], far)
    fourier_shape = noise.shape[:4] + (latitudes,)
    fourier_block = pl.BlockSpec((block,) + fourier_shape[1:], far)
    received_block = pl.BlockSpec(
        (groups, block * per_slot, lat_local), lambda step, w: (0, step, 0)
    )
    return pl.pallas_call(
        functools.partial(finish_kernel, first, block),
        grid_spec=pltpu.PrefetchScalarGridSpec(
            num_scalar_prefetch=1,
            grid=(all_rows // (block * per_slot),),
            in_specs=[received_block, noise_block, table, table]
            + [pl.BlockSpec(memory_space=pl.ANY)] * 2,
            out_specs=[noise_block, fourier_block],
        ),
        out_shape=[
            jax.ShapeDtypeStruct(noise.shape, jnp.bfloat16),
            jax.ShapeDtypeStruct(fourier_shape, jnp.bfloat16),
        ],
        input_output_aliases={5: 0, 6: 1},
        compiler_params=pltpu.CompilerParams(vmem_limit_bytes=VMEM_BYTES),
        cost_estimate=pl.CostEstimate(
            flops=8 * all_rows * truncation * latitudes,
            bytes_accessed=2 * all_rows * (2 * truncation + 2 * latitudes) + 4 * even.size,
            transcendentals=0,
        ),
        name="finish",
    )(waves, received, noise, even, odd, *outs)


def chunk_bounds(slots_here, block):
    blocks = slots_here // block
    edges = [0, (blocks * 4 + 10) // 11, (blocks * 8 + 10) // 11, blocks]
    edges = [edge * block for edge in edges]
    return [(start, stop) for start, stop in zip(edges[:-1], edges[1:]) if stop > start]


def per_device(velocity, tracer, wave_slots, parents, noise):
    lat_count = lax.axis_size("lat")
    lat_index = lax.axis_index("lat")
    mem_count = lax.axis_size("member")
    group_index = lax.axis_index("member")
    mem_local, fields, lat_local, longitudes = velocity.shape
    slots_here, truncation = noise.shape[0], noise.shape[-1]
    block = math.gcd(slots_here, 8)
    per_member = 2 * fields
    per_slot = mem_local * per_member
    latitudes = lat_count * lat_local
    own_waves = lax.dynamic_slice_in_dim(wave_slots, lat_index * slots_here, slots_here)
    first_member = group_index * mem_local
    own_parents = lax.dynamic_slice_in_dim(parents, first_member, mem_local)
    offsets = own_parents - first_member + SPREAD
    upward = [(i, i + 1) for i in range(mem_count - 1)]
    downward = [(target, source) for source, target in upward]
    slot_grid = wave_slots.reshape(lat_count, slots_here)
    bounds = chunk_bounds(slots_here, block)
    inner = min(lat_local, LANES)
    starts = jnp.arange(latitudes // inner, dtype=jnp.int32) * inner

    def zonal(at):
        start, stop = bounds[at]
        factors = zonal_factors(slot_grid[:, start:stop].reshape(-1), longitudes, truncation)
        return zonal_transform(factors, velocity, tracer, [])

    def neighbours(rows, per_member):
        low = lax.ppermute(rows[:, rows.shape[1] - SPREAD * per_member :], "member", upward)
        high = lax.ppermute(rows[:, : SPREAD * per_member], "member", downward)
        return low, rows, high

    def exchanged(outgoing):
        outgoing = outgoing.reshape(lat_count, -1, lat_local)
        moved = lax.all_to_all(outgoing, "lat", split_axis=0, concat_axis=0, tiled=True)
        if lat_local % LANES != 0:
            moved = jnp.swapaxes(moved, 0, 1).reshape(1, -1, latitudes)
        return moved

    received = exchanged(zonal(0))
    even, odd = meridional_tables(truncation, latitudes, starts, inner)
    later = [copy_parents(offsets, *neighbours(zonal(at), per_member)) for at in range(1, len(bounds))]
    later = [exchanged(outgoing) for outgoing in later]
    spectra, _ = forward_transform(
        (own_waves, per_member), 0, block, received, even, odd, mem_local, []
    )
    *outs, _ = inverse_transform(
        own_waves, offsets, 0, block, *neighbours(spectra, 1), noise, even, odd, None
    )
    for (start, _), received in zip(bounds[1:], later):
        outs = finish_transform(own_waves, start, block, received, noise, even, odd, outs)
    return tuple(outs)


def solution(mesh):
    in_specs = (
        P("member", None, "lat", None),
        P("member", None, "lat", None),
        P(),
        P(),
        P("lat", "member", None, None, None),
    )
    out_specs = (P("lat", "member", None, None, None), P("lat", "member", None, None, None))
    return jax.shard_map(
        per_device, mesh=mesh, in_specs=in_specs, out_specs=out_specs, check_vma=False
    )
```

```python
import functools
import math

import jax
import jax.numpy as jnp
from jax import lax
from jax.experimental import pallas as pl
from jax.experimental.pallas import tpu as pltpu
from jax.sharding import PartitionSpec as P

SPREAD = 2
VMEM_BYTES = 48 * 1024 * 1024
LANES = 128
TOKEN = (8, 128)


def zonal_factors(wavenumbers, longitudes, truncation):
    coarse = jnp.arange(longitudes // LANES, dtype=jnp.int32) * LANES
    fine = jnp.arange(LANES, dtype=jnp.int32)
    weight = (wavenumbers < truncation).astype(jnp.float32) / math.sqrt(longitudes)

    def angles(points):
        phase = wavenumbers[:, None] * points[None, :] % longitudes
        return phase.astype(jnp.float32) * (2.0 * math.pi / longitudes)

    coarse_angle, fine_angle = angles(coarse), angles(fine)
    return (
        jnp.cos(coarse_angle) * weight[:, None],
        jnp.sin(coarse_angle) * weight[:, None],
        jnp.cos(fine_angle),
        jnp.sin(fine_angle),
    )


def meridional_factors(truncation, latitudes, starts, width):
    degree = jnp.arange(truncation, dtype=jnp.int32)

    def angles(points):
        phase = degree[:, None] * points[None, :] % (4 * latitudes)
        return phase.astype(jnp.float32) * (math.pi / (2 * latitudes))

    coarse = angles(2 * starts)
    fine = angles(2 * jnp.arange(width, dtype=jnp.int32) + 1)
    factor = math.sqrt(2.0 / latitudes)
    return jnp.cos(coarse) * factor, jnp.sin(coarse) * factor, jnp.cos(fine), jnp.sin(fine)


def tables_kernel(cos_c, sin_c, cos_f, sin_f, even, odd):
    width = cos_f.shape[1]
    cos_b, sin_b = cos_f[...], sin_f[...]
    for at in range(cos_c.shape[1]):
        cos_a, sin_a = cos_c[:, at : at + 1], sin_c[:, at : at + 1]
        columns = slice(at * width, (at + 1) * width)
        even[:, columns] = (cos_a * cos_b - sin_a * sin_b).astype(even.dtype)
        odd[:, columns] = (sin_a * cos_b + cos_a * sin_b).astype(odd.dtype)


def meridional_tables(truncation, latitudes, starts, width):
    factors = meridional_factors(truncation, latitudes, starts, width)
    shape = jax.ShapeDtypeStruct((truncation, starts.shape[0] * width), jnp.bfloat16)
    return pl.pallas_call(
        tables_kernel,
        out_shape=[shape, shape],
        compiler_params=pltpu.CompilerParams(vmem_limit_bytes=VMEM_BYTES),
        cost_estimate=pl.CostEstimate(
            flops=6 * truncation * latitudes, bytes_accessed=4 * truncation * latitudes,
            transcendentals=0,
        ),
        name="tables",
    )(*factors)


def zonal_kernel(
    fields_step, fields, tokens, cos_c, sin_c, cos_f, sin_f, velocity, tracer, *rest
):
    out, table, total = rest[tokens:]
    step = pl.program_id(0)
    rows = cos_f.shape[0]
    lat_local, longitudes = velocity.shape[2:]
    out_rows = out.shape[1]

    @pl.when(step == 0)
    def _():
        cos_b, sin_b = cos_f[...], sin_f[...]
        for at in range(longitudes // LANES):
            cos_a, sin_a = cos_c[:, at : at + 1], sin_c[:, at : at + 1]
            columns = slice(at * LANES, (at + 1) * LANES)
            table[:rows, columns] = (cos_a * cos_b - sin_a * sin_b).astype(table.dtype)
            table[rows:, columns] = (-sin_a * cos_b - cos_a * sin_b).astype(table.dtype)

    product = velocity[...].astype(jnp.float32) * tracer[...].astype(jnp.float32)
    product = product.astype(jnp.bfloat16).reshape(fields_step * lat_local, longitudes)
    sums = lax.dot_general(
        table[...], product, (((1,), (1,)), ((), ())), preferred_element_type=jnp.float32
    )
    steps_per_member = fields // fields_step
    member = step // steps_per_member
    first_field = step % steps_per_member * fields_step
    for part in range(2):
        for field in range(fields_step):
            row = (member * 2 + part) * fields + first_field + field
            total[pl.ds(row, rows, stride=out_rows), :] = sums[
                part * rows : (part + 1) * rows, field * lat_local : (field + 1) * lat_local
            ]

    @pl.when(step == pl.num_programs(0) - 1)
    def _():
        out[...] = total[...].reshape(out.shape).astype(out.dtype)


def zonal_transform(factors, velocity, tracer, tokens):
    mem_local, fields, lat_local, longitudes = velocity.shape
    rows = factors[0].shape[0]
    fields_step = min(fields, max(1, 512 // lat_local))
    steps = fields // fields_step
    out_rows = mem_local * 2 * fields
    whole = lambda step: (0, 0)
    grid_block = pl.BlockSpec(
        (1, fields_step, lat_local, longitudes), lambda step: (step // steps, step % steps, 0, 0)
    )
    flops = 2 * 2 * rows * longitudes * mem_local * fields * lat_local
    moved = 2 * velocity.size * 2 + rows * out_rows * lat_local * 2
    return pl.pallas_call(
        functools.partial(zonal_kernel, fields_step, fields, len(tokens)),
        grid=(mem_local * steps,),
        in_specs=[pl.BlockSpec(f.shape, whole) for f in factors]
        + [grid_block, grid_block]
        + [pl.BlockSpec(memory_space=pl.ANY)] * len(tokens),
        out_specs=pl.BlockSpec((rows, out_rows, lat_local), lambda step: (0, 0, 0)),
        out_shape=jax.ShapeDtypeStruct((rows, out_rows, lat_local), jnp.bfloat16),
        scratch_shapes=[
            pltpu.VMEM((2 * rows, longitudes), jnp.bfloat16),
            pltpu.VMEM((rows * out_rows, lat_local), jnp.float32),
        ],
        compiler_params=pltpu.CompilerParams(vmem_limit_bytes=VMEM_BYTES),
        cost_estimate=pl.CostEstimate(flops=flops, bytes_accessed=moved, transcendentals=0),
        name="zonal",
    )(*factors, velocity, tracer, *tokens)


def forward_kernel(first, block, waves, received, even, odd, *rest):
    out, token = rest[-2:]
    truncation = even.shape[0]
    step = pl.program_id(0)
    per_slot = received.shape[1] // block
    rows = jnp.concatenate([received[g] for g in range(received.shape[0])], axis=-1)
    contract = (((1,), (1,)), ((), ()))
    by_even = lax.dot_general(rows, even[...], contract, preferred_element_type=jnp.float32)
    by_odd = lax.dot_general(rows, odd[...], contract, preferred_element_type=jnp.float32)
    degree = lax.broadcasted_iota(jnp.int32, (per_slot, truncation), 1)
    for slot in range(block):
        wave = waves[first + step * block + slot]
        least = jnp.where(wave < truncation, wave, truncation)
        here = slice(slot * per_slot, (slot + 1) * per_slot)
        chosen = jnp.where(wave % 2 == 1, by_odd[here], by_even[here])
        chosen = jnp.where(degree >= least, chosen, 0.0)
        out[slot] = chosen.astype(out.dtype).reshape(out.shape[1:])
    token[...] = jnp.zeros_like(token)


def forward_transform(waves, first, block, received, even, odd, mem_local, tokens):
    groups, all_rows, lat_local = received.shape
    truncation, latitudes = even.shape
    slots = all_rows // (waves[1] * mem_local)
    out_shape = (slots, mem_local, waves[1], truncation)
    per_block = block * mem_local * waves[1]
    table = pl.BlockSpec(even.shape, lambda step, w: (0, 0))
    return pl.pallas_call(
        functools.partial(forward_kernel, first, block),
        grid_spec=pltpu.PrefetchScalarGridSpec(
            num_scalar_prefetch=1,
            grid=(slots // block,),
            in_specs=[
                pl.BlockSpec((groups, per_block, lat_local), lambda step, w: (0, step, 0)),
                table,
                table,
            ]
            + [pl.BlockSpec(memory_space=pl.ANY)] * len(tokens),
            out_specs=[
                pl.BlockSpec((block,) + out_shape[1:], lambda step, w: (step, 0, 0, 0)),
                pl.BlockSpec(TOKEN, lambda step, w: (0, 0)),
            ],
        ),
        out_shape=[
            jax.ShapeDtypeStruct(out_shape, jnp.bfloat16),
            jax.ShapeDtypeStruct(TOKEN, jnp.float32),
        ],
        compiler_params=pltpu.CompilerParams(vmem_limit_bytes=VMEM_BYTES),
        cost_estimate=pl.CostEstimate(
            flops=4 * all_rows * truncation * latitudes,
            bytes_accessed=2 * (all_rows * latitudes + 2 * even.size + all_rows * truncation),
            transcendentals=0,
        ),
        name="forward",
    )(waves[0], received, even, odd, *tokens)


def inverse_kernel(first, block, waves, offsets, low, own, high, noise, even, odd, *rest):
    spectra_out, fourier_out, token = rest[-3:]
    token[...] = jnp.zeros_like(token)
    truncation, latitudes = even.shape
    step = pl.program_id(0)
    mem_local, parts, fields = noise.shape[1:4]
    degree = lax.broadcasted_iota(jnp.int32, (fields, truncation), 1)
    sources = [low[:, m] for m in range(low.shape[1])]
    sources += [own[:, m] for m in range(own.shape[1])]
    sources += [high[:, m] for m in range(high.shape[1])]
    even_rows, odd_rows = [], []
    parents = []
    for child in range(mem_local):
        parent = sources[0]
        for at in range(1, len(sources)):
            parent = jnp.where(offsets[child] == at, sources[at], parent)
        parents.append(parent)
    for slot in range(block):
        wave = waves[first + step * block + slot]
        least = jnp.where(wave < truncation, wave, truncation)
        is_odd = wave % 2 == 1
        active = degree >= least
        for child in range(mem_local):
            parent = parents[child][slot].astype(jnp.float32)
            parent = parent.reshape(parts, fields, truncation)
            added = jnp.where(active[None], noise[slot, child].astype(jnp.float32), 0.0)
            total = parent + added
            spectra_out[slot, child] = total.astype(spectra_out.dtype)
            rows = total.reshape(parts * fields, truncation)
            even_rows.append(jnp.where(is_odd, 0.0, rows).astype(jnp.bfloat16))
            odd_rows.append(jnp.where(is_odd, rows, 0.0).astype(jnp.bfloat16))
    result = jnp.dot(
        jnp.concatenate(even_rows, axis=0), even[...], preferred_element_type=jnp.float32
    )
    result += jnp.dot(
        jnp.concatenate(odd_rows, axis=0), odd[...], preferred_element_type=jnp.float32
    )
    fourier_out[...] = result.reshape(fourier_out.shape).astype(fourier_out.dtype)


def inverse_transform(waves, offsets, first, block, low, own, high, noise, even, odd, outs):
    slots_all, mem_local, parts, fields, truncation = noise.shape
    latitudes = even.shape[1]
    slots = own.shape[0]
    at = first // block
    near = lambda step, w, o: (step, 0, 0, 0)
    far = lambda step, w, o: (at + step, 0, 0, 0, 0)
    table = pl.BlockSpec(even.shape, lambda step, w, o: (0, 0))
    noise_block = pl.BlockSpec((block,) + noise.shape[1:], far)
    fourier_shape = noise.shape[:4] + (latitudes,)
    fourier_block = pl.BlockSpec((block,) + fourier_shape[1:], far)
    operands = [low, own, high, noise, even, odd]
    in_specs = [pl.BlockSpec((block,) + a.shape[1:], near) for a in operands[:3]]
    in_specs += [noise_block, table, table]
    aliases = {}
    if outs is not None:
        aliases = {8: 0, 9: 1}
        operands += list(outs)
        in_specs += [pl.BlockSpec(memory_space=pl.ANY)] * 2
    rows = slots * mem_local * parts * fields
    return pl.pallas_call(
        functools.partial(inverse_kernel, first, block),
        grid_spec=pltpu.PrefetchScalarGridSpec(
            num_scalar_prefetch=2,
            grid=(slots // block,),
            in_specs=in_specs,
            out_specs=[
                noise_block,
                fourier_block,
                pl.BlockSpec(TOKEN, lambda step, w, o: (0, 0)),
            ],
        ),
        out_shape=[
            jax.ShapeDtypeStruct(noise.shape, jnp.bfloat16),
            jax.ShapeDtypeStruct(fourier_shape, jnp.bfloat16),
            jax.ShapeDtypeStruct(TOKEN, jnp.float32),
        ],
        input_output_aliases=aliases,
        compiler_params=pltpu.CompilerParams(vmem_limit_bytes=VMEM_BYTES),
        cost_estimate=pl.CostEstimate(
            flops=4 * rows * truncation * latitudes,
            bytes_accessed=2 * rows * (5 * truncation + latitudes) + 4 * even.size,
            transcendentals=0,
        ),
        name="inverse",
    )(waves, offsets, *operands)


def copy_kernel(offsets, low, own, high, out):
    rows = out.shape[1] // offsets.shape[0]
    for child in range(offsets.shape[0]):
        index, chosen = 0, None
        for source in (low, own, high):
            for at in range(source.shape[1] // rows):
                value = source[:, at * rows : (at + 1) * rows]
                chosen = value if index == 0 else jnp.where(offsets[child] == index, value, chosen)
                index += 1
        out[:, child * rows : (child + 1) * rows] = chosen


def copy_parents(offsets, low, own, high):
    steps = math.gcd(own.shape[0], 4)
    block = lambda array: pl.BlockSpec(
        (array.shape[0] // steps,) + array.shape[1:], lambda step, o: (step, 0, 0)
    )
    return pl.pallas_call(
        copy_kernel,
        grid_spec=pltpu.PrefetchScalarGridSpec(
            num_scalar_prefetch=1,
            grid=(steps,),
            in_specs=[block(low), block(own), block(high)],
            out_specs=block(own),
        ),
        out_shape=jax.ShapeDtypeStruct(own.shape, own.dtype),
        compiler_params=pltpu.CompilerParams(vmem_limit_bytes=VMEM_BYTES),
        cost_estimate=pl.CostEstimate(flops=0, bytes_accessed=8 * own.size, transcendentals=0),
        name="parents",
    )(offsets, low, own, high)


def finish_kernel(first, block, waves, received, noise, even, odd, *rest):
    spectra_out, fourier_out = rest[-2:]
    truncation = even.shape[0]
    mem_local, parts, fields = noise.shape[1:4]
    step = pl.program_id(0)
    per_slot = received.shape[1] // block
    rows = jnp.concatenate([received[g] for g in range(received.shape[0])], axis=-1)
    contract = (((1,), (1,)), ((), ()))
    by_even = lax.dot_general(rows, even[...], contract, preferred_element_type=jnp.float32)
    by_odd = lax.dot_general(rows, odd[...], contract, preferred_element_type=jnp.float32)
    degree = lax.broadcasted_iota(jnp.int32, (per_slot, truncation), 1)
    even_rows, odd_rows = [], []
    for slot in range(block):
        wave = waves[first + step * block + slot]
        least = jnp.where(wave < truncation, wave, truncation)
        is_odd = wave % 2 == 1
        active = degree >= least
        here = slice(slot * per_slot, (slot + 1) * per_slot)
        spectra = jnp.where(is_odd, by_odd[here], by_even[here])
        spectra = spectra.astype(jnp.bfloat16).astype(jnp.float32)
        added = noise[slot].astype(jnp.float32).reshape(per_slot, truncation)
        child = jnp.where(active, spectra + added, 0.0)
        spectra_out[slot] = child.reshape(noise.shape[1:]).astype(spectra_out.dtype)
        even_rows.append(jnp.where(is_odd, 0.0, child).astype(jnp.bfloat16))
        odd_rows.append(jnp.where(is_odd, child, 0.0).astype(jnp.bfloat16))
    result = jnp.dot(
        jnp.concatenate(even_rows, axis=0), even[...], preferred_element_type=jnp.float32
    )
    result += jnp.dot(
        jnp.concatenate(odd_rows, axis=0), odd[...], preferred_element_type=jnp.float32
    )
    fourier_out[...] = result.reshape(fourier_out.shape).astype(fourier_out.dtype)


def finish_transform(waves, first, block, received, noise, even, odd, outs):
    slots_all, mem_local, parts, fields, truncation = noise.shape
    latitudes = even.shape[1]
    groups, all_rows, lat_local = received.shape
    per_slot = mem_local * parts * fields
    at = first // block
    far = lambda step, w: (at + step, 0, 0, 0, 0)
    table = pl.BlockSpec(even.shape, lambda step, w: (0, 0))
    noise_block = pl.BlockSpec((block,) + noise.shape[1:], far)
    fourier_shape = noise.shape[:4] + (latitudes,)
    fourier_block = pl.BlockSpec((block,) + fourier_shape[1:], far)
    received_block = pl.BlockSpec(
        (groups, block * per_slot, lat_local), lambda step, w: (0, step, 0)
    )
    return pl.pallas_call(
        functools.partial(finish_kernel, first, block),
        grid_spec=pltpu.PrefetchScalarGridSpec(
            num_scalar_prefetch=1,
            grid=(all_rows // (block * per_slot),),
            in_specs=[received_block, noise_block, table, table]
            + [pl.BlockSpec(memory_space=pl.ANY)] * 2,
            out_specs=[noise_block, fourier_block],
        ),
        out_shape=[
            jax.ShapeDtypeStruct(noise.shape, jnp.bfloat16),
            jax.ShapeDtypeStruct(fourier_shape, jnp.bfloat16),
        ],
        input_output_aliases={5: 0, 6: 1},
        compiler_params=pltpu.CompilerParams(vmem_limit_bytes=VMEM_BYTES),
        cost_estimate=pl.CostEstimate(
            flops=8 * all_rows * truncation * latitudes,
            bytes_accessed=2 * all_rows * (2 * truncation + 2 * latitudes) + 4 * even.size,
            transcendentals=0,
        ),
        name="finish",
    )(waves, received, noise, even, odd, *outs)


def chunk_bounds(slots_here, block):
    blocks = slots_here // block
    edges = [0, (blocks * 5 + 10) // 11, (blocks * 9 + 10) // 11, blocks]
    edges = [edge * block for edge in edges]
    return [(start, stop) for start, stop in zip(edges[:-1], edges[1:]) if stop > start]


def per_device(velocity, tracer, wave_slots, parents, noise):
    lat_count = lax.axis_size("lat")
    lat_index = lax.axis_index("lat")
    mem_count = lax.axis_size("member")
    group_index = lax.axis_index("member")
    mem_local, fields, lat_local, longitudes = velocity.shape
    slots_here, truncation = noise.shape[0], noise.shape[-1]
    block = math.gcd(slots_here, 8)
    per_member = 2 * fields
    per_slot = mem_local * per_member
    latitudes = lat_count * lat_local
    own_waves = lax.dynamic_slice_in_dim(wave_slots, lat_index * slots_here, slots_here)
    first_member = group_index * mem_local
    own_parents = lax.dynamic_slice_in_dim(parents, first_member, mem_local)
    offsets = own_parents - first_member + SPREAD
    upward = [(i, i + 1) for i in range(mem_count - 1)]
    downward = [(target, source) for source, target in upward]
    slot_grid = wave_slots.reshape(lat_count, slots_here)
    bounds = chunk_bounds(slots_here, block)
    inner = min(lat_local, LANES)
    starts = jnp.arange(latitudes // inner, dtype=jnp.int32) * inner

    def zonal(at):
        start, stop = bounds[at]
        factors = zonal_factors(slot_grid[:, start:stop].reshape(-1), longitudes, truncation)
        return zonal_transform(factors, velocity, tracer, [])

    def neighbours(rows, per_member):
        low = lax.ppermute(rows[:, rows.shape[1] - SPREAD * per_member :], "member", upward)
        high = lax.ppermute(rows[:, : SPREAD * per_member], "member", downward)
        return low, rows, high

    def exchanged(outgoing):
        outgoing = outgoing.reshape(lat_count, -1, lat_local)
        moved = lax.all_to_all(outgoing, "lat", split_axis=0, concat_axis=0, tiled=True)
        if lat_local % LANES != 0:
            moved = jnp.swapaxes(moved, 0, 1).reshape(1, -1, latitudes)
        return moved

    received = exchanged(zonal(0))
    even, odd = meridional_tables(truncation, latitudes, starts, inner)
    later = [copy_parents(offsets, *neighbours(zonal(at), per_member)) for at in range(1, len(bounds))]
    later = [exchanged(outgoing) for outgoing in later]
    spectra, _ = forward_transform(
        (own_waves, per_member), 0, block, received, even, odd, mem_local, []
    )
    *outs, _ = inverse_transform(
        own_waves, offsets, 0, block, *neighbours(spectra, 1), noise, even, odd, None
    )
    for (start, _), received in zip(bounds[1:], later):
        outs = finish_transform(own_waves, start, block, received, noise, even, odd, outs)
    return tuple(outs)


def solution(mesh):
    in_specs = (
        P("member", None, "lat", None),
        P("member", None, "lat", None),
        P(),
        P(),
        P("lat", "member", None, None, None),
    )
    out_specs = (P("lat", "member", None, None, None), P("lat", "member", None, None, None))
    return jax.shard_map(
        per_device, mesh=mesh, in_specs=in_specs, out_specs=out_specs, check_vma=False
    )
```

```python
import functools
import math

import jax
import jax.numpy as jnp
from jax import lax
from jax.experimental import pallas as pl
from jax.experimental.pallas import tpu as pltpu
from jax.sharding import PartitionSpec as P

SPREAD = 2
VMEM_BYTES = 24 * 1024 * 1024
ZONAL_BYTES = 44 * 1024 * 1024
LANES = 128
SUBLANES = 8
TOKEN = (8, 128)


def meridional_factors(truncation, latitudes, starts, width):
    degree = jnp.arange(truncation, dtype=jnp.int32)

    def angles(points):
        phase = degree[:, None] * points[None, :] % (4 * latitudes)
        return phase.astype(jnp.float32) * (math.pi / (2 * latitudes))

    coarse = angles(2 * starts)
    fine = angles(2 * jnp.arange(width, dtype=jnp.int32) + 1)
    factor = math.sqrt(2.0 / latitudes)
    return jnp.cos(coarse) * factor, jnp.sin(coarse) * factor, jnp.cos(fine), jnp.sin(fine)


def tables_kernel(cos_c, sin_c, cos_f, sin_f, even, odd):
    width = cos_f.shape[1]
    cos_b, sin_b = cos_f[...], sin_f[...]
    for at in range(cos_c.shape[1]):
        cos_a, sin_a = cos_c[:, at : at + 1], sin_c[:, at : at + 1]
        columns = slice(at * width, (at + 1) * width)
        even[:, columns] = (cos_a * cos_b - sin_a * sin_b).astype(even.dtype)
        odd[:, columns] = (sin_a * cos_b + cos_a * sin_b).astype(odd.dtype)


def meridional_tables(truncation, latitudes, starts, width):
    factors = meridional_factors(truncation, latitudes, starts, width)
    shape = jax.ShapeDtypeStruct((truncation, starts.shape[0] * width), jnp.bfloat16)
    return pl.pallas_call(
        tables_kernel,
        out_shape=[shape, shape],
        compiler_params=pltpu.CompilerParams(vmem_limit_bytes=VMEM_BYTES),
        cost_estimate=pl.CostEstimate(
            flops=6 * truncation * latitudes, bytes_accessed=4 * truncation * latitudes,
            transcendentals=0,
        ),
        name="tables",
    )(*factors)


def zonal_kernel(truncation, tokens, waves, velocity, tracer, *rest):
    out, table, total, velocity_here, tracer_here, sems = rest[tokens:]
    members, fields, lat_local, longitudes = velocity.shape
    rows = waves.shape[0]
    groups = velocity_here.shape[0]
    step_fields = velocity_here.shape[1]
    steps = fields // step_fields

    def copies(step):
        part = (step // steps, pl.ds(step % steps * step_fields, step_fields))
        return [
            pltpu.make_async_copy(source.at[part], target.at[step], sems.at[step, at])
            for at, (source, target) in enumerate(
                ((velocity, velocity_here), (tracer, tracer_here))
            )
        ]

    for step in range(groups):
        for copy in copies(step):
            copy.start()

    wave = waves[...]
    weight = jnp.where(wave < truncation, 1.0 / math.sqrt(longitudes), 0.0)

    def angles(count, stride):
        points = lax.broadcasted_iota(jnp.int32, (rows, count), 1) * stride
        phase = lax.rem(wave * points, jnp.full((), longitudes, jnp.int32))
        return phase.astype(jnp.float32) * (2.0 * math.pi / longitudes)

    coarse, fine = angles(longitudes // LANES, LANES), angles(LANES, 1)
    cos_c, sin_c = jnp.cos(coarse) * weight, jnp.sin(coarse) * weight
    cos_f, sin_f = jnp.cos(fine), jnp.sin(fine)
    for at in range(longitudes // LANES):
        cos_a, sin_a = cos_c[:, at : at + 1], sin_c[:, at : at + 1]
        columns = slice(at * LANES, (at + 1) * LANES)
        table[:rows, columns] = (cos_a * cos_f - sin_a * sin_f).astype(table.dtype)
        table[rows:, columns] = (-sin_a * cos_f - cos_a * sin_f).astype(table.dtype)

    def body(step, carry):
        for copy in copies(step):
            copy.wait()
        product = velocity_here[step].astype(jnp.float32) * tracer_here[step].astype(jnp.float32)
        product = product.astype(jnp.bfloat16).reshape(step_fields * lat_local, longitudes)
        sums = lax.dot_general(
            table[...], product, (((1,), (1,)), ((), ())), preferred_element_type=jnp.float32
        )
        first = step // steps * 2 * fields + step % steps * step_fields
        for part in range(2):
            for field in range(step_fields):
                block = sums[
                    part * rows : (part + 1) * rows, field * lat_local : (field + 1) * lat_local
                ]
                total[:, first + part * fields + field] = block.reshape(
                    rows // SUBLANES, SUBLANES, lat_local
                )
        return carry

    lax.fori_loop(0, groups, body, 0)

    def turn(at, carry):
        first = pl.multiple_of(at * SUBLANES, SUBLANES)
        out[pl.ds(first, SUBLANES)] = jnp.swapaxes(total[at], 0, 1).astype(out.dtype)
        return carry

    lax.fori_loop(0, rows // SUBLANES, turn, 0)


def zonal_transform(waves, truncation, velocity, tracer, tokens):
    mem_local, fields, lat_local, longitudes = velocity.shape
    rows = waves.shape[0]
    fields_step = min(fields, max(1, 512 // lat_local))
    groups = mem_local * (fields // fields_step)
    out_rows = mem_local * 2 * fields
    grid_part = pltpu.VMEM((groups, fields_step, lat_local, longitudes), velocity.dtype)
    flops = 2 * 2 * rows * longitudes * mem_local * fields * lat_local
    moved = 2 * velocity.size * 2 + rows * out_rows * lat_local * 2
    return pl.pallas_call(
        functools.partial(zonal_kernel, truncation, len(tokens)),
        in_specs=[pl.BlockSpec(memory_space=pltpu.VMEM)]
        + [pl.BlockSpec(memory_space=pl.ANY)] * (2 + len(tokens)),
        out_specs=pl.BlockSpec(memory_space=pltpu.VMEM),
        out_shape=jax.ShapeDtypeStruct((rows, out_rows, lat_local), jnp.bfloat16),
        scratch_shapes=[
            pltpu.VMEM((2 * rows, longitudes), jnp.bfloat16),
            pltpu.VMEM((rows // SUBLANES, out_rows, SUBLANES, lat_local), jnp.float32),
            grid_part,
            grid_part,
            pltpu.SemaphoreType.DMA((groups, 2)),
        ],
        compiler_params=pltpu.CompilerParams(vmem_limit_bytes=ZONAL_BYTES),
        cost_estimate=pl.CostEstimate(flops=flops, bytes_accessed=moved, transcendentals=0),
        name="zonal",
    )(waves, velocity, tracer, *tokens)


def forward_kernel(first, block, waves, received, even, odd, *rest):
    out, token = rest[-2:]
    truncation = even.shape[0]
    step = pl.program_id(0)
    per_slot = received.shape[1] // block
    rows = jnp.concatenate([received[g] for g in range(received.shape[0])], axis=-1)
    contract = (((1,), (1,)), ((), ()))
    by_even = lax.dot_general(rows, even[...], contract, preferred_element_type=jnp.float32)
    by_odd = lax.dot_general(rows, odd[...], contract, preferred_element_type=jnp.float32)
    degree = lax.broadcasted_iota(jnp.int32, (per_slot, truncation), 1)
    for slot in range(block):
        wave = waves[first + step * block + slot]
        least = jnp.where(wave < truncation, wave, truncation)
        here = slice(slot * per_slot, (slot + 1) * per_slot)
        chosen = jnp.where(wave % 2 == 1, by_odd[here], by_even[here])
        chosen = jnp.where(degree >= least, chosen, 0.0)
        out[slot] = chosen.astype(out.dtype).reshape(out.shape[1:])
    token[...] = jnp.zeros_like(token)


def forward_transform(waves, first, block, received, even, odd, mem_local, tokens):
    groups, all_rows, lat_local = received.shape
    truncation, latitudes = even.shape
    slots = all_rows // (waves[1] * mem_local)
    out_shape = (slots, mem_local, waves[1], truncation)
    per_block = block * mem_local * waves[1]
    table = pl.BlockSpec(even.shape, lambda step, w: (0, 0))
    return pl.pallas_call(
        functools.partial(forward_kernel, first, block),
        grid_spec=pltpu.PrefetchScalarGridSpec(
            num_scalar_prefetch=1,
            grid=(slots // block,),
            in_specs=[
                pl.BlockSpec((groups, per_block, lat_local), lambda step, w: (0, step, 0)),
                table,
                table,
            ]
            + [pl.BlockSpec(memory_space=pl.ANY)] * len(tokens),
            out_specs=[
                pl.BlockSpec((block,) + out_shape[1:], lambda step, w: (step, 0, 0, 0)),
                pl.BlockSpec(TOKEN, lambda step, w: (0, 0)),
            ],
        ),
        out_shape=[
            jax.ShapeDtypeStruct(out_shape, jnp.bfloat16),
            jax.ShapeDtypeStruct(TOKEN, jnp.float32),
        ],
        compiler_params=pltpu.CompilerParams(vmem_limit_bytes=VMEM_BYTES),
        cost_estimate=pl.CostEstimate(
            flops=4 * all_rows * truncation * latitudes,
            bytes_accessed=2 * (all_rows * latitudes + 2 * even.size + all_rows * truncation),
            transcendentals=0,
        ),
        name="forward",
    )(waves[0], received, even, odd, *tokens)


def inverse_kernel(first, block, waves, offsets, low, own, high, noise, even, odd, *rest):
    spectra_out, fourier_out, token = rest[-3:]
    token[...] = jnp.zeros_like(token)
    truncation, latitudes = even.shape
    step = pl.program_id(0)
    mem_local, parts, fields = noise.shape[1:4]
    degree = lax.broadcasted_iota(jnp.int32, (fields, truncation), 1)
    sources = [low[:, m] for m in range(low.shape[1])]
    sources += [own[:, m] for m in range(own.shape[1])]
    sources += [high[:, m] for m in range(high.shape[1])]
    even_rows, odd_rows = [], []
    parents = []
    for child in range(mem_local):
        parent = sources[0]
        for at in range(1, len(sources)):
            parent = jnp.where(offsets[child] == at, sources[at], parent)
        parents.append(parent)
    for slot in range(block):
        wave = waves[first + step * block + slot]
        least = jnp.where(wave < truncation, wave, truncation)
        is_odd = wave % 2 == 1
        active = degree >= least
        for child in range(mem_local):
            parent = parents[child][slot].astype(jnp.float32)
            parent = parent.reshape(parts, fields, truncation)
            added = jnp.where(active[None], noise[slot, child].astype(jnp.float32), 0.0)
            total = parent + added
            spectra_out[slot, child] = total.astype(spectra_out.dtype)
            rows = total.reshape(parts * fields, truncation)
            even_rows.append(jnp.where(is_odd, 0.0, rows).astype(jnp.bfloat16))
            odd_rows.append(jnp.where(is_odd, rows, 0.0).astype(jnp.bfloat16))
    result = jnp.dot(
        jnp.concatenate(even_rows, axis=0), even[...], preferred_element_type=jnp.float32
    )
    result += jnp.dot(
        jnp.concatenate(odd_rows, axis=0), odd[...], preferred_element_type=jnp.float32
    )
    fourier_out[...] = result.reshape(fourier_out.shape).astype(fourier_out.dtype)


def inverse_transform(waves, offsets, first, block, low, own, high, noise, even, odd, outs):
    slots_all, mem_local, parts, fields, truncation = noise.shape
    latitudes = even.shape[1]
    slots = own.shape[0]
    at = first // block
    near = lambda step, w, o: (step, 0, 0, 0)
    far = lambda step, w, o: (at + step, 0, 0, 0, 0)
    table = pl.BlockSpec(even.shape, lambda step, w, o: (0, 0))
    noise_block = pl.BlockSpec((block,) + noise.shape[1:], far)
    fourier_shape = noise.shape[:4] + (latitudes,)
    fourier_block = pl.BlockSpec((block,) + fourier_shape[1:], far)
    operands = [low, own, high, noise, even, odd]
    in_specs = [pl.BlockSpec((block,) + a.shape[1:], near) for a in operands[:3]]
    in_specs += [noise_block, table, table]
    aliases = {}
    if outs is not None:
        aliases = {8: 0, 9: 1}
        operands += list(outs)
        in_specs += [pl.BlockSpec(memory_space=pl.ANY)] * 2
    rows = slots * mem_local * parts * fields
    return pl.pallas_call(
        functools.partial(inverse_kernel, first, block),
        grid_spec=pltpu.PrefetchScalarGridSpec(
            num_scalar_prefetch=2,
            grid=(slots // block,),
            in_specs=in_specs,
            out_specs=[
                noise_block,
                fourier_block,
                pl.BlockSpec(TOKEN, lambda step, w, o: (0, 0)),
            ],
        ),
        out_shape=[
            jax.ShapeDtypeStruct(noise.shape, jnp.bfloat16),
            jax.ShapeDtypeStruct(fourier_shape, jnp.bfloat16),
            jax.ShapeDtypeStruct(TOKEN, jnp.float32),
        ],
        input_output_aliases=aliases,
        compiler_params=pltpu.CompilerParams(vmem_limit_bytes=VMEM_BYTES),
        cost_estimate=pl.CostEstimate(
            flops=4 * rows * truncation * latitudes,
            bytes_accessed=2 * rows * (5 * truncation + latitudes) + 4 * even.size,
            transcendentals=0,
        ),
        name="inverse",
    )(waves, offsets, *operands)


def copy_kernel(offsets, low, own, high, *rest):
    out = rest[-1]
    rows = out.shape[1] // offsets.shape[0]
    for child in range(offsets.shape[0]):
        index, chosen = 0, None
        for source in (low, own, high):
            for at in range(source.shape[1] // rows):
                value = source[:, at * rows : (at + 1) * rows]
                chosen = value if index == 0 else jnp.where(offsets[child] == index, value, chosen)
                index += 1
        out[:, child * rows : (child + 1) * rows] = chosen


def copy_parents(offsets, low, own, high, tokens):
    steps = math.gcd(own.shape[0], 4)
    block = lambda array: pl.BlockSpec(
        (array.shape[0] // steps,) + array.shape[1:], lambda step, o: (step, 0, 0)
    )
    return pl.pallas_call(
        copy_kernel,
        grid_spec=pltpu.PrefetchScalarGridSpec(
            num_scalar_prefetch=1,
            grid=(steps,),
            in_specs=[block(low), block(own), block(high)]
            + [pl.BlockSpec(memory_space=pl.ANY)] * len(tokens),
            out_specs=block(own),
        ),
        out_shape=jax.ShapeDtypeStruct(own.shape, own.dtype),
        compiler_params=pltpu.CompilerParams(vmem_limit_bytes=VMEM_BYTES),
        cost_estimate=pl.CostEstimate(flops=0, bytes_accessed=8 * own.size, transcendentals=0),
        name="parents",
    )(offsets, low, own, high, *tokens)


def finish_kernel(first, block, waves, received, noise, even, odd, *rest):
    spectra_out, fourier_out = rest[-2:]
    truncation = even.shape[0]
    mem_local, parts, fields = noise.shape[1:4]
    step = pl.program_id(0)
    per_slot = received.shape[1] // block
    rows = jnp.concatenate([received[g] for g in range(received.shape[0])], axis=-1)
    contract = (((1,), (1,)), ((), ()))
    by_even = lax.dot_general(rows, even[...], contract, preferred_element_type=jnp.float32)
    by_odd = lax.dot_general(rows, odd[...], contract, preferred_element_type=jnp.float32)
    degree = lax.broadcasted_iota(jnp.int32, (per_slot, truncation), 1)
    even_rows, odd_rows = [], []
    for slot in range(block):
        wave = waves[first + step * block + slot]
        least = jnp.where(wave < truncation, wave, truncation)
        is_odd = wave % 2 == 1
        active = degree >= least
        here = slice(slot * per_slot, (slot + 1) * per_slot)
        spectra = jnp.where(is_odd, by_odd[here], by_even[here])
        spectra = spectra.astype(jnp.bfloat16).astype(jnp.float32)
        added = noise[slot].astype(jnp.float32).reshape(per_slot, truncation)
        child = jnp.where(active, spectra + added, 0.0)
        spectra_out[slot] = child.reshape(noise.shape[1:]).astype(spectra_out.dtype)
        even_rows.append(jnp.where(is_odd, 0.0, child).astype(jnp.bfloat16))
        odd_rows.append(jnp.where(is_odd, child, 0.0).astype(jnp.bfloat16))
    result = jnp.dot(
        jnp.concatenate(even_rows, axis=0), even[...], preferred_element_type=jnp.float32
    )
    result += jnp.dot(
        jnp.concatenate(odd_rows, axis=0), odd[...], preferred_element_type=jnp.float32
    )
    fourier_out[...] = result.reshape(fourier_out.shape).astype(fourier_out.dtype)


def finish_transform(waves, first, block, received, noise, even, odd, outs):
    slots_all, mem_local, parts, fields, truncation = noise.shape
    latitudes = even.shape[1]
    groups, all_rows, lat_local = received.shape
    per_slot = mem_local * parts * fields
    at = first // block
    far = lambda step, w: (at + step, 0, 0, 0, 0)
    table = pl.BlockSpec(even.shape, lambda step, w: (0, 0))
    noise_block = pl.BlockSpec((block,) + noise.shape[1:], far)
    fourier_shape = noise.shape[:4] + (latitudes,)
    fourier_block = pl.BlockSpec((block,) + fourier_shape[1:], far)
    received_block = pl.BlockSpec(
        (groups, block * per_slot, lat_local), lambda step, w: (0, step, 0)
    )
    return pl.pallas_call(
        functools.partial(finish_kernel, first, block),
        grid_spec=pltpu.PrefetchScalarGridSpec(
            num_scalar_prefetch=1,
            grid=(all_rows // (block * per_slot),),
            in_specs=[received_block, noise_block, table, table]
            + [pl.BlockSpec(memory_space=pl.ANY)] * 2,
            out_specs=[noise_block, fourier_block],
        ),
        out_shape=[
            jax.ShapeDtypeStruct(noise.shape, jnp.bfloat16),
            jax.ShapeDtypeStruct(fourier_shape, jnp.bfloat16),
        ],
        input_output_aliases={5: 0, 6: 1},
        compiler_params=pltpu.CompilerParams(vmem_limit_bytes=VMEM_BYTES),
        cost_estimate=pl.CostEstimate(
            flops=8 * all_rows * truncation * latitudes,
            bytes_accessed=2 * all_rows * (2 * truncation + 2 * latitudes) + 4 * even.size,
            transcendentals=0,
        ),
        name="finish",
    )(waves, received, noise, even, odd, *outs)


def chunk_bounds(slots_here, block):
    blocks = slots_here // block
    edges = [0, (blocks * 5 + 10) // 11, (blocks * 10 + 10) // 11, blocks]
    edges = [edge * block for edge in edges]
    return [(start, stop) for start, stop in zip(edges[:-1], edges[1:]) if stop > start]


def per_device(velocity, tracer, wave_slots, parents, noise):
    lat_count = lax.axis_size("lat")
    lat_index = lax.axis_index("lat")
    mem_count = lax.axis_size("member")
    group_index = lax.axis_index("member")
    mem_local, fields, lat_local, longitudes = velocity.shape
    slots_here, truncation = noise.shape[0], noise.shape[-1]
    block = math.gcd(slots_here, 8)
    per_member = 2 * fields
    per_slot = mem_local * per_member
    latitudes = lat_count * lat_local
    own_waves = lax.dynamic_slice_in_dim(wave_slots, lat_index * slots_here, slots_here)
    first_member = group_index * mem_local
    own_parents = lax.dynamic_slice_in_dim(parents, first_member, mem_local)
    offsets = own_parents - first_member + SPREAD
    upward = [(i, i + 1) for i in range(mem_count - 1)]
    downward = [(target, source) for source, target in upward]
    slot_grid = wave_slots.reshape(lat_count, slots_here)
    bounds = chunk_bounds(slots_here, block)
    inner = min(lat_local, LANES)
    starts = jnp.arange(latitudes // inner, dtype=jnp.int32) * inner

    def zonal(at):
        start, stop = bounds[at]
        waves = slot_grid[:, start:stop].reshape(-1, 1)
        return zonal_transform(waves, truncation, velocity, tracer, [])

    def neighbours(rows, per_member):
        low = lax.ppermute(rows[:, rows.shape[1] - SPREAD * per_member :], "member", upward)
        high = lax.ppermute(rows[:, : SPREAD * per_member], "member", downward)
        return low, rows, high

    def exchanged(outgoing):
        outgoing = outgoing.reshape(lat_count, -1, lat_local)
        moved = lax.all_to_all(outgoing, "lat", split_axis=0, concat_axis=0, tiled=True)
        if lat_local % LANES != 0:
            moved = jnp.swapaxes(moved, 0, 1).reshape(1, -1, latitudes)
        return moved

    def copied(at, tokens):
        return copy_parents(offsets, *neighbours(zonal(at), per_member), tokens)

    received = exchanged(zonal(0))
    even, odd = meridional_tables(truncation, latitudes, starts, inner)
    later = [exchanged(copied(1, []))] if len(bounds) > 1 else []
    spectra, _ = forward_transform(
        (own_waves, per_member), 0, block, received, even, odd, mem_local, []
    )
    *outs, token = inverse_transform(
        own_waves, offsets, 0, block, *neighbours(spectra, 1), noise, even, odd, None
    )
    later += [exchanged(copied(at, [token])) for at in range(2, len(bounds))]
    for (start, _), received in zip(bounds[1:], later):
        outs = finish_transform(own_waves, start, block, received, noise, even, odd, outs)
    return tuple(outs)


def solution(mesh):
    in_specs = (
        P("member", None, "lat", None),
        P("member", None, "lat", None),
        P(),
        P(),
        P("lat", "member", None, None, None),
    )
    out_specs = (P("lat", "member", None, None, None), P("lat", "member", None, None, None))
    return jax.shard_map(
        per_device, mesh=mesh, in_specs=in_specs, out_specs=out_specs, check_vma=False
    )
```

```python
import functools
import math

import jax
import jax.numpy as jnp
from jax import lax
from jax.experimental import pallas as pl
from jax.experimental.pallas import tpu as pltpu
from jax.sharding import PartitionSpec as P

SPREAD = 2
VMEM_BYTES = 24 * 1024 * 1024
ZONAL_BYTES = 44 * 1024 * 1024
LANES = 128
SUBLANES = 8
TOKEN = (8, 128)


def in_hbm(*arrays):
    return [pltpu.with_memory_space_constraint(array, pltpu.HBM) for array in arrays]


def in_vmem(*arrays):
    return [pltpu.with_memory_space_constraint(array, pltpu.VMEM) for array in arrays]


def meridional_factors(truncation, latitudes, starts, width):
    degree = jnp.arange(truncation, dtype=jnp.int32)

    def angles(points):
        phase = degree[:, None] * points[None, :] % (4 * latitudes)
        return phase.astype(jnp.float32) * (math.pi / (2 * latitudes))

    coarse = angles(2 * starts)
    fine = angles(2 * jnp.arange(width, dtype=jnp.int32) + 1)
    factor = math.sqrt(2.0 / latitudes)
    return jnp.cos(coarse) * factor, jnp.sin(coarse) * factor, jnp.cos(fine), jnp.sin(fine)


def tables_kernel(cos_c, sin_c, cos_f, sin_f, even, odd):
    width = cos_f.shape[1]
    cos_b, sin_b = cos_f[...], sin_f[...]
    for at in range(cos_c.shape[1]):
        cos_a, sin_a = cos_c[:, at : at + 1], sin_c[:, at : at + 1]
        columns = slice(at * width, (at + 1) * width)
        even[:, columns] = (cos_a * cos_b - sin_a * sin_b).astype(even.dtype)
        odd[:, columns] = (sin_a * cos_b + cos_a * sin_b).astype(odd.dtype)


def meridional_tables(truncation, latitudes, starts, width):
    factors = meridional_factors(truncation, latitudes, starts, width)
    shape = pltpu.VMEM((truncation, starts.shape[0] * width), jnp.bfloat16)
    return pl.pallas_call(
        tables_kernel,
        out_shape=[shape, shape],
        compiler_params=pltpu.CompilerParams(vmem_limit_bytes=VMEM_BYTES),
        cost_estimate=pl.CostEstimate(
            flops=6 * truncation * latitudes, bytes_accessed=4 * truncation * latitudes,
            transcendentals=0,
        ),
        name="tables",
    )(*factors)


def zonal_kernel(truncation, tokens, waves, velocity, tracer, *rest):
    out, table, total, turned, velocity_here, tracer_here, sems, out_sems = rest[tokens:]
    members, fields, lat_local, longitudes = velocity.shape
    rows = waves.shape[0]
    groups = velocity_here.shape[0]
    step_fields = velocity_here.shape[1]
    steps = fields // step_fields

    def copies(step):
        part = (step // steps, pl.ds(step % steps * step_fields, step_fields))
        return [
            pltpu.make_async_copy(source.at[part], target.at[step], sems.at[step, at])
            for at, (source, target) in enumerate(
                ((velocity, velocity_here), (tracer, tracer_here))
            )
        ]

    for step in range(groups):
        for copy in copies(step):
            copy.start()

    wave = waves[...]
    weight = jnp.where(wave < truncation, 1.0 / math.sqrt(longitudes), 0.0)

    def angles(count, stride):
        points = lax.broadcasted_iota(jnp.int32, (rows, count), 1) * stride
        phase = lax.rem(wave * points, jnp.full((), longitudes, jnp.int32))
        return phase.astype(jnp.float32) * (2.0 * math.pi / longitudes)

    coarse, fine = angles(longitudes // LANES, LANES), angles(LANES, 1)
    cos_c, sin_c = jnp.cos(coarse) * weight, jnp.sin(coarse) * weight
    cos_f, sin_f = jnp.cos(fine), jnp.sin(fine)
    for at in range(longitudes // LANES):
        cos_a, sin_a = cos_c[:, at : at + 1], sin_c[:, at : at + 1]
        columns = slice(at * LANES, (at + 1) * LANES)
        table[:rows, columns] = (cos_a * cos_f - sin_a * sin_f).astype(table.dtype)
        table[rows:, columns] = (-sin_a * cos_f - cos_a * sin_f).astype(table.dtype)

    def body(step, carry):
        for copy in copies(step):
            copy.wait()
        product = velocity_here[step].astype(jnp.float32) * tracer_here[step].astype(jnp.float32)
        product = product.astype(jnp.bfloat16).reshape(step_fields * lat_local, longitudes)
        sums = lax.dot_general(
            table[...], product, (((1,), (1,)), ((), ())), preferred_element_type=jnp.float32
        )
        first = step // steps * 2 * fields + step % steps * step_fields
        for part in range(2):
            for field in range(step_fields):
                block = sums[
                    part * rows : (part + 1) * rows, field * lat_local : (field + 1) * lat_local
                ]
                total[:, first + part * fields + field] = block.reshape(
                    rows // SUBLANES, SUBLANES, lat_local
                )
        return carry

    lax.fori_loop(0, groups, body, 0)

    tiles = rows // SUBLANES
    batch = math.gcd(tiles, 4)

    def leave(at):
        part = pl.ds(pl.multiple_of(at * batch * SUBLANES, SUBLANES), batch * SUBLANES)
        return pltpu.make_async_copy(turned.at[part], out.at[part], out_sems.at[at])

    def turn(at, carry):
        for tile in range(batch):
            first = pl.multiple_of((at * batch + tile) * SUBLANES, SUBLANES)
            tiles_here = jnp.swapaxes(total[at * batch + tile], 0, 1)
            turned[pl.ds(first, SUBLANES)] = tiles_here.astype(out.dtype)
        leave(at).start()
        return carry

    def end(at, carry):
        leave(at).wait()
        return carry

    lax.fori_loop(0, tiles // batch, turn, 0)
    lax.fori_loop(0, tiles // batch, end, 0)


def zonal_transform(waves, truncation, velocity, tracer, tokens):
    mem_local, fields, lat_local, longitudes = velocity.shape
    rows = waves.shape[0]
    fields_step = min(fields, max(1, 512 // lat_local))
    groups = mem_local * (fields // fields_step)
    out_rows = mem_local * 2 * fields
    grid_part = pltpu.VMEM((groups, fields_step, lat_local, longitudes), velocity.dtype)
    flops = 2 * 2 * rows * longitudes * mem_local * fields * lat_local
    moved = 2 * velocity.size * 2 + rows * out_rows * lat_local * 2
    return pl.pallas_call(
        functools.partial(zonal_kernel, truncation, len(tokens)),
        in_specs=[pl.BlockSpec(memory_space=pltpu.VMEM)]
        + [pl.BlockSpec(memory_space=pl.ANY)] * (2 + len(tokens)),
        out_specs=pl.BlockSpec(memory_space=pl.ANY),
        out_shape=pltpu.HBM((rows, out_rows, lat_local), jnp.bfloat16),
        scratch_shapes=[
            pltpu.VMEM((2 * rows, longitudes), jnp.bfloat16),
            pltpu.VMEM((rows // SUBLANES, out_rows, SUBLANES, lat_local), jnp.float32),
            pltpu.VMEM((rows, out_rows, lat_local), jnp.bfloat16),
            grid_part,
            grid_part,
            pltpu.SemaphoreType.DMA((groups, 2)),
            pltpu.SemaphoreType.DMA((rows // SUBLANES,)),
        ],
        compiler_params=pltpu.CompilerParams(vmem_limit_bytes=ZONAL_BYTES),
        cost_estimate=pl.CostEstimate(flops=flops, bytes_accessed=moved, transcendentals=0),
        name="zonal",
    )(waves, *in_hbm(velocity, tracer), *tokens)


def forward_kernel(first, block, waves, received, even, odd, *rest):
    out, token = rest[-2:]
    truncation = even.shape[0]
    step = pl.program_id(0)
    per_slot = received.shape[1] // block
    rows = jnp.concatenate([received[g] for g in range(received.shape[0])], axis=-1)
    contract = (((1,), (1,)), ((), ()))
    by_even = lax.dot_general(rows, even[...], contract, preferred_element_type=jnp.float32)
    by_odd = lax.dot_general(rows, odd[...], contract, preferred_element_type=jnp.float32)
    degree = lax.broadcasted_iota(jnp.int32, (per_slot, truncation), 1)
    for slot in range(block):
        wave = waves[first + step * block + slot]
        least = jnp.where(wave < truncation, wave, truncation)
        here = slice(slot * per_slot, (slot + 1) * per_slot)
        chosen = jnp.where(wave % 2 == 1, by_odd[here], by_even[here])
        chosen = jnp.where(degree >= least, chosen, 0.0)
        out[slot] = chosen.astype(out.dtype).reshape(out.shape[1:])
    token[...] = jnp.zeros_like(token)


def forward_transform(waves, first, block, received, even, odd, mem_local, tokens):
    groups, all_rows, lat_local = received.shape
    truncation, latitudes = even.shape
    slots = all_rows // (waves[1] * mem_local)
    out_shape = (slots, mem_local, waves[1], truncation)
    per_block = block * mem_local * waves[1]
    table = pl.BlockSpec(even.shape, lambda step, w: (0, 0))
    return pl.pallas_call(
        functools.partial(forward_kernel, first, block),
        grid_spec=pltpu.PrefetchScalarGridSpec(
            num_scalar_prefetch=1,
            grid=(slots // block,),
            in_specs=[
                pl.BlockSpec((groups, per_block, lat_local), lambda step, w: (0, step, 0)),
                table,
                table,
            ]
            + [pl.BlockSpec(memory_space=pl.ANY)] * len(tokens),
            out_specs=[
                pl.BlockSpec((block,) + out_shape[1:], lambda step, w: (step, 0, 0, 0)),
                pl.BlockSpec(TOKEN, lambda step, w: (0, 0)),
            ],
        ),
        out_shape=[
            pltpu.HBM(out_shape, jnp.bfloat16),
            jax.ShapeDtypeStruct(TOKEN, jnp.float32),
        ],
        compiler_params=pltpu.CompilerParams(vmem_limit_bytes=VMEM_BYTES),
        cost_estimate=pl.CostEstimate(
            flops=4 * all_rows * truncation * latitudes,
            bytes_accessed=2 * (all_rows * latitudes + 2 * even.size + all_rows * truncation),
            transcendentals=0,
        ),
        name="forward",
    )(waves[0], *in_hbm(received), *in_vmem(even, odd), *tokens)


def inverse_kernel(first, block, waves, offsets, low, own, high, noise, even, odd, *rest):
    spectra_out, fourier_out, token = rest[-3:]
    token[...] = jnp.zeros_like(token)
    truncation, latitudes = even.shape
    step = pl.program_id(0)
    mem_local, parts, fields = noise.shape[1:4]
    degree = lax.broadcasted_iota(jnp.int32, (fields, truncation), 1)
    sources = [low[:, m] for m in range(low.shape[1])]
    sources += [own[:, m] for m in range(own.shape[1])]
    sources += [high[:, m] for m in range(high.shape[1])]
    even_rows, odd_rows = [], []
    parents = []
    for child in range(mem_local):
        parent = sources[0]
        for at in range(1, len(sources)):
            parent = jnp.where(offsets[child] == at, sources[at], parent)
        parents.append(parent)
    for slot in range(block):
        wave = waves[first + step * block + slot]
        least = jnp.where(wave < truncation, wave, truncation)
        is_odd = wave % 2 == 1
        active = degree >= least
        for child in range(mem_local):
            parent = parents[child][slot].astype(jnp.float32)
            parent = parent.reshape(parts, fields, truncation)
            added = jnp.where(active[None], noise[slot, child].astype(jnp.float32), 0.0)
            total = parent + added
            spectra_out[slot, child] = total.astype(spectra_out.dtype)
            rows = total.reshape(parts * fields, truncation)
            even_rows.append(jnp.where(is_odd, 0.0, rows).astype(jnp.bfloat16))
            odd_rows.append(jnp.where(is_odd, rows, 0.0).astype(jnp.bfloat16))
    result = jnp.dot(
        jnp.concatenate(even_rows, axis=0), even[...], preferred_element_type=jnp.float32
    )
    result += jnp.dot(
        jnp.concatenate(odd_rows, axis=0), odd[...], preferred_element_type=jnp.float32
    )
    fourier_out[...] = result.reshape(fourier_out.shape).astype(fourier_out.dtype)


def inverse_transform(waves, offsets, first, block, low, own, high, noise, even, odd, outs):
    slots_all, mem_local, parts, fields, truncation = noise.shape
    latitudes = even.shape[1]
    slots = own.shape[0]
    at = first // block
    near = lambda step, w, o: (step, 0, 0, 0)
    far = lambda step, w, o: (at + step, 0, 0, 0, 0)
    table = pl.BlockSpec(even.shape, lambda step, w, o: (0, 0))
    noise_block = pl.BlockSpec((block,) + noise.shape[1:], far)
    fourier_shape = noise.shape[:4] + (latitudes,)
    fourier_block = pl.BlockSpec((block,) + fourier_shape[1:], far)
    operands = [low, *in_hbm(own), high, *in_hbm(noise), *in_vmem(even, odd)]
    in_specs = [pl.BlockSpec((block,) + a.shape[1:], near) for a in operands[:3]]
    in_specs += [noise_block, table, table]
    aliases = {}
    if outs is not None:
        aliases = {8: 0, 9: 1}
        operands += in_hbm(*outs)
        in_specs += [pl.BlockSpec(memory_space=pl.ANY)] * 2
    rows = slots * mem_local * parts * fields
    return pl.pallas_call(
        functools.partial(inverse_kernel, first, block),
        grid_spec=pltpu.PrefetchScalarGridSpec(
            num_scalar_prefetch=2,
            grid=(slots // block,),
            in_specs=in_specs,
            out_specs=[
                noise_block,
                fourier_block,
                pl.BlockSpec(TOKEN, lambda step, w, o: (0, 0)),
            ],
        ),
        out_shape=[
            jax.ShapeDtypeStruct(noise.shape, jnp.bfloat16),
            jax.ShapeDtypeStruct(fourier_shape, jnp.bfloat16),
            jax.ShapeDtypeStruct(TOKEN, jnp.float32),
        ],
        input_output_aliases=aliases,
        compiler_params=pltpu.CompilerParams(vmem_limit_bytes=VMEM_BYTES),
        cost_estimate=pl.CostEstimate(
            flops=4 * rows * truncation * latitudes,
            bytes_accessed=2 * rows * (5 * truncation + latitudes) + 4 * even.size,
            transcendentals=0,
        ),
        name="inverse",
    )(waves, offsets, *operands)


def copy_kernel(offsets, low, own, high, *rest):
    out = rest[-1]
    rows = out.shape[1] // offsets.shape[0]
    for child in range(offsets.shape[0]):
        index, chosen = 0, None
        for source in (low, own, high):
            for at in range(source.shape[1] // rows):
                value = source[:, at * rows : (at + 1) * rows]
                chosen = value if index == 0 else jnp.where(offsets[child] == index, value, chosen)
                index += 1
        out[:, child * rows : (child + 1) * rows] = chosen


def copy_parents(offsets, low, own, high, tokens):
    steps = math.gcd(own.shape[0], 4)
    block = lambda array: pl.BlockSpec(
        (array.shape[0] // steps,) + array.shape[1:], lambda step, o: (step, 0, 0)
    )
    return pl.pallas_call(
        copy_kernel,
        grid_spec=pltpu.PrefetchScalarGridSpec(
            num_scalar_prefetch=1,
            grid=(steps,),
            in_specs=[block(low), block(own), block(high)]
            + [pl.BlockSpec(memory_space=pl.ANY)] * len(tokens),
            out_specs=block(own),
        ),
        out_shape=pltpu.HBM(own.shape, own.dtype),
        compiler_params=pltpu.CompilerParams(vmem_limit_bytes=VMEM_BYTES),
        cost_estimate=pl.CostEstimate(flops=0, bytes_accessed=8 * own.size, transcendentals=0),
        name="parents",
    )(offsets, low, *in_hbm(own), high, *tokens)


def finish_kernel(first, block, waves, received, noise, even, odd, *rest):
    spectra_out, fourier_out = rest[-2:]
    truncation = even.shape[0]
    mem_local, parts, fields = noise.shape[1:4]
    step = pl.program_id(0)
    per_slot = received.shape[1] // block
    rows = jnp.concatenate([received[g] for g in range(received.shape[0])], axis=-1)
    contract = (((1,), (1,)), ((), ()))
    by_even = lax.dot_general(rows, even[...], contract, preferred_element_type=jnp.float32)
    by_odd = lax.dot_general(rows, odd[...], contract, preferred_element_type=jnp.float32)
    degree = lax.broadcasted_iota(jnp.int32, (per_slot, truncation), 1)
    even_rows, odd_rows = [], []
    for slot in range(block):
        wave = waves[first + step * block + slot]
        least = jnp.where(wave < truncation, wave, truncation)
        is_odd = wave % 2 == 1
        active = degree >= least
        here = slice(slot * per_slot, (slot + 1) * per_slot)
        spectra = jnp.where(is_odd, by_odd[here], by_even[here])
        spectra = spectra.astype(jnp.bfloat16).astype(jnp.float32)
        added = noise[slot].astype(jnp.float32).reshape(per_slot, truncation)
        child = jnp.where(active, spectra + added, 0.0)
        spectra_out[slot] = child.reshape(noise.shape[1:]).astype(spectra_out.dtype)
        even_rows.append(jnp.where(is_odd, 0.0, child).astype(jnp.bfloat16))
        odd_rows.append(jnp.where(is_odd, child, 0.0).astype(jnp.bfloat16))
    result = jnp.dot(
        jnp.concatenate(even_rows, axis=0), even[...], preferred_element_type=jnp.float32
    )
    result += jnp.dot(
        jnp.concatenate(odd_rows, axis=0), odd[...], preferred_element_type=jnp.float32
    )
    fourier_out[...] = result.reshape(fourier_out.shape).astype(fourier_out.dtype)


def finish_transform(waves, first, block, received, noise, even, odd, outs):
    slots_all, mem_local, parts, fields, truncation = noise.shape
    latitudes = even.shape[1]
    groups, all_rows, lat_local = received.shape
    per_slot = mem_local * parts * fields
    at = first // block
    far = lambda step, w: (at + step, 0, 0, 0, 0)
    table = pl.BlockSpec(even.shape, lambda step, w: (0, 0))
    noise_block = pl.BlockSpec((block,) + noise.shape[1:], far)
    fourier_shape = noise.shape[:4] + (latitudes,)
    fourier_block = pl.BlockSpec((block,) + fourier_shape[1:], far)
    received_block = pl.BlockSpec(
        (groups, block * per_slot, lat_local), lambda step, w: (0, step, 0)
    )
    return pl.pallas_call(
        functools.partial(finish_kernel, first, block),
        grid_spec=pltpu.PrefetchScalarGridSpec(
            num_scalar_prefetch=1,
            grid=(all_rows // (block * per_slot),),
            in_specs=[received_block, noise_block, table, table]
            + [pl.BlockSpec(memory_space=pl.ANY)] * 2,
            out_specs=[noise_block, fourier_block],
        ),
        out_shape=[
            jax.ShapeDtypeStruct(noise.shape, jnp.bfloat16),
            jax.ShapeDtypeStruct(fourier_shape, jnp.bfloat16),
        ],
        input_output_aliases={5: 0, 6: 1},
        compiler_params=pltpu.CompilerParams(vmem_limit_bytes=VMEM_BYTES),
        cost_estimate=pl.CostEstimate(
            flops=8 * all_rows * truncation * latitudes,
            bytes_accessed=2 * all_rows * (2 * truncation + 2 * latitudes) + 4 * even.size,
            transcendentals=0,
        ),
        name="finish",
    )(waves, *in_hbm(received, noise), *in_vmem(even, odd), *in_hbm(*outs))


def chunk_bounds(slots_here, block):
    blocks = slots_here // block
    edges = [0, (blocks * 5 + 10) // 11, (blocks * 10 + 10) // 11, blocks]
    edges = [edge * block for edge in edges]
    return [(start, stop) for start, stop in zip(edges[:-1], edges[1:]) if stop > start]


def per_device(velocity, tracer, wave_slots, parents, noise):
    lat_count = lax.axis_size("lat")
    lat_index = lax.axis_index("lat")
    mem_count = lax.axis_size("member")
    group_index = lax.axis_index("member")
    mem_local, fields, lat_local, longitudes = velocity.shape
    slots_here, truncation = noise.shape[0], noise.shape[-1]
    block = math.gcd(slots_here, 8)
    per_member = 2 * fields
    per_slot = mem_local * per_member
    latitudes = lat_count * lat_local
    own_waves = lax.dynamic_slice_in_dim(wave_slots, lat_index * slots_here, slots_here)
    first_member = group_index * mem_local
    own_parents = lax.dynamic_slice_in_dim(parents, first_member, mem_local)
    offsets = own_parents - first_member + SPREAD
    upward = [(i, i + 1) for i in range(mem_count - 1)]
    downward = [(target, source) for source, target in upward]
    slot_grid = wave_slots.reshape(lat_count, slots_here)
    bounds = chunk_bounds(slots_here, block)
    inner = min(lat_local, LANES)
    starts = jnp.arange(latitudes // inner, dtype=jnp.int32) * inner

    def zonal(at):
        start, stop = bounds[at]
        waves = slot_grid[:, start:stop].reshape(-1, 1)
        return zonal_transform(waves, truncation, velocity, tracer, [])

    def neighbours(rows, per_member):
        low = lax.ppermute(rows[:, rows.shape[1] - SPREAD * per_member :], "member", upward)
        high = lax.ppermute(rows[:, : SPREAD * per_member], "member", downward)
        return low, rows, high

    def exchanged(outgoing):
        outgoing = outgoing.reshape(lat_count, -1, lat_local)
        moved = lax.all_to_all(outgoing, "lat", split_axis=0, concat_axis=0, tiled=True)
        if lat_local % LANES != 0:
            moved = jnp.swapaxes(moved, 0, 1).reshape(1, -1, latitudes)
        return moved

    def copied(at, tokens):
        return copy_parents(offsets, *neighbours(zonal(at), per_member), tokens)

    received = exchanged(zonal(0))
    even, odd = meridional_tables(truncation, latitudes, starts, inner)
    later = [exchanged(copied(1, []))] if len(bounds) > 1 else []
    spectra, _ = forward_transform(
        (own_waves, per_member), 0, block, received, even, odd, mem_local, []
    )
    *outs, token = inverse_transform(
        own_waves, offsets, 0, block, *neighbours(spectra, 1), noise, even, odd, None
    )
    later += [exchanged(copied(at, [token])) for at in range(2, len(bounds))]
    for (start, _), received in zip(bounds[1:], later):
        outs = finish_transform(own_waves, start, block, received, noise, even, odd, outs)
    return tuple(outs)


def solution(mesh):
    in_specs = (
        P("member", None, "lat", None),
        P("member", None, "lat", None),
        P(),
        P(),
        P("lat", "member", None, None, None),
    )
    out_specs = (P("lat", "member", None, None, None), P("lat", "member", None, None, None))
    return jax.shard_map(
        per_device, mesh=mesh, in_specs=in_specs, out_specs=out_specs, check_vma=False
    )
```

```python
import functools
import math

import jax
import jax.numpy as jnp
from jax import lax
from jax.experimental import pallas as pl
from jax.experimental.pallas import tpu as pltpu
from jax.sharding import PartitionSpec as P

SPREAD = 2
VMEM_BYTES = 24 * 1024 * 1024
ZONAL_BYTES = 44 * 1024 * 1024
LANES = 128
SUBLANES = 8
TOKEN = (8, 128)


def in_hbm(*arrays):
    return [pltpu.with_memory_space_constraint(array, pltpu.HBM) for array in arrays]


def in_vmem(*arrays):
    return [pltpu.with_memory_space_constraint(array, pltpu.VMEM) for array in arrays]


def meridional_factors(truncation, latitudes, starts, width):
    degree = jnp.arange(truncation, dtype=jnp.int32)

    def angles(points):
        phase = degree[:, None] * points[None, :] % (4 * latitudes)
        return phase.astype(jnp.float32) * (math.pi / (2 * latitudes))

    coarse = angles(2 * starts)
    fine = angles(2 * jnp.arange(width, dtype=jnp.int32) + 1)
    factor = math.sqrt(2.0 / latitudes)
    return jnp.cos(coarse) * factor, jnp.sin(coarse) * factor, jnp.cos(fine), jnp.sin(fine)


def tables_kernel(cos_c, sin_c, cos_f, sin_f, even, odd):
    width = cos_f.shape[1]
    cos_b, sin_b = cos_f[...], sin_f[...]
    for at in range(cos_c.shape[1]):
        cos_a, sin_a = cos_c[:, at : at + 1], sin_c[:, at : at + 1]
        columns = slice(at * width, (at + 1) * width)
        even[:, columns] = (cos_a * cos_b - sin_a * sin_b).astype(even.dtype)
        odd[:, columns] = (sin_a * cos_b + cos_a * sin_b).astype(odd.dtype)


def meridional_tables(truncation, latitudes, starts, width):
    factors = meridional_factors(truncation, latitudes, starts, width)
    shape = pltpu.VMEM((truncation, starts.shape[0] * width), jnp.bfloat16)
    return pl.pallas_call(
        tables_kernel,
        out_shape=[shape, shape],
        compiler_params=pltpu.CompilerParams(vmem_limit_bytes=VMEM_BYTES),
        cost_estimate=pl.CostEstimate(
            flops=6 * truncation * latitudes, bytes_accessed=4 * truncation * latitudes,
            transcendentals=0,
        ),
        name="tables",
    )(*factors)


def zonal_kernel(truncation, tokens, waves, velocity, tracer, *rest):
    out, table, total, turned, velocity_here, tracer_here, sems, out_sems = rest[tokens:]
    members, fields, lat_local, longitudes = velocity.shape
    rows = waves.shape[0]
    groups = velocity_here.shape[0]
    step_fields = velocity_here.shape[1]
    steps = fields // step_fields

    def copies(step):
        part = (step // steps, pl.ds(step % steps * step_fields, step_fields))
        return [
            pltpu.make_async_copy(source.at[part], target.at[step], sems.at[step, at])
            for at, (source, target) in enumerate(
                ((velocity, velocity_here), (tracer, tracer_here))
            )
        ]

    for step in range(groups):
        for copy in copies(step):
            copy.start()

    wave = waves[...]
    weight = jnp.where(wave < truncation, 1.0 / math.sqrt(longitudes), 0.0)

    def angles(count, stride):
        points = lax.broadcasted_iota(jnp.int32, (rows, count), 1) * stride
        phase = lax.rem(wave * points, jnp.full((), longitudes, jnp.int32))
        return phase.astype(jnp.float32) * (2.0 * math.pi / longitudes)

    coarse, fine = angles(longitudes // LANES, LANES), angles(LANES, 1)
    cos_c, sin_c = jnp.cos(coarse) * weight, jnp.sin(coarse) * weight
    cos_f, sin_f = jnp.cos(fine), jnp.sin(fine)
    for at in range(longitudes // LANES):
        cos_a, sin_a = cos_c[:, at : at + 1], sin_c[:, at : at + 1]
        columns = slice(at * LANES, (at + 1) * LANES)
        table[:rows, columns] = (cos_a * cos_f - sin_a * sin_f).astype(table.dtype)
        table[rows:, columns] = (-sin_a * cos_f - cos_a * sin_f).astype(table.dtype)

    def body(step, carry):
        for copy in copies(step):
            copy.wait()
        product = velocity_here[step].astype(jnp.float32) * tracer_here[step].astype(jnp.float32)
        product = product.astype(jnp.bfloat16).reshape(step_fields * lat_local, longitudes)
        sums = lax.dot_general(
            table[...], product, (((1,), (1,)), ((), ())), preferred_element_type=jnp.float32
        )
        first = step // steps * 2 * fields + step % steps * step_fields
        for part in range(2):
            for field in range(step_fields):
                block = sums[
                    part * rows : (part + 1) * rows, field * lat_local : (field + 1) * lat_local
                ]
                total[:, first + part * fields + field] = block.reshape(
                    rows // SUBLANES, SUBLANES, lat_local
                )
        return carry

    lax.fori_loop(0, groups, body, 0)

    tiles = rows // SUBLANES
    batch = math.gcd(tiles, 4)

    def leave(at):
        part = pl.ds(pl.multiple_of(at * batch * SUBLANES, SUBLANES), batch * SUBLANES)
        return pltpu.make_async_copy(turned.at[part], out.at[part], out_sems.at[at])

    def turn(at, carry):
        for tile in range(batch):
            first = pl.multiple_of((at * batch + tile) * SUBLANES, SUBLANES)
            tiles_here = jnp.swapaxes(total[at * batch + tile], 0, 1)
            turned[pl.ds(first, SUBLANES)] = tiles_here.astype(out.dtype)
        leave(at).start()
        return carry

    def end(at, carry):
        leave(at).wait()
        return carry

    lax.fori_loop(0, tiles // batch, turn, 0)
    lax.fori_loop(0, tiles // batch, end, 0)


def zonal_transform(waves, truncation, velocity, tracer, tokens):
    mem_local, fields, lat_local, longitudes = velocity.shape
    rows = waves.shape[0]
    fields_step = min(fields, max(1, 512 // lat_local))
    groups = mem_local * (fields // fields_step)
    out_rows = mem_local * 2 * fields
    grid_part = pltpu.VMEM((groups, fields_step, lat_local, longitudes), velocity.dtype)
    flops = 2 * 2 * rows * longitudes * mem_local * fields * lat_local
    moved = 2 * velocity.size * 2 + rows * out_rows * lat_local * 2
    return pl.pallas_call(
        functools.partial(zonal_kernel, truncation, len(tokens)),
        in_specs=[pl.BlockSpec(memory_space=pltpu.VMEM)]
        + [pl.BlockSpec(memory_space=pl.ANY)] * (2 + len(tokens)),
        out_specs=pl.BlockSpec(memory_space=pl.ANY),
        out_shape=pltpu.HBM((rows, out_rows, lat_local), jnp.bfloat16),
        scratch_shapes=[
            pltpu.VMEM((2 * rows, longitudes), jnp.bfloat16),
            pltpu.VMEM((rows // SUBLANES, out_rows, SUBLANES, lat_local), jnp.float32),
            pltpu.VMEM((rows, out_rows, lat_local), jnp.bfloat16),
            grid_part,
            grid_part,
            pltpu.SemaphoreType.DMA((groups, 2)),
            pltpu.SemaphoreType.DMA((rows // SUBLANES,)),
        ],
        compiler_params=pltpu.CompilerParams(vmem_limit_bytes=ZONAL_BYTES),
        cost_estimate=pl.CostEstimate(flops=flops, bytes_accessed=moved, transcendentals=0),
        name="zonal",
    )(waves, *in_hbm(velocity, tracer), *tokens)


def forward_kernel(first, block, waves, received, even, odd, *rest):
    out, token = rest[-2:]
    truncation = even.shape[0]
    step = pl.program_id(0)
    per_slot = received.shape[1] // block
    rows = jnp.concatenate([received[g] for g in range(received.shape[0])], axis=-1)
    contract = (((1,), (1,)), ((), ()))
    by_even = lax.dot_general(rows, even[...], contract, preferred_element_type=jnp.float32)
    by_odd = lax.dot_general(rows, odd[...], contract, preferred_element_type=jnp.float32)
    degree = lax.broadcasted_iota(jnp.int32, (per_slot, truncation), 1)
    for slot in range(block):
        wave = waves[first + step * block + slot]
        least = jnp.where(wave < truncation, wave, truncation)
        here = slice(slot * per_slot, (slot + 1) * per_slot)
        chosen = jnp.where(wave % 2 == 1, by_odd[here], by_even[here])
        chosen = jnp.where(degree >= least, chosen, 0.0)
        out[slot] = chosen.astype(out.dtype).reshape(out.shape[1:])
    token[...] = jnp.zeros_like(token)


def forward_transform(waves, first, block, received, even, odd, mem_local, tokens):
    groups, all_rows, lat_local = received.shape
    truncation, latitudes = even.shape
    slots = all_rows // (waves[1] * mem_local)
    out_shape = (slots, mem_local, waves[1], truncation)
    per_block = block * mem_local * waves[1]
    table = pl.BlockSpec(even.shape, lambda step, w: (0, 0))
    return pl.pallas_call(
        functools.partial(forward_kernel, first, block),
        grid_spec=pltpu.PrefetchScalarGridSpec(
            num_scalar_prefetch=1,
            grid=(slots // block,),
            in_specs=[
                pl.BlockSpec((groups, per_block, lat_local), lambda step, w: (0, step, 0)),
                table,
                table,
            ]
            + [pl.BlockSpec(memory_space=pl.ANY)] * len(tokens),
            out_specs=[
                pl.BlockSpec((block,) + out_shape[1:], lambda step, w: (step, 0, 0, 0)),
                pl.BlockSpec(TOKEN, lambda step, w: (0, 0)),
            ],
        ),
        out_shape=[
            pltpu.HBM(out_shape, jnp.bfloat16),
            jax.ShapeDtypeStruct(TOKEN, jnp.float32),
        ],
        compiler_params=pltpu.CompilerParams(vmem_limit_bytes=VMEM_BYTES),
        cost_estimate=pl.CostEstimate(
            flops=4 * all_rows * truncation * latitudes,
            bytes_accessed=2 * (all_rows * latitudes + 2 * even.size + all_rows * truncation),
            transcendentals=0,
        ),
        name="forward",
    )(waves[0], *in_hbm(received), *in_vmem(even, odd), *tokens)


def inverse_kernel(first, block, waves, offsets, low, own, high, noise, even, odd, *rest):
    spectra_out, fourier_out, token = rest[-3:]
    token[...] = jnp.zeros_like(token)
    truncation, latitudes = even.shape
    step = pl.program_id(0)
    mem_local, parts, fields = noise.shape[1:4]
    degree = lax.broadcasted_iota(jnp.int32, (fields, truncation), 1)
    sources = [low[:, m] for m in range(low.shape[1])]
    sources += [own[:, m] for m in range(own.shape[1])]
    sources += [high[:, m] for m in range(high.shape[1])]
    even_rows, odd_rows = [], []
    parents = []
    for child in range(mem_local):
        parent = sources[0]
        for at in range(1, len(sources)):
            parent = jnp.where(offsets[child] == at, sources[at], parent)
        parents.append(parent)
    for slot in range(block):
        wave = waves[first + step * block + slot]
        least = jnp.where(wave < truncation, wave, truncation)
        is_odd = wave % 2 == 1
        active = degree >= least
        for child in range(mem_local):
            parent = parents[child][slot].astype(jnp.float32)
            parent = parent.reshape(parts, fields, truncation)
            added = jnp.where(active[None], noise[slot, child].astype(jnp.float32), 0.0)
            total = parent + added
            spectra_out[slot, child] = total.astype(spectra_out.dtype)
            rows = total.reshape(parts * fields, truncation)
            even_rows.append(jnp.where(is_odd, 0.0, rows).astype(jnp.bfloat16))
            odd_rows.append(jnp.where(is_odd, rows, 0.0).astype(jnp.bfloat16))
    result = jnp.dot(
        jnp.concatenate(even_rows, axis=0), even[...], preferred_element_type=jnp.float32
    )
    result += jnp.dot(
        jnp.concatenate(odd_rows, axis=0), odd[...], preferred_element_type=jnp.float32
    )
    fourier_out[...] = result.reshape(fourier_out.shape).astype(fourier_out.dtype)


def inverse_transform(waves, offsets, first, block, low, own, high, noise, even, odd, outs):
    slots_all, mem_local, parts, fields, truncation = noise.shape
    latitudes = even.shape[1]
    slots = own.shape[0]
    at = first // block
    near = lambda step, w, o: (step, 0, 0, 0)
    far = lambda step, w, o: (at + step, 0, 0, 0, 0)
    table = pl.BlockSpec(even.shape, lambda step, w, o: (0, 0))
    noise_block = pl.BlockSpec((block,) + noise.shape[1:], far)
    fourier_shape = noise.shape[:4] + (latitudes,)
    fourier_block = pl.BlockSpec((block,) + fourier_shape[1:], far)
    operands = [low, *in_hbm(own), high, *in_hbm(noise), *in_vmem(even, odd)]
    in_specs = [pl.BlockSpec((block,) + a.shape[1:], near) for a in operands[:3]]
    in_specs += [noise_block, table, table]
    aliases = {}
    if outs is not None:
        aliases = {8: 0, 9: 1}
        operands += in_hbm(*outs)
        in_specs += [pl.BlockSpec(memory_space=pl.ANY)] * 2
    rows = slots * mem_local * parts * fields
    return pl.pallas_call(
        functools.partial(inverse_kernel, first, block),
        grid_spec=pltpu.PrefetchScalarGridSpec(
            num_scalar_prefetch=2,
            grid=(slots // block,),
            in_specs=in_specs,
            out_specs=[
                noise_block,
                fourier_block,
                pl.BlockSpec(TOKEN, lambda step, w, o: (0, 0)),
            ],
        ),
        out_shape=[
            jax.ShapeDtypeStruct(noise.shape, jnp.bfloat16),
            jax.ShapeDtypeStruct(fourier_shape, jnp.bfloat16),
            jax.ShapeDtypeStruct(TOKEN, jnp.float32),
        ],
        input_output_aliases=aliases,
        compiler_params=pltpu.CompilerParams(vmem_limit_bytes=VMEM_BYTES),
        cost_estimate=pl.CostEstimate(
            flops=4 * rows * truncation * latitudes,
            bytes_accessed=2 * rows * (5 * truncation + latitudes) + 4 * even.size,
            transcendentals=0,
        ),
        name="inverse",
    )(waves, offsets, *operands)


def copy_kernel(offsets, low, own, high, *rest):
    out = rest[-1]
    rows = out.shape[1] // offsets.shape[0]
    for child in range(offsets.shape[0]):
        index, chosen = 0, None
        for source in (low, own, high):
            for at in range(source.shape[1] // rows):
                value = source[:, at * rows : (at + 1) * rows]
                chosen = value if index == 0 else jnp.where(offsets[child] == index, value, chosen)
                index += 1
        out[:, child * rows : (child + 1) * rows] = chosen


def copy_parents(offsets, low, own, high, tokens):
    steps = math.gcd(own.shape[0], 4)
    block = lambda array: pl.BlockSpec(
        (array.shape[0] // steps,) + array.shape[1:], lambda step, o: (step, 0, 0)
    )
    return pl.pallas_call(
        copy_kernel,
        grid_spec=pltpu.PrefetchScalarGridSpec(
            num_scalar_prefetch=1,
            grid=(steps,),
            in_specs=[block(low), block(own), block(high)]
            + [pl.BlockSpec(memory_space=pl.ANY)] * len(tokens),
            out_specs=block(own),
        ),
        out_shape=pltpu.HBM(own.shape, own.dtype),
        compiler_params=pltpu.CompilerParams(vmem_limit_bytes=VMEM_BYTES),
        cost_estimate=pl.CostEstimate(flops=0, bytes_accessed=8 * own.size, transcendentals=0),
        name="parents",
    )(offsets, low, *in_hbm(own), high, *tokens)


def finish_block(first, waves, received, noise, even, odd, spectra_out, fourier_out, ready, store):
    truncation = even.shape[0]
    block, mem_local, parts, fields = noise.shape[:4]
    per_slot = received.shape[1] // block
    rows = jnp.concatenate([received[g] for g in range(received.shape[0])], axis=-1)
    contract = (((1,), (1,)), ((), ()))
    by_even = lax.dot_general(rows, even[...], contract, preferred_element_type=jnp.float32)
    by_odd = lax.dot_general(rows, odd[...], contract, preferred_element_type=jnp.float32)
    degree = lax.broadcasted_iota(jnp.int32, (per_slot, truncation), 1)
    even_rows, odd_rows = [], []
    ready()
    for slot in range(block):
        wave = waves[first + slot]
        least = jnp.where(wave < truncation, wave, truncation)
        is_odd = wave % 2 == 1
        active = degree >= least
        here = slice(slot * per_slot, (slot + 1) * per_slot)
        spectra = jnp.where(is_odd, by_odd[here], by_even[here])
        spectra = spectra.astype(jnp.bfloat16).astype(jnp.float32)
        added = noise[slot].astype(jnp.float32).reshape(per_slot, truncation)
        child = jnp.where(active, spectra + added, 0.0)
        spectra_out[slot] = child.reshape(noise.shape[1:]).astype(spectra_out.dtype)
        even_rows.append(jnp.where(is_odd, 0.0, child).astype(jnp.bfloat16))
        odd_rows.append(jnp.where(is_odd, child, 0.0).astype(jnp.bfloat16))
    store()
    result = jnp.dot(
        jnp.concatenate(even_rows, axis=0), even[...], preferred_element_type=jnp.float32
    )
    result += jnp.dot(
        jnp.concatenate(odd_rows, axis=0), odd[...], preferred_element_type=jnp.float32
    )
    fourier_out[...] = result.reshape(fourier_out.shape).astype(fourier_out.dtype)


def finish_kernel(first, block, waves, received, noise, even, odd, *rest):
    start = first + pl.program_id(0) * block
    nothing = lambda: None
    finish_block(start, waves, received, noise, even, odd, *rest[-2:], nothing, nothing)


def last_kernel(first, waves, received, noise, even, odd, *rest):
    spectra_out, fourier_out, noise_here, spectra_here, fourier_here, sems = rest[-6:]
    part = pl.ds(first, noise_here.shape[0])
    fetch = pltpu.make_async_copy(noise.at[part], noise_here, sems.at[0])
    leave = pltpu.make_async_copy(spectra_here, spectra_out.at[part], sems.at[1])
    leave_too = pltpu.make_async_copy(fourier_here, fourier_out.at[part], sems.at[2])
    fetch.start()
    finish_block(
        first,
        waves,
        received,
        noise_here,
        even,
        odd,
        spectra_here,
        fourier_here,
        fetch.wait,
        leave.start,
    )
    leave_too.start()
    leave.wait()
    leave_too.wait()


def last_transform(waves, first, received, noise, even, odd, outs):
    slots_all, mem_local, parts, fields, truncation = noise.shape
    latitudes = even.shape[1]
    all_rows = received.shape[1]
    block = all_rows // (mem_local * parts * fields)
    fourier_shape = noise.shape[:4] + (latitudes,)
    here = pl.BlockSpec(memory_space=pltpu.VMEM)
    anywhere = pl.BlockSpec(memory_space=pl.ANY)
    return pl.pallas_call(
        functools.partial(last_kernel, first),
        in_specs=[pl.BlockSpec(memory_space=pltpu.SMEM), here, anywhere, here, here]
        + [anywhere] * 2,
        out_specs=[anywhere, anywhere],
        out_shape=[
            jax.ShapeDtypeStruct(noise.shape, jnp.bfloat16),
            jax.ShapeDtypeStruct(fourier_shape, jnp.bfloat16),
        ],
        scratch_shapes=[
            pltpu.VMEM((block,) + noise.shape[1:], jnp.bfloat16),
            pltpu.VMEM((block,) + noise.shape[1:], jnp.bfloat16),
            pltpu.VMEM((block,) + fourier_shape[1:], jnp.bfloat16),
            pltpu.SemaphoreType.DMA((3,)),
        ],
        input_output_aliases={5: 0, 6: 1},
        compiler_params=pltpu.CompilerParams(vmem_limit_bytes=VMEM_BYTES),
        cost_estimate=pl.CostEstimate(
            flops=8 * all_rows * truncation * latitudes,
            bytes_accessed=2 * all_rows * (2 * truncation + 2 * latitudes) + 4 * even.size,
            transcendentals=0,
        ),
        name="last",
    )(waves, received, *in_hbm(noise), *in_vmem(even, odd), *in_hbm(*outs))


def finish_transform(waves, first, block, received, noise, even, odd, outs):
    slots_all, mem_local, parts, fields, truncation = noise.shape
    latitudes = even.shape[1]
    groups, all_rows, lat_local = received.shape
    per_slot = mem_local * parts * fields
    at = first // block
    far = lambda step, w: (at + step, 0, 0, 0, 0)
    table = pl.BlockSpec(even.shape, lambda step, w: (0, 0))
    noise_block = pl.BlockSpec((block,) + noise.shape[1:], far)
    fourier_shape = noise.shape[:4] + (latitudes,)
    fourier_block = pl.BlockSpec((block,) + fourier_shape[1:], far)
    received_block = pl.BlockSpec(
        (groups, block * per_slot, lat_local), lambda step, w: (0, step, 0)
    )
    return pl.pallas_call(
        functools.partial(finish_kernel, first, block),
        grid_spec=pltpu.PrefetchScalarGridSpec(
            num_scalar_prefetch=1,
            grid=(all_rows // (block * per_slot),),
            in_specs=[received_block, noise_block, table, table]
            + [pl.BlockSpec(memory_space=pl.ANY)] * 2,
            out_specs=[noise_block, fourier_block],
        ),
        out_shape=[
            jax.ShapeDtypeStruct(noise.shape, jnp.bfloat16),
            jax.ShapeDtypeStruct(fourier_shape, jnp.bfloat16),
        ],
        input_output_aliases={5: 0, 6: 1},
        compiler_params=pltpu.CompilerParams(vmem_limit_bytes=VMEM_BYTES),
        cost_estimate=pl.CostEstimate(
            flops=8 * all_rows * truncation * latitudes,
            bytes_accessed=2 * all_rows * (2 * truncation + 2 * latitudes) + 4 * even.size,
            transcendentals=0,
        ),
        name="finish",
    )(waves, *in_hbm(received, noise), *in_vmem(even, odd), *in_hbm(*outs))


def chunk_bounds(slots_here, block):
    blocks = slots_here // block
    edges = [0, (blocks * 5 + 10) // 11, (blocks * 10 + 10) // 11, blocks]
    edges = [edge * block for edge in edges]
    return [(start, stop) for start, stop in zip(edges[:-1], edges[1:]) if stop > start]


def per_device(velocity, tracer, wave_slots, parents, noise):
    lat_count = lax.axis_size("lat")
    lat_index = lax.axis_index("lat")
    mem_count = lax.axis_size("member")
    group_index = lax.axis_index("member")
    mem_local, fields, lat_local, longitudes = velocity.shape
    slots_here, truncation = noise.shape[0], noise.shape[-1]
    block = math.gcd(slots_here, 8)
    per_member = 2 * fields
    per_slot = mem_local * per_member
    latitudes = lat_count * lat_local
    own_waves = lax.dynamic_slice_in_dim(wave_slots, lat_index * slots_here, slots_here)
    first_member = group_index * mem_local
    own_parents = lax.dynamic_slice_in_dim(parents, first_member, mem_local)
    offsets = own_parents - first_member + SPREAD
    upward = [(i, i + 1) for i in range(mem_count - 1)]
    downward = [(target, source) for source, target in upward]
    slot_grid = wave_slots.reshape(lat_count, slots_here)
    bounds = chunk_bounds(slots_here, block)
    inner = min(lat_local, LANES)
    starts = jnp.arange(latitudes // inner, dtype=jnp.int32) * inner

    def zonal(at):
        start, stop = bounds[at]
        waves = slot_grid[:, start:stop].reshape(-1, 1)
        return zonal_transform(waves, truncation, velocity, tracer, [])

    def neighbours(rows, per_member):
        low = lax.ppermute(rows[:, rows.shape[1] - SPREAD * per_member :], "member", upward)
        high = lax.ppermute(rows[:, : SPREAD * per_member], "member", downward)
        return low, rows, high

    def exchanged(outgoing):
        outgoing = outgoing.reshape(lat_count, -1, lat_local)
        moved = lax.all_to_all(outgoing, "lat", split_axis=0, concat_axis=0, tiled=True)
        if lat_local % LANES != 0:
            moved = jnp.swapaxes(moved, 0, 1).reshape(1, -1, latitudes)
        return moved

    def copied(at, tokens):
        return copy_parents(offsets, *neighbours(zonal(at), per_member), tokens)

    received = exchanged(zonal(0))
    even, odd = meridional_tables(truncation, latitudes, starts, inner)
    later = [exchanged(copied(1, []))] if len(bounds) > 1 else []
    spectra, _ = forward_transform(
        (own_waves, per_member), 0, block, received, even, odd, mem_local, []
    )
    *outs, token = inverse_transform(
        own_waves, offsets, 0, block, *neighbours(spectra, 1), noise, even, odd, None
    )
    later += [exchanged(copied(at, [token])) for at in range(2, len(bounds))]
    for (start, stop), received in zip(bounds[1:], later):
        if stop - start == block:
            outs = last_transform(own_waves, start, received, noise, even, odd, outs)
        else:
            outs = finish_transform(own_waves, start, block, received, noise, even, odd, outs)
    return tuple(outs)


def solution(mesh):
    in_specs = (
        P("member", None, "lat", None),
        P("member", None, "lat", None),
        P(),
        P(),
        P("lat", "member", None, None, None),
    )
    out_specs = (P("lat", "member", None, None, None), P("lat", "member", None, None, None))
    return jax.shard_map(
        per_device, mesh=mesh, in_specs=in_specs, out_specs=out_specs, check_vma=False
    )
```

```python
import functools
import math

import jax
import jax.numpy as jnp
from jax import lax
from jax.experimental import pallas as pl
from jax.experimental.pallas import tpu as pltpu
from jax.sharding import PartitionSpec as P

SPREAD = 2
VMEM_BYTES = 24 * 1024 * 1024
ZONAL_BYTES = 44 * 1024 * 1024
LANES = 128
SUBLANES = 8
TOKEN = (8, 128)


def in_hbm(*arrays):
    return [pltpu.with_memory_space_constraint(array, pltpu.HBM) for array in arrays]


def in_vmem(*arrays):
    return [pltpu.with_memory_space_constraint(array, pltpu.VMEM) for array in arrays]


def meridional_factors(truncation, latitudes, starts, width):
    degree = jnp.arange(truncation, dtype=jnp.int32)

    def angles(points):
        phase = degree[:, None] * points[None, :] % (4 * latitudes)
        return phase.astype(jnp.float32) * (math.pi / (2 * latitudes))

    coarse = angles(2 * starts)
    fine = angles(2 * jnp.arange(width, dtype=jnp.int32) + 1)
    factor = math.sqrt(2.0 / latitudes)
    return jnp.cos(coarse) * factor, jnp.sin(coarse) * factor, jnp.cos(fine), jnp.sin(fine)


def tables_kernel(cos_c, sin_c, cos_f, sin_f, even, odd):
    width = cos_f.shape[1]
    cos_b, sin_b = cos_f[...], sin_f[...]
    for at in range(cos_c.shape[1]):
        cos_a, sin_a = cos_c[:, at : at + 1], sin_c[:, at : at + 1]
        columns = slice(at * width, (at + 1) * width)
        even[:, columns] = (cos_a * cos_b - sin_a * sin_b).astype(even.dtype)
        odd[:, columns] = (sin_a * cos_b + cos_a * sin_b).astype(odd.dtype)


def meridional_tables(truncation, latitudes, starts, width):
    factors = meridional_factors(truncation, latitudes, starts, width)
    shape = pltpu.VMEM((truncation, starts.shape[0] * width), jnp.bfloat16)
    return pl.pallas_call(
        tables_kernel,
        out_shape=[shape, shape],
        compiler_params=pltpu.CompilerParams(vmem_limit_bytes=VMEM_BYTES),
        cost_estimate=pl.CostEstimate(
            flops=6 * truncation * latitudes, bytes_accessed=4 * truncation * latitudes,
            transcendentals=0,
        ),
        name="tables",
    )(*factors)


def zonal_kernel(truncation, tokens, waves, velocity, tracer, *rest):
    out, table, total, turned, velocity_here, tracer_here, sems, out_sems = rest[tokens:]
    members, fields, lat_local, longitudes = velocity.shape
    rows = waves.shape[0]
    groups = velocity_here.shape[0]
    step_fields = velocity_here.shape[1]
    steps = fields // step_fields

    def copies(step):
        part = (step // steps, pl.ds(step % steps * step_fields, step_fields))
        return [
            pltpu.make_async_copy(source.at[part], target.at[step], sems.at[step, at])
            for at, (source, target) in enumerate(
                ((velocity, velocity_here), (tracer, tracer_here))
            )
        ]

    for step in range(groups):
        for copy in copies(step):
            copy.start()

    wave = waves[...]
    weight = jnp.where(wave < truncation, 1.0 / math.sqrt(longitudes), 0.0)

    def cos_sin(count, stride):
        points = lax.broadcasted_iota(jnp.int32, (rows, count), 1) * stride
        phase = lax.rem(wave * points, jnp.full((), longitudes, jnp.int32))
        quarter = longitudes // 4
        turns = lax.div(phase + quarter // 2, jnp.full((), quarter, jnp.int32))
        angle = (phase - turns * quarter).astype(jnp.float32) * (2.0 * math.pi / longitudes)
        square = angle * angle
        cos, sin = 1.0 / 40320, -1.0 / 5040
        for power in (6, 4, 2, 0):
            sign = -1.0 if power % 4 else 1.0
            cos = cos * square + sign / math.factorial(power)
        for power in (5, 3, 1):
            sign = -1.0 if power % 4 == 3 else 1.0
            sin = sin * square + sign / math.factorial(power)
        sin = sin * angle
        swap = turns % 2 == 1
        cos, sin = jnp.where(swap, sin, cos), jnp.where(swap, cos, sin)
        cos = jnp.where((turns == 1) | (turns == 2), -cos, cos)
        sin = jnp.where((turns == 2) | (turns == 3), -sin, sin)
        return cos, sin

    (cos_c, sin_c), (cos_f, sin_f) = cos_sin(longitudes // LANES, LANES), cos_sin(LANES, 1)
    cos_c, sin_c = cos_c * weight, sin_c * weight
    for at in range(longitudes // LANES):
        cos_a, sin_a = cos_c[:, at : at + 1], sin_c[:, at : at + 1]
        columns = slice(at * LANES, (at + 1) * LANES)
        table[:rows, columns] = (cos_a * cos_f - sin_a * sin_f).astype(table.dtype)
        table[rows:, columns] = (-sin_a * cos_f - cos_a * sin_f).astype(table.dtype)

    def body(step, carry):
        for copy in copies(step):
            copy.wait()
        product = velocity_here[step].astype(jnp.float32) * tracer_here[step].astype(jnp.float32)
        product = product.astype(jnp.bfloat16).reshape(step_fields * lat_local, longitudes)
        sums = lax.dot_general(
            table[...], product, (((1,), (1,)), ((), ())), preferred_element_type=jnp.float32
        )
        first = step // steps * 2 * fields + step % steps * step_fields
        for part in range(2):
            for field in range(step_fields):
                block = sums[
                    part * rows : (part + 1) * rows, field * lat_local : (field + 1) * lat_local
                ]
                total[:, first + part * fields + field] = block.reshape(
                    rows // SUBLANES, SUBLANES, lat_local
                )
        return carry

    lax.fori_loop(0, groups, body, 0)

    tiles = rows // SUBLANES
    batch = math.gcd(tiles, 4)

    def leave(at):
        part = pl.ds(pl.multiple_of(at * batch * SUBLANES, SUBLANES), batch * SUBLANES)
        return pltpu.make_async_copy(turned.at[part], out.at[part], out_sems.at[at])

    def turn(at, carry):
        for tile in range(batch):
            first = pl.multiple_of((at * batch + tile) * SUBLANES, SUBLANES)
            tiles_here = jnp.swapaxes(total[at * batch + tile], 0, 1)
            turned[pl.ds(first, SUBLANES)] = tiles_here.astype(out.dtype)
        leave(at).start()
        return carry

    def end(at, carry):
        leave(at).wait()
        return carry

    lax.fori_loop(0, tiles // batch, turn, 0)
    lax.fori_loop(0, tiles // batch, end, 0)


def zonal_transform(waves, truncation, velocity, tracer, tokens):
    mem_local, fields, lat_local, longitudes = velocity.shape
    rows = waves.shape[0]
    fields_step = min(fields, max(1, 512 // lat_local))
    groups = mem_local * (fields // fields_step)
    out_rows = mem_local * 2 * fields
    grid_part = pltpu.VMEM((groups, fields_step, lat_local, longitudes), velocity.dtype)
    flops = 2 * 2 * rows * longitudes * mem_local * fields * lat_local
    moved = 2 * velocity.size * 2 + rows * out_rows * lat_local * 2
    return pl.pallas_call(
        functools.partial(zonal_kernel, truncation, len(tokens)),
        in_specs=[pl.BlockSpec(memory_space=pltpu.VMEM)]
        + [pl.BlockSpec(memory_space=pl.ANY)] * (2 + len(tokens)),
        out_specs=pl.BlockSpec(memory_space=pl.ANY),
        out_shape=pltpu.HBM((rows, out_rows, lat_local), jnp.bfloat16),
        scratch_shapes=[
            pltpu.VMEM((2 * rows, longitudes), jnp.bfloat16),
            pltpu.VMEM((rows // SUBLANES, out_rows, SUBLANES, lat_local), jnp.float32),
            pltpu.VMEM((rows, out_rows, lat_local), jnp.bfloat16),
            grid_part,
            grid_part,
            pltpu.SemaphoreType.DMA((groups, 2)),
            pltpu.SemaphoreType.DMA((rows // SUBLANES,)),
        ],
        compiler_params=pltpu.CompilerParams(vmem_limit_bytes=ZONAL_BYTES),
        cost_estimate=pl.CostEstimate(flops=flops, bytes_accessed=moved, transcendentals=0),
        name="zonal",
    )(waves, *in_hbm(velocity, tracer), *tokens)


def forward_kernel(first, block, waves, received, even, odd, *rest):
    out, token = rest[-2:]
    truncation = even.shape[0]
    step = pl.program_id(0)
    per_slot = received.shape[1] // block
    rows = jnp.concatenate([received[g] for g in range(received.shape[0])], axis=-1)
    contract = (((1,), (1,)), ((), ()))
    by_even = lax.dot_general(rows, even[...], contract, preferred_element_type=jnp.float32)
    by_odd = lax.dot_general(rows, odd[...], contract, preferred_element_type=jnp.float32)
    degree = lax.broadcasted_iota(jnp.int32, (per_slot, truncation), 1)
    for slot in range(block):
        wave = waves[first + step * block + slot]
        least = jnp.where(wave < truncation, wave, truncation)
        here = slice(slot * per_slot, (slot + 1) * per_slot)
        chosen = jnp.where(wave % 2 == 1, by_odd[here], by_even[here])
        chosen = jnp.where(degree >= least, chosen, 0.0)
        out[slot] = chosen.astype(out.dtype).reshape(out.shape[1:])
    token[...] = jnp.zeros_like(token)


def forward_transform(waves, first, block, received, even, odd, mem_local, tokens):
    groups, all_rows, lat_local = received.shape
    truncation, latitudes = even.shape
    slots = all_rows // (waves[1] * mem_local)
    out_shape = (slots, mem_local, waves[1], truncation)
    per_block = block * mem_local * waves[1]
    table = pl.BlockSpec(even.shape, lambda step, w: (0, 0))
    return pl.pallas_call(
        functools.partial(forward_kernel, first, block),
        grid_spec=pltpu.PrefetchScalarGridSpec(
            num_scalar_prefetch=1,
            grid=(slots // block,),
            in_specs=[
                pl.BlockSpec((groups, per_block, lat_local), lambda step, w: (0, step, 0)),
                table,
                table,
            ]
            + [pl.BlockSpec(memory_space=pl.ANY)] * len(tokens),
            out_specs=[
                pl.BlockSpec((block,) + out_shape[1:], lambda step, w: (step, 0, 0, 0)),
                pl.BlockSpec(TOKEN, lambda step, w: (0, 0)),
            ],
        ),
        out_shape=[
            pltpu.HBM(out_shape, jnp.bfloat16),
            jax.ShapeDtypeStruct(TOKEN, jnp.float32),
        ],
        compiler_params=pltpu.CompilerParams(vmem_limit_bytes=VMEM_BYTES),
        cost_estimate=pl.CostEstimate(
            flops=4 * all_rows * truncation * latitudes,
            bytes_accessed=2 * (all_rows * latitudes + 2 * even.size + all_rows * truncation),
            transcendentals=0,
        ),
        name="forward",
    )(waves[0], *in_hbm(received), *in_vmem(even, odd), *tokens)


def inverse_kernel(first, block, waves, offsets, low, own, high, noise, even, odd, *rest):
    spectra_out, fourier_out, token = rest[-3:]
    token[...] = jnp.zeros_like(token)
    truncation, latitudes = even.shape
    step = pl.program_id(0)
    mem_local, parts, fields = noise.shape[1:4]
    degree = lax.broadcasted_iota(jnp.int32, (fields, truncation), 1)
    sources = [low[:, m] for m in range(low.shape[1])]
    sources += [own[:, m] for m in range(own.shape[1])]
    sources += [high[:, m] for m in range(high.shape[1])]
    even_rows, odd_rows = [], []
    parents = []
    for child in range(mem_local):
        parent = sources[0]
        for at in range(1, len(sources)):
            parent = jnp.where(offsets[child] == at, sources[at], parent)
        parents.append(parent)
    for slot in range(block):
        wave = waves[first + step * block + slot]
        least = jnp.where(wave < truncation, wave, truncation)
        is_odd = wave % 2 == 1
        active = degree >= least
        for child in range(mem_local):
            parent = parents[child][slot].astype(jnp.float32)
            parent = parent.reshape(parts, fields, truncation)
            added = jnp.where(active[None], noise[slot, child].astype(jnp.float32), 0.0)
            total = parent + added
            spectra_out[slot, child] = total.astype(spectra_out.dtype)
            rows = total.reshape(parts * fields, truncation)
            even_rows.append(jnp.where(is_odd, 0.0, rows).astype(jnp.bfloat16))
            odd_rows.append(jnp.where(is_odd, rows, 0.0).astype(jnp.bfloat16))
    result = jnp.dot(
        jnp.concatenate(even_rows, axis=0), even[...], preferred_element_type=jnp.float32
    )
    result += jnp.dot(
        jnp.concatenate(odd_rows, axis=0), odd[...], preferred_element_type=jnp.float32
    )
    fourier_out[...] = result.reshape(fourier_out.shape).astype(fourier_out.dtype)


def inverse_transform(waves, offsets, first, block, low, own, high, noise, even, odd, outs):
    slots_all, mem_local, parts, fields, truncation = noise.shape
    latitudes = even.shape[1]
    slots = own.shape[0]
    at = first // block
    near = lambda step, w, o: (step, 0, 0, 0)
    far = lambda step, w, o: (at + step, 0, 0, 0, 0)
    table = pl.BlockSpec(even.shape, lambda step, w, o: (0, 0))
    noise_block = pl.BlockSpec((block,) + noise.shape[1:], far)
    fourier_shape = noise.shape[:4] + (latitudes,)
    fourier_block = pl.BlockSpec((block,) + fourier_shape[1:], far)
    operands = [low, *in_hbm(own), high, *in_hbm(noise), *in_vmem(even, odd)]
    in_specs = [pl.BlockSpec((block,) + a.shape[1:], near) for a in operands[:3]]
    in_specs += [noise_block, table, table]
    aliases = {}
    if outs is not None:
        aliases = {8: 0, 9: 1}
        operands += in_hbm(*outs)
        in_specs += [pl.BlockSpec(memory_space=pl.ANY)] * 2
    rows = slots * mem_local * parts * fields
    return pl.pallas_call(
        functools.partial(inverse_kernel, first, block),
        grid_spec=pltpu.PrefetchScalarGridSpec(
            num_scalar_prefetch=2,
            grid=(slots // block,),
            in_specs=in_specs,
            out_specs=[
                noise_block,
                fourier_block,
                pl.BlockSpec(TOKEN, lambda step, w, o: (0, 0)),
            ],
        ),
        out_shape=[
            jax.ShapeDtypeStruct(noise.shape, jnp.bfloat16),
            jax.ShapeDtypeStruct(fourier_shape, jnp.bfloat16),
            jax.ShapeDtypeStruct(TOKEN, jnp.float32),
        ],
        input_output_aliases=aliases,
        compiler_params=pltpu.CompilerParams(vmem_limit_bytes=VMEM_BYTES),
        cost_estimate=pl.CostEstimate(
            flops=4 * rows * truncation * latitudes,
            bytes_accessed=2 * rows * (5 * truncation + latitudes) + 4 * even.size,
            transcendentals=0,
        ),
        name="inverse",
    )(waves, offsets, *operands)


def copy_kernel(offsets, low, own, high, *rest):
    out = rest[-1]
    rows = out.shape[1] // offsets.shape[0]
    for child in range(offsets.shape[0]):
        index, chosen = 0, None
        for source in (low, own, high):
            for at in range(source.shape[1] // rows):
                value = source[:, at * rows : (at + 1) * rows]
                chosen = value if index == 0 else jnp.where(offsets[child] == index, value, chosen)
                index += 1
        out[:, child * rows : (child + 1) * rows] = chosen


def copy_parents(offsets, low, own, high, tokens):
    steps = math.gcd(own.shape[0], 4)
    block = lambda array: pl.BlockSpec(
        (array.shape[0] // steps,) + array.shape[1:], lambda step, o: (step, 0, 0)
    )
    return pl.pallas_call(
        copy_kernel,
        grid_spec=pltpu.PrefetchScalarGridSpec(
            num_scalar_prefetch=1,
            grid=(steps,),
            in_specs=[block(low), block(own), block(high)]
            + [pl.BlockSpec(memory_space=pl.ANY)] * len(tokens),
            out_specs=block(own),
        ),
        out_shape=pltpu.HBM(own.shape, own.dtype),
        compiler_params=pltpu.CompilerParams(vmem_limit_bytes=VMEM_BYTES),
        cost_estimate=pl.CostEstimate(flops=0, bytes_accessed=8 * own.size, transcendentals=0),
        name="parents",
    )(offsets, low, *in_hbm(own), high, *tokens)


def last_kernel(first, block, waves, received, noise, even, odd, *rest):
    spectra_out, fourier_out, noise_here, spectra_here, fourier_here, order, sems, out_sems = rest[-8:]
    truncation = even.shape[0]
    slots, mem_local, parts, fields = noise_here.shape[:4]
    per_slot = received.shape[1] // slots
    fetch = pltpu.make_async_copy(noise.at[pl.ds(first, slots)], noise_here, sems.at[0])
    fetch.start()

    def place(slot, evens):
        is_odd = waves[first + slot] % 2
        order[jnp.where(is_odd == 1, slots - 1 - (slot - evens), evens)] = slot
        return evens + 1 - is_odd

    evens = lax.fori_loop(0, slots, place, jnp.int32(0))

    def leave(slot):
        return (
            pltpu.make_async_copy(
                spectra_here.at[slot], spectra_out.at[first + slot], out_sems.at[0, slot]
            ),
            pltpu.make_async_copy(
                fourier_here.at[slot], fourier_out.at[first + slot], out_sems.at[1, slot]
            ),
        )

    def transform(at, tables):
        here = [order[at * block + slot] for slot in range(block)]
        rows = []
        for slot in here:
            part = pl.ds(pl.multiple_of(slot * per_slot, per_slot), per_slot)
            pieces = [received[g, part] for g in range(received.shape[0])]
            rows.append(jnp.concatenate(pieces, axis=-1))
        rows = jnp.concatenate(rows, axis=0)
        contract = (((1,), (1,)), ((), ()))
        results = [
            lax.dot_general(rows, table[...], contract, preferred_element_type=jnp.float32)
            for table in tables
        ]

        @pl.when(at == 0)
        def _():
            fetch.wait()

        degree = lax.broadcasted_iota(jnp.int32, (per_slot, truncation), 1)
        children = [[] for _ in tables]
        for index, slot in enumerate(here):
            wave = waves[first + slot]
            least = jnp.where(wave < truncation, wave, truncation)
            own = slice(index * per_slot, (index + 1) * per_slot)
            spectra = results[0][own]
            if len(tables) == 2:
                spectra = jnp.where(wave % 2 == 1, results[1][own], spectra)
            spectra = spectra.astype(jnp.bfloat16).astype(jnp.float32)
            added = noise_here[slot].astype(jnp.float32).reshape(per_slot, truncation)
            child = jnp.where(degree >= least, spectra + added, 0.0)
            spectra_here[slot] = child.reshape(noise.shape[1:]).astype(spectra_out.dtype)
            for parity, kept in enumerate(children):
                if len(tables) == 2:
                    kept.append(jnp.where(wave % 2 == parity, child, 0.0).astype(jnp.bfloat16))
                else:
                    kept.append(child.astype(jnp.bfloat16))
        result = 0.0
        for kept, table in zip(children, tables):
            result += jnp.dot(
                jnp.concatenate(kept, axis=0), table[...], preferred_element_type=jnp.float32
            )
        for index, slot in enumerate(here):
            own = result[index * per_slot : (index + 1) * per_slot]
            fourier_here[slot] = own.reshape(fourier_here.shape[1:]).astype(fourier_out.dtype)
            for copy in leave(slot):
                copy.start()

    def body(at, carry):
        all_even, all_odd = (at + 1) * block <= evens, at * block >= evens
        pl.when(all_even)(lambda: transform(at, [even]))
        pl.when(all_odd)(lambda: transform(at, [odd]))
        pl.when(jnp.logical_not(all_even | all_odd))(lambda: transform(at, [even, odd]))
        return carry

    def end(slot, carry):
        for copy in leave(slot):
            copy.wait()
        return carry

    lax.fori_loop(0, slots // block, body, 0)
    lax.fori_loop(0, slots, end, 0)


def last_transform(waves, first, block, received, noise, even, odd, outs):
    slots_all, mem_local, parts, fields, truncation = noise.shape
    latitudes = even.shape[1]
    all_rows = received.shape[1]
    slots = all_rows // (mem_local * parts * fields)
    fourier_shape = noise.shape[:4] + (latitudes,)
    here = pl.BlockSpec(memory_space=pltpu.VMEM)
    anywhere = pl.BlockSpec(memory_space=pl.ANY)
    return pl.pallas_call(
        functools.partial(last_kernel, first, block),
        in_specs=[pl.BlockSpec(memory_space=pltpu.SMEM), here, anywhere, here, here]
        + [anywhere] * 2,
        out_specs=[anywhere, anywhere],
        out_shape=[
            jax.ShapeDtypeStruct(noise.shape, jnp.bfloat16),
            jax.ShapeDtypeStruct(fourier_shape, jnp.bfloat16),
        ],
        scratch_shapes=[
            pltpu.VMEM((slots,) + noise.shape[1:], jnp.bfloat16),
            pltpu.VMEM((slots,) + noise.shape[1:], jnp.bfloat16),
            pltpu.VMEM((slots,) + fourier_shape[1:], jnp.bfloat16),
            pltpu.SMEM((slots,), jnp.int32),
            pltpu.SemaphoreType.DMA((1,)),
            pltpu.SemaphoreType.DMA((2, slots)),
        ],
        input_output_aliases={5: 0, 6: 1},
        compiler_params=pltpu.CompilerParams(vmem_limit_bytes=VMEM_BYTES),
        cost_estimate=pl.CostEstimate(
            flops=8 * all_rows * truncation * latitudes,
            bytes_accessed=2 * all_rows * (2 * truncation + 2 * latitudes) + 4 * even.size,
            transcendentals=0,
        ),
        name="last",
    )(waves, received, *in_hbm(noise), *in_vmem(even, odd), *in_hbm(*outs))


def chunk_bounds(slots_here, block):
    blocks = slots_here // block
    edge = (blocks * 6 + 10) // 11 * block
    return [(0, edge)] + ([(edge, slots_here)] if edge < slots_here else [])


def per_device(velocity, tracer, wave_slots, parents, noise):
    lat_count = lax.axis_size("lat")
    lat_index = lax.axis_index("lat")
    mem_count = lax.axis_size("member")
    group_index = lax.axis_index("member")
    mem_local, fields, lat_local, longitudes = velocity.shape
    slots_here, truncation = noise.shape[0], noise.shape[-1]
    block = math.gcd(slots_here, 8)
    per_member = 2 * fields
    per_slot = mem_local * per_member
    latitudes = lat_count * lat_local
    own_waves = lax.dynamic_slice_in_dim(wave_slots, lat_index * slots_here, slots_here)
    first_member = group_index * mem_local
    own_parents = lax.dynamic_slice_in_dim(parents, first_member, mem_local)
    offsets = own_parents - first_member + SPREAD
    upward = [(i, i + 1) for i in range(mem_count - 1)]
    downward = [(target, source) for source, target in upward]
    slot_grid = wave_slots.reshape(lat_count, slots_here)
    bounds = chunk_bounds(slots_here, block)
    inner = min(lat_local, LANES)
    starts = jnp.arange(latitudes // inner, dtype=jnp.int32) * inner

    def zonal(at):
        start, stop = bounds[at]
        waves = slot_grid[:, start:stop].reshape(-1, 1)
        return zonal_transform(waves, truncation, velocity, tracer, [])

    def neighbours(rows, per_member):
        low = lax.ppermute(rows[:, rows.shape[1] - SPREAD * per_member :], "member", upward)
        high = lax.ppermute(rows[:, : SPREAD * per_member], "member", downward)
        return low, rows, high

    def exchanged(outgoing):
        outgoing = outgoing.reshape(lat_count, -1, lat_local)
        moved = lax.all_to_all(outgoing, "lat", split_axis=0, concat_axis=0, tiled=True)
        if lat_local % LANES != 0:
            moved = jnp.swapaxes(moved, 0, 1).reshape(1, -1, latitudes)
        return moved

    received = exchanged(zonal(0))
    even, odd = meridional_tables(truncation, latitudes, starts, inner)
    later = [
        exchanged(copy_parents(offsets, *neighbours(zonal(at), per_member), []))
        for at in range(1, len(bounds))
    ]
    spectra, _ = forward_transform(
        (own_waves, per_member), 0, block, received, even, odd, mem_local, []
    )
    *outs, _ = inverse_transform(
        own_waves, offsets, 0, block, *neighbours(spectra, 1), noise, even, odd, None
    )
    for (start, _), received in zip(bounds[1:], later):
        outs = last_transform(own_waves, start, block, received, noise, even, odd, outs)
    return tuple(outs)


def solution(mesh):
    in_specs = (
        P("member", None, "lat", None),
        P("member", None, "lat", None),
        P(),
        P(),
        P("lat", "member", None, None, None),
    )
    out_specs = (P("lat", "member", None, None, None), P("lat", "member", None, None, None))
    return jax.shard_map(
        per_device, mesh=mesh, in_specs=in_specs, out_specs=out_specs, check_vma=False
    )
```

```python
import functools
import math

import jax
import jax.numpy as jnp
from jax import lax
from jax.experimental import pallas as pl
from jax.experimental.pallas import tpu as pltpu
from jax.sharding import PartitionSpec as P

SPREAD = 2
VMEM_BYTES = 24 * 1024 * 1024
ZONAL_BYTES = 44 * 1024 * 1024
LANES = 128
SUBLANES = 8
TOKEN = (8, 128)


def in_hbm(*arrays):
    return [pltpu.with_memory_space_constraint(array, pltpu.HBM) for array in arrays]


def in_vmem(*arrays):
    return [pltpu.with_memory_space_constraint(array, pltpu.VMEM) for array in arrays]


def meridional_factors(truncation, latitudes, starts, width):
    degree = jnp.arange(truncation, dtype=jnp.int32)

    def angles(points):
        phase = degree[:, None] * points[None, :] % (4 * latitudes)
        return phase.astype(jnp.float32) * (math.pi / (2 * latitudes))

    coarse = angles(2 * starts)
    fine = angles(2 * jnp.arange(width, dtype=jnp.int32) + 1)
    factor = math.sqrt(2.0 / latitudes)
    return jnp.cos(coarse) * factor, jnp.sin(coarse) * factor, jnp.cos(fine), jnp.sin(fine)


def tables_kernel(cos_c, sin_c, cos_f, sin_f, even, odd):
    width = cos_f.shape[1]
    cos_b, sin_b = cos_f[...], sin_f[...]
    for at in range(cos_c.shape[1]):
        cos_a, sin_a = cos_c[:, at : at + 1], sin_c[:, at : at + 1]
        columns = slice(at * width, (at + 1) * width)
        even[:, columns] = (cos_a * cos_b - sin_a * sin_b).astype(even.dtype)
        odd[:, columns] = (sin_a * cos_b + cos_a * sin_b).astype(odd.dtype)


def meridional_tables(truncation, latitudes, starts, width):
    factors = meridional_factors(truncation, latitudes, starts, width)
    shape = pltpu.VMEM((truncation, starts.shape[0] * width), jnp.bfloat16)
    return pl.pallas_call(
        tables_kernel,
        out_shape=[shape, shape],
        compiler_params=pltpu.CompilerParams(vmem_limit_bytes=VMEM_BYTES),
        cost_estimate=pl.CostEstimate(
            flops=6 * truncation * latitudes, bytes_accessed=4 * truncation * latitudes,
            transcendentals=0,
        ),
        name="tables",
    )(*factors)


def zonal_kernel(truncation, tokens, waves, velocity, tracer, *rest):
    outs, rest = rest[tokens:-7], rest[-7:]
    table, total, turned, velocity_here, tracer_here, sems, out_sems = rest
    members, fields, lat_local, longitudes = velocity.shape
    rows = waves.shape[0]
    groups = velocity_here.shape[0]
    step_fields = velocity_here.shape[1]
    steps = fields // step_fields

    def copies(step):
        part = (step // steps, pl.ds(step % steps * step_fields, step_fields))
        return [
            pltpu.make_async_copy(source.at[part], target.at[step], sems.at[step, at])
            for at, (source, target) in enumerate(
                ((velocity, velocity_here), (tracer, tracer_here))
            )
        ]

    for step in range(groups):
        for copy in copies(step):
            copy.start()

    wave = waves[...]
    weight = jnp.where(wave < truncation, 1.0 / math.sqrt(longitudes), 0.0)

    def cos_sin(count, stride):
        points = lax.broadcasted_iota(jnp.int32, (rows, count), 1) * stride
        phase = lax.rem(wave * points, jnp.full((), longitudes, jnp.int32))
        quarter = longitudes // 4
        turns = lax.div(phase + quarter // 2, jnp.full((), quarter, jnp.int32))
        angle = (phase - turns * quarter).astype(jnp.float32) * (2.0 * math.pi / longitudes)
        square = angle * angle
        cos, sin = 1.0 / 40320, -1.0 / 5040
        for power in (6, 4, 2, 0):
            sign = -1.0 if power % 4 else 1.0
            cos = cos * square + sign / math.factorial(power)
        for power in (5, 3, 1):
            sign = -1.0 if power % 4 == 3 else 1.0
            sin = sin * square + sign / math.factorial(power)
        sin = sin * angle
        swap = turns % 2 == 1
        cos, sin = jnp.where(swap, sin, cos), jnp.where(swap, cos, sin)
        cos = jnp.where((turns == 1) | (turns == 2), -cos, cos)
        sin = jnp.where((turns == 2) | (turns == 3), -sin, sin)
        return cos, sin

    (cos_c, sin_c), (cos_f, sin_f) = cos_sin(longitudes // LANES, LANES), cos_sin(LANES, 1)
    cos_c, sin_c = cos_c * weight, sin_c * weight
    for at in range(longitudes // LANES):
        cos_a, sin_a = cos_c[:, at : at + 1], sin_c[:, at : at + 1]
        columns = slice(at * LANES, (at + 1) * LANES)
        table[:rows, columns] = (cos_a * cos_f - sin_a * sin_f).astype(table.dtype)
        table[rows:, columns] = (-sin_a * cos_f - cos_a * sin_f).astype(table.dtype)

    def body(step, carry):
        for copy in copies(step):
            copy.wait()
        product = velocity_here[step].astype(jnp.float32) * tracer_here[step].astype(jnp.float32)
        product = product.astype(jnp.bfloat16).reshape(step_fields * lat_local, longitudes)
        sums = lax.dot_general(
            table[...], product, (((1,), (1,)), ((), ())), preferred_element_type=jnp.float32
        )
        first = step // steps * 2 * fields + step % steps * step_fields
        for part in range(2):
            for field in range(step_fields):
                block = sums[
                    part * rows : (part + 1) * rows, field * lat_local : (field + 1) * lat_local
                ]
                total[:, first + part * fields + field] = block.reshape(
                    rows // SUBLANES, SUBLANES, lat_local
                )
        return carry

    lax.fori_loop(0, groups, body, 0)

    tiles = rows // SUBLANES // len(outs)
    batch = math.gcd(tiles, 4)

    def leave(piece, at):
        size = batch * SUBLANES
        part = pl.ds(pl.multiple_of(at * size, SUBLANES), size)
        source = turned.at[pl.ds(pl.multiple_of((piece * tiles + at * batch) * SUBLANES, SUBLANES), size)]
        return pltpu.make_async_copy(source, outs[piece].at[part], out_sems.at[piece, at])

    for piece in range(len(outs)):

        def turn(at, carry):
            for tile in range(batch):
                index = piece * tiles + at * batch + tile
                first = pl.multiple_of(index * SUBLANES, SUBLANES)
                turned[pl.ds(first, SUBLANES)] = jnp.swapaxes(total[index], 0, 1).astype(turned.dtype)
            leave(piece, at).start()
            return carry

        lax.fori_loop(0, tiles // batch, turn, 0)

    for piece in range(len(outs)):

        def end(at, carry):
            leave(piece, at).wait()
            return carry

        lax.fori_loop(0, tiles // batch, end, 0)


def zonal_transform(waves, truncation, velocity, tracer, pieces, tokens):
    mem_local, fields, lat_local, longitudes = velocity.shape
    rows = waves.shape[0]
    fields_step = min(fields, max(1, 512 // lat_local))
    groups = mem_local * (fields // fields_step)
    out_rows = mem_local * 2 * fields
    grid_part = pltpu.VMEM((groups, fields_step, lat_local, longitudes), velocity.dtype)
    flops = 2 * 2 * rows * longitudes * mem_local * fields * lat_local
    moved = 2 * velocity.size * 2 + rows * out_rows * lat_local * 2
    return pl.pallas_call(
        functools.partial(zonal_kernel, truncation, len(tokens)),
        in_specs=[pl.BlockSpec(memory_space=pltpu.VMEM)]
        + [pl.BlockSpec(memory_space=pl.ANY)] * (2 + len(tokens)),
        out_specs=[pl.BlockSpec(memory_space=pl.ANY)] * pieces,
        out_shape=[pltpu.HBM((rows // pieces, out_rows, lat_local), jnp.bfloat16)] * pieces,
        scratch_shapes=[
            pltpu.VMEM((2 * rows, longitudes), jnp.bfloat16),
            pltpu.VMEM((rows // SUBLANES, out_rows, SUBLANES, lat_local), jnp.float32),
            pltpu.VMEM((rows, out_rows, lat_local), jnp.bfloat16),
            grid_part,
            grid_part,
            pltpu.SemaphoreType.DMA((groups, 2)),
            pltpu.SemaphoreType.DMA((pieces, rows // SUBLANES // pieces)),
        ],
        compiler_params=pltpu.CompilerParams(vmem_limit_bytes=ZONAL_BYTES),
        cost_estimate=pl.CostEstimate(flops=flops, bytes_accessed=moved, transcendentals=0),
        name="zonal",
    )(waves, *in_hbm(velocity, tracer), *tokens)


def forward_kernel(first, block, waves, received, even, odd, *rest):
    out, token = rest[-2:]
    truncation = even.shape[0]
    step = pl.program_id(0)
    per_slot = received.shape[1] // block
    rows = jnp.concatenate([received[g] for g in range(received.shape[0])], axis=-1)
    contract = (((1,), (1,)), ((), ()))
    by_even = lax.dot_general(rows, even[...], contract, preferred_element_type=jnp.float32)
    by_odd = lax.dot_general(rows, odd[...], contract, preferred_element_type=jnp.float32)
    degree = lax.broadcasted_iota(jnp.int32, (per_slot, truncation), 1)
    for slot in range(block):
        wave = waves[first + step * block + slot]
        least = jnp.where(wave < truncation, wave, truncation)
        here = slice(slot * per_slot, (slot + 1) * per_slot)
        chosen = jnp.where(wave % 2 == 1, by_odd[here], by_even[here])
        chosen = jnp.where(degree >= least, chosen, 0.0)
        out[slot] = chosen.astype(out.dtype).reshape(out.shape[1:])
    token[...] = jnp.zeros_like(token)


def forward_transform(waves, first, block, received, even, odd, mem_local, tokens):
    groups, all_rows, lat_local = received.shape
    truncation, latitudes = even.shape
    slots = all_rows // (waves[1] * mem_local)
    out_shape = (slots, mem_local, waves[1], truncation)
    per_block = block * mem_local * waves[1]
    table = pl.BlockSpec(even.shape, lambda step, w: (0, 0))
    return pl.pallas_call(
        functools.partial(forward_kernel, first, block),
        grid_spec=pltpu.PrefetchScalarGridSpec(
            num_scalar_prefetch=1,
            grid=(slots // block,),
            in_specs=[
                pl.BlockSpec((groups, per_block, lat_local), lambda step, w: (0, step, 0)),
                table,
                table,
            ]
            + [pl.BlockSpec(memory_space=pl.ANY)] * len(tokens),
            out_specs=[
                pl.BlockSpec((block,) + out_shape[1:], lambda step, w: (step, 0, 0, 0)),
                pl.BlockSpec(TOKEN, lambda step, w: (0, 0)),
            ],
        ),
        out_shape=[
            pltpu.HBM(out_shape, jnp.bfloat16),
            jax.ShapeDtypeStruct(TOKEN, jnp.float32),
        ],
        compiler_params=pltpu.CompilerParams(vmem_limit_bytes=VMEM_BYTES),
        cost_estimate=pl.CostEstimate(
            flops=4 * all_rows * truncation * latitudes,
            bytes_accessed=2 * (all_rows * latitudes + 2 * even.size + all_rows * truncation),
            transcendentals=0,
        ),
        name="forward",
    )(waves[0], *in_hbm(received), *in_vmem(even, odd), *tokens)


def paired_kernel(first, waves, place, *refs):
    received, (even, odd, out, rows) = refs[:-4], refs[-4:]
    truncation = even.shape[0]
    block = out.shape[0]
    lat_local = received[0].shape[2]
    per_slot = rows.shape[0] // block
    me = place[0]
    for k, piece in enumerate(received):
        columns = pl.ds(pl.multiple_of((me ^ k) * lat_local, LANES), lat_local)
        rows[:, columns] = piece[place[k]] if k > 0 else piece[0]
    contract = (((1,), (1,)), ((), ()))
    lines = rows[...]
    by_even = lax.dot_general(lines, even[...], contract, preferred_element_type=jnp.float32)
    by_odd = lax.dot_general(lines, odd[...], contract, preferred_element_type=jnp.float32)
    degree = lax.broadcasted_iota(jnp.int32, (per_slot, truncation), 1)
    for slot in range(block):
        wave = waves[first + slot]
        least = jnp.where(wave < truncation, wave, truncation)
        here = slice(slot * per_slot, (slot + 1) * per_slot)
        chosen = jnp.where(wave % 2 == 1, by_odd[here], by_even[here])
        chosen = jnp.where(degree >= least, chosen, 0.0)
        out[slot] = chosen.astype(out.dtype).reshape(out.shape[1:])


def paired_transform(waves, first, place, received, even, odd, mem_local, per_member):
    truncation, latitudes = even.shape
    all_rows = received[0].shape[1]
    slots = all_rows // (mem_local * per_member)
    here = pl.BlockSpec(memory_space=pltpu.VMEM)
    scalars = pl.BlockSpec(memory_space=pltpu.SMEM)
    out_shape = (slots, mem_local, per_member, truncation)
    return pl.pallas_call(
        functools.partial(paired_kernel, first),
        in_specs=[scalars, scalars] + [here] * (len(received) + 2),
        out_specs=here,
        out_shape=jax.ShapeDtypeStruct(out_shape, jnp.bfloat16),
        scratch_shapes=[pltpu.VMEM((all_rows, latitudes), jnp.bfloat16)],
        compiler_params=pltpu.CompilerParams(vmem_limit_bytes=VMEM_BYTES),
        cost_estimate=pl.CostEstimate(
            flops=4 * all_rows * truncation * latitudes,
            bytes_accessed=2 * (all_rows * latitudes + 2 * even.size + all_rows * truncation),
            transcendentals=0,
        ),
        name="paired",
    )(waves, place, *received, *in_vmem(even, odd))


def inverse_kernel(first, block, waves, offsets, low, own, high, noise, even, odd, *rest):
    spectra_out, fourier_out, token = rest[-3:]
    token[...] = jnp.zeros_like(token)
    truncation, latitudes = even.shape
    step = pl.program_id(0)
    mem_local, parts, fields = noise.shape[1:4]
    degree = lax.broadcasted_iota(jnp.int32, (fields, truncation), 1)
    sources = [low[:, m] for m in range(low.shape[1])]
    sources += [own[:, m] for m in range(own.shape[1])]
    sources += [high[:, m] for m in range(high.shape[1])]
    even_rows, odd_rows = [], []
    parents = []
    for child in range(mem_local):
        parent = sources[0]
        for at in range(1, len(sources)):
            parent = jnp.where(offsets[child] == at, sources[at], parent)
        parents.append(parent)
    for slot in range(block):
        wave = waves[first + step * block + slot]
        least = jnp.where(wave < truncation, wave, truncation)
        is_odd = wave % 2 == 1
        active = degree >= least
        for child in range(mem_local):
            parent = parents[child][slot].astype(jnp.float32)
            parent = parent.reshape(parts, fields, truncation)
            added = jnp.where(active[None], noise[slot, child].astype(jnp.float32), 0.0)
            total = parent + added
            spectra_out[slot, child] = total.astype(spectra_out.dtype)
            rows = total.reshape(parts * fields, truncation)
            even_rows.append(jnp.where(is_odd, 0.0, rows).astype(jnp.bfloat16))
            odd_rows.append(jnp.where(is_odd, rows, 0.0).astype(jnp.bfloat16))
    result = jnp.dot(
        jnp.concatenate(even_rows, axis=0), even[...], preferred_element_type=jnp.float32
    )
    result += jnp.dot(
        jnp.concatenate(odd_rows, axis=0), odd[...], preferred_element_type=jnp.float32
    )
    fourier_out[...] = result.reshape(fourier_out.shape).astype(fourier_out.dtype)


def inverse_transform(waves, offsets, first, block, low, own, high, noise, even, odd, outs):
    slots_all, mem_local, parts, fields, truncation = noise.shape
    latitudes = even.shape[1]
    slots = own.shape[0]
    at = first // block
    near = lambda step, w, o: (step, 0, 0, 0)
    far = lambda step, w, o: (at + step, 0, 0, 0, 0)
    table = pl.BlockSpec(even.shape, lambda step, w, o: (0, 0))
    noise_block = pl.BlockSpec((block,) + noise.shape[1:], far)
    fourier_shape = noise.shape[:4] + (latitudes,)
    fourier_block = pl.BlockSpec((block,) + fourier_shape[1:], far)
    operands = [low, *in_hbm(own), high, *in_hbm(noise), *in_vmem(even, odd)]
    in_specs = [pl.BlockSpec((block,) + a.shape[1:], near) for a in operands[:3]]
    in_specs += [noise_block, table, table]
    aliases = {}
    if outs is not None:
        aliases = {8: 0, 9: 1}
        operands += in_hbm(*outs)
        in_specs += [pl.BlockSpec(memory_space=pl.ANY)] * 2
    rows = slots * mem_local * parts * fields
    return pl.pallas_call(
        functools.partial(inverse_kernel, first, block),
        grid_spec=pltpu.PrefetchScalarGridSpec(
            num_scalar_prefetch=2,
            grid=(slots // block,),
            in_specs=in_specs,
            out_specs=[
                noise_block,
                fourier_block,
                pl.BlockSpec(TOKEN, lambda step, w, o: (0, 0)),
            ],
        ),
        out_shape=[
            jax.ShapeDtypeStruct(noise.shape, jnp.bfloat16),
            jax.ShapeDtypeStruct(fourier_shape, jnp.bfloat16),
            jax.ShapeDtypeStruct(TOKEN, jnp.float32),
        ],
        input_output_aliases=aliases,
        compiler_params=pltpu.CompilerParams(vmem_limit_bytes=VMEM_BYTES),
        cost_estimate=pl.CostEstimate(
            flops=4 * rows * truncation * latitudes,
            bytes_accessed=2 * rows * (5 * truncation + latitudes) + 4 * even.size,
            transcendentals=0,
        ),
        name="inverse",
    )(waves, offsets, *operands)


def copy_kernel(offsets, low, own, high, *rest):
    out = rest[-1]
    rows = out.shape[1] // offsets.shape[0]
    for child in range(offsets.shape[0]):
        index, chosen = 0, None
        for source in (low, own, high):
            for at in range(source.shape[1] // rows):
                value = source[:, at * rows : (at + 1) * rows]
                chosen = value if index == 0 else jnp.where(offsets[child] == index, value, chosen)
                index += 1
        out[:, child * rows : (child + 1) * rows] = chosen


def copy_parents(offsets, low, own, high, tokens):
    steps = math.gcd(own.shape[0], 4)
    block = lambda array: pl.BlockSpec(
        (array.shape[0] // steps,) + array.shape[1:], lambda step, o: (step, 0, 0)
    )
    return pl.pallas_call(
        copy_kernel,
        grid_spec=pltpu.PrefetchScalarGridSpec(
            num_scalar_prefetch=1,
            grid=(steps,),
            in_specs=[block(low), block(own), block(high)]
            + [pl.BlockSpec(memory_space=pl.ANY)] * len(tokens),
            out_specs=block(own),
        ),
        out_shape=pltpu.HBM(own.shape, own.dtype),
        compiler_params=pltpu.CompilerParams(vmem_limit_bytes=VMEM_BYTES),
        cost_estimate=pl.CostEstimate(flops=0, bytes_accessed=8 * own.size, transcendentals=0),
        name="parents",
    )(offsets, low, *in_hbm(own), high, *tokens)


def finish_block(first, waves, received, noise, even, odd, spectra_out, fourier_out, ready, store):
    truncation = even.shape[0]
    block, mem_local, parts, fields = noise.shape[:4]
    per_slot = received.shape[1] // block
    rows = jnp.concatenate([received[g] for g in range(received.shape[0])], axis=-1)
    contract = (((1,), (1,)), ((), ()))
    by_even = lax.dot_general(rows, even[...], contract, preferred_element_type=jnp.float32)
    by_odd = lax.dot_general(rows, odd[...], contract, preferred_element_type=jnp.float32)
    degree = lax.broadcasted_iota(jnp.int32, (per_slot, truncation), 1)
    even_rows, odd_rows = [], []
    ready()
    for slot in range(block):
        wave = waves[first + slot]
        least = jnp.where(wave < truncation, wave, truncation)
        is_odd = wave % 2 == 1
        active = degree >= least
        here = slice(slot * per_slot, (slot + 1) * per_slot)
        spectra = jnp.where(is_odd, by_odd[here], by_even[here])
        spectra = spectra.astype(jnp.bfloat16).astype(jnp.float32)
        added = noise[slot].astype(jnp.float32).reshape(per_slot, truncation)
        child = jnp.where(active, spectra + added, 0.0)
        spectra_out[slot] = child.reshape(noise.shape[1:]).astype(spectra_out.dtype)
        even_rows.append(jnp.where(is_odd, 0.0, child).astype(jnp.bfloat16))
        odd_rows.append(jnp.where(is_odd, child, 0.0).astype(jnp.bfloat16))
    store()
    result = jnp.dot(
        jnp.concatenate(even_rows, axis=0), even[...], preferred_element_type=jnp.float32
    )
    result += jnp.dot(
        jnp.concatenate(odd_rows, axis=0), odd[...], preferred_element_type=jnp.float32
    )
    fourier_out[...] = result.reshape(fourier_out.shape).astype(fourier_out.dtype)


def finish_kernel(first, block, waves, received, noise, even, odd, *rest):
    start = first + pl.program_id(0) * block
    nothing = lambda: None
    finish_block(start, waves, received, noise, even, odd, *rest[-2:], nothing, nothing)


def finish_transform(waves, first, block, received, noise, even, odd, outs):
    slots_all, mem_local, parts, fields, truncation = noise.shape
    latitudes = even.shape[1]
    groups, all_rows, lat_local = received.shape
    per_slot = mem_local * parts * fields
    at = first // block
    far = lambda step, w: (at + step, 0, 0, 0, 0)
    table = pl.BlockSpec(even.shape, lambda step, w: (0, 0))
    noise_block = pl.BlockSpec((block,) + noise.shape[1:], far)
    fourier_shape = noise.shape[:4] + (latitudes,)
    fourier_block = pl.BlockSpec((block,) + fourier_shape[1:], far)
    received_block = pl.BlockSpec(
        (groups, block * per_slot, lat_local), lambda step, w: (0, step, 0)
    )
    return pl.pallas_call(
        functools.partial(finish_kernel, first, block),
        grid_spec=pltpu.PrefetchScalarGridSpec(
            num_scalar_prefetch=1,
            grid=(all_rows // (block * per_slot),),
            in_specs=[received_block, noise_block, table, table]
            + [pl.BlockSpec(memory_space=pl.ANY)] * 2,
            out_specs=[noise_block, fourier_block],
        ),
        out_shape=[
            jax.ShapeDtypeStruct(noise.shape, jnp.bfloat16),
            jax.ShapeDtypeStruct(fourier_shape, jnp.bfloat16),
        ],
        input_output_aliases={5: 0, 6: 1},
        compiler_params=pltpu.CompilerParams(vmem_limit_bytes=VMEM_BYTES),
        cost_estimate=pl.CostEstimate(
            flops=8 * all_rows * truncation * latitudes,
            bytes_accessed=2 * all_rows * (2 * truncation + 2 * latitudes) + 4 * even.size,
            transcendentals=0,
        ),
        name="finish",
    )(waves, *in_hbm(received, noise), *in_vmem(even, odd), *in_hbm(*outs))


def chunk_bounds(slots_here, block):
    blocks = slots_here // block
    edges = [0, (blocks * 6 + 10) // 11, (blocks * 10 + 10) // 11, blocks]
    edges = [edge * block for edge in edges]
    return [(start, stop) for start, stop in zip(edges[:-1], edges[1:]) if stop > start]


def per_device(velocity, tracer, wave_slots, parents, noise):
    lat_count = lax.axis_size("lat")
    lat_index = lax.axis_index("lat")
    mem_count = lax.axis_size("member")
    group_index = lax.axis_index("member")
    mem_local, fields, lat_local, longitudes = velocity.shape
    slots_here, truncation = noise.shape[0], noise.shape[-1]
    block = math.gcd(slots_here, 8)
    per_member = 2 * fields
    per_slot = mem_local * per_member
    latitudes = lat_count * lat_local
    own_waves = lax.dynamic_slice_in_dim(wave_slots, lat_index * slots_here, slots_here)
    first_member = group_index * mem_local
    own_parents = lax.dynamic_slice_in_dim(parents, first_member, mem_local)
    offsets = own_parents - first_member + SPREAD
    upward = [(i, i + 1) for i in range(mem_count - 1)]
    downward = [(target, source) for source, target in upward]
    slot_grid = wave_slots.reshape(lat_count, slots_here)
    bounds = chunk_bounds(slots_here, block)
    inner = min(lat_local, LANES)
    starts = jnp.arange(latitudes // inner, dtype=jnp.int32) * inner

    def zonal(at, grid, pieces):
        start, stop = bounds[at]
        waves = grid[:, start:stop].reshape(-1, 1)
        return zonal_transform(waves, truncation, velocity, tracer, pieces, [])

    def neighbours(rows, per_member):
        low = lax.ppermute(rows[:, rows.shape[1] - SPREAD * per_member :], "member", upward)
        high = lax.ppermute(rows[:, : SPREAD * per_member], "member", downward)
        return low, rows, high

    def exchanged(outgoing):
        outgoing = outgoing.reshape(lat_count, -1, lat_local)
        moved = lax.all_to_all(outgoing, "lat", split_axis=0, concat_axis=0, tiled=True)
        if lat_local % LANES != 0:
            moved = jnp.swapaxes(moved, 0, 1).reshape(1, -1, latitudes)
        return moved

    def inverse(start, spectra, outs):
        *outs, _ = inverse_transform(
            own_waves, offsets, start, block, *neighbours(spectra, 1), noise, even, odd, outs
        )
        return outs

    received = exchanged(zonal(0, slot_grid, 1)[0])
    even, odd = meridional_tables(truncation, latitudes, starts, inner)
    in_pairs = len(bounds) > 2 and lat_local % LANES == 0 and lat_count & (lat_count - 1) == 0
    tokens = []
    if in_pairs:
        ranks = jnp.arange(lat_count, dtype=jnp.int32)
        pieces = zonal(2, slot_grid[ranks ^ lat_index], lat_count)
        tokens = [pieces[0]]
        highest = jnp.array([1 << max(k.bit_length() - 1, 0) for k in range(lat_count)], jnp.int32)
        place = jnp.where(ranks == 0, lat_index, (lat_index & highest == 0).astype(jnp.int32))
        moved = [pieces[0].reshape(1, -1, lat_local)]
        for k in range(1, lat_count):
            pairs = [[i, i ^ k] for i in range(lat_count) if i < i ^ k]
            piece = pieces[k].reshape(-1, lat_local)
            moved.append(lax.all_gather(piece, "lat", axis_index_groups=pairs))
    second = None
    if len(bounds) > 1:
        outgoing = neighbours(zonal(1, slot_grid, 1)[0], per_member)
        second = exchanged(copy_parents(offsets, *outgoing, tokens))
    spectra, _ = forward_transform(
        (own_waves, per_member), 0, block, received, even, odd, mem_local, []
    )
    outs = inverse(0, spectra, None)
    if len(bounds) > 2:
        start = bounds[2][0]
        if in_pairs:
            spectra = paired_transform(
                own_waves, start, place, moved, even, odd, mem_local, per_member
            )
        else:
            spectra, _ = forward_transform(
                (own_waves, per_member),
                start,
                block,
                exchanged(zonal(2, slot_grid, 1)[0]),
                even,
                odd,
                mem_local,
                [],
            )
        outs = inverse(start, spectra, outs)
    if second is not None:
        outs = finish_transform(own_waves, bounds[1][0], block, second, noise, even, odd, outs)
    return tuple(outs)


def solution(mesh):
    in_specs = (
        P("member", None, "lat", None),
        P("member", None, "lat", None),
        P(),
        P(),
        P("lat", "member", None, None, None),
    )
    out_specs = (P("lat", "member", None, None, None), P("lat", "member", None, None, None))
    return jax.shard_map(
        per_device, mesh=mesh, in_specs=in_specs, out_specs=out_specs, check_vma=False
    )
```

```python
import functools
import math

import jax
import jax.numpy as jnp
from jax import lax
from jax.experimental import pallas as pl
from jax.experimental.pallas import tpu as pltpu
from jax.sharding import PartitionSpec as P

SPREAD = 2
VMEM_BYTES = 24 * 1024 * 1024
ZONAL_BYTES = 44 * 1024 * 1024
LANES = 128
SUBLANES = 8
TOKEN = (8, 128)


def in_hbm(*arrays):
    return [pltpu.with_memory_space_constraint(array, pltpu.HBM) for array in arrays]


def in_vmem(*arrays):
    return [pltpu.with_memory_space_constraint(array, pltpu.VMEM) for array in arrays]


def meridional_factors(truncation, latitudes, starts, width):
    degree = jnp.arange(truncation, dtype=jnp.int32)

    def angles(points):
        phase = degree[:, None] * points[None, :] % (4 * latitudes)
        return phase.astype(jnp.float32) * (math.pi / (2 * latitudes))

    coarse = angles(2 * starts)
    fine = angles(2 * jnp.arange(width, dtype=jnp.int32) + 1)
    factor = math.sqrt(2.0 / latitudes)
    return jnp.cos(coarse) * factor, jnp.sin(coarse) * factor, jnp.cos(fine), jnp.sin(fine)


def tables_kernel(cos_c, sin_c, cos_f, sin_f, even, odd):
    width = cos_f.shape[1]
    cos_b, sin_b = cos_f[...], sin_f[...]
    for at in range(cos_c.shape[1]):
        cos_a, sin_a = cos_c[:, at : at + 1], sin_c[:, at : at + 1]
        columns = slice(at * width, (at + 1) * width)
        even[:, columns] = (cos_a * cos_b - sin_a * sin_b).astype(even.dtype)
        odd[:, columns] = (sin_a * cos_b + cos_a * sin_b).astype(odd.dtype)


def meridional_tables(truncation, latitudes, starts, width):
    factors = meridional_factors(truncation, latitudes, starts, width)
    shape = pltpu.VMEM((truncation, starts.shape[0] * width), jnp.bfloat16)
    return pl.pallas_call(
        tables_kernel,
        out_shape=[shape, shape],
        compiler_params=pltpu.CompilerParams(vmem_limit_bytes=VMEM_BYTES),
        cost_estimate=pl.CostEstimate(
            flops=6 * truncation * latitudes, bytes_accessed=4 * truncation * latitudes,
            transcendentals=0,
        ),
        name="tables",
    )(*factors)


def zonal_kernel(truncation, tokens, waves, velocity, tracer, *rest):
    out, table, total, turned, velocity_here, tracer_here, sems, out_sems = rest[tokens:]
    members, fields, lat_local, longitudes = velocity.shape
    rows = waves.shape[0]
    groups = velocity_here.shape[0]
    step_fields = velocity_here.shape[1]
    steps = fields // step_fields

    def copies(step):
        part = (step // steps, pl.ds(step % steps * step_fields, step_fields))
        return [
            pltpu.make_async_copy(source.at[part], target.at[step], sems.at[step, at])
            for at, (source, target) in enumerate(
                ((velocity, velocity_here), (tracer, tracer_here))
            )
        ]

    for step in range(groups):
        for copy in copies(step):
            copy.start()

    wave = waves[...]
    weight = jnp.where(wave < truncation, 1.0 / math.sqrt(longitudes), 0.0)

    def cos_sin(count, stride):
        points = lax.broadcasted_iota(jnp.int32, (rows, count), 1) * stride
        phase = lax.rem(wave * points, jnp.full((), longitudes, jnp.int32))
        quarter = longitudes // 4
        turns = lax.div(phase + quarter // 2, jnp.full((), quarter, jnp.int32))
        angle = (phase - turns * quarter).astype(jnp.float32) * (2.0 * math.pi / longitudes)
        square = angle * angle
        cos, sin = 1.0 / 40320, -1.0 / 5040
        for power in (6, 4, 2, 0):
            sign = -1.0 if power % 4 else 1.0
            cos = cos * square + sign / math.factorial(power)
        for power in (5, 3, 1):
            sign = -1.0 if power % 4 == 3 else 1.0
            sin = sin * square + sign / math.factorial(power)
        sin = sin * angle
        swap = turns % 2 == 1
        cos, sin = jnp.where(swap, sin, cos), jnp.where(swap, cos, sin)
        cos = jnp.where((turns == 1) | (turns == 2), -cos, cos)
        sin = jnp.where((turns == 2) | (turns == 3), -sin, sin)
        return cos, sin

    (cos_c, sin_c), (cos_f, sin_f) = cos_sin(longitudes // LANES, LANES), cos_sin(LANES, 1)
    cos_c, sin_c = cos_c * weight, sin_c * weight
    for at in range(longitudes // LANES):
        cos_a, sin_a = cos_c[:, at : at + 1], sin_c[:, at : at + 1]
        columns = slice(at * LANES, (at + 1) * LANES)
        table[:rows, columns] = (cos_a * cos_f - sin_a * sin_f).astype(table.dtype)
        table[rows:, columns] = (-sin_a * cos_f - cos_a * sin_f).astype(table.dtype)

    def body(step, carry):
        for copy in copies(step):
            copy.wait()
        product = velocity_here[step].astype(jnp.float32) * tracer_here[step].astype(jnp.float32)
        product = product.astype(jnp.bfloat16).reshape(step_fields * lat_local, longitudes)
        sums = lax.dot_general(
            table[...], product, (((1,), (1,)), ((), ())), preferred_element_type=jnp.float32
        )
        first = step // steps * 2 * fields + step % steps * step_fields
        for part in range(2):
            for field in range(step_fields):
                block = sums[
                    part * rows : (part + 1) * rows, field * lat_local : (field + 1) * lat_local
                ]
                total[:, first + part * fields + field] = block.reshape(
                    rows // SUBLANES, SUBLANES, lat_local
                )
        return carry

    lax.fori_loop(0, groups, body, 0)

    tiles = rows // SUBLANES
    batch = math.gcd(tiles, 4)

    def leave(at):
        part = pl.ds(pl.multiple_of(at * batch * SUBLANES, SUBLANES), batch * SUBLANES)
        return pltpu.make_async_copy(turned.at[part], out.at[part], out_sems.at[at])

    def turn(at, carry):
        for tile in range(batch):
            first = pl.multiple_of((at * batch + tile) * SUBLANES, SUBLANES)
            tiles_here = jnp.swapaxes(total[at * batch + tile], 0, 1)
            turned[pl.ds(first, SUBLANES)] = tiles_here.astype(out.dtype)
        leave(at).start()
        return carry

    def end(at, carry):
        leave(at).wait()
        return carry

    lax.fori_loop(0, tiles // batch, turn, 0)
    lax.fori_loop(0, tiles // batch, end, 0)


def zonal_transform(waves, truncation, velocity, tracer, tokens):
    mem_local, fields, lat_local, longitudes = velocity.shape
    rows = waves.shape[0]
    fields_step = min(fields, max(1, 512 // lat_local))
    groups = mem_local * (fields // fields_step)
    out_rows = mem_local * 2 * fields
    grid_part = pltpu.VMEM((groups, fields_step, lat_local, longitudes), velocity.dtype)
    flops = 2 * 2 * rows * longitudes * mem_local * fields * lat_local
    moved = 2 * velocity.size * 2 + rows * out_rows * lat_local * 2
    return pl.pallas_call(
        functools.partial(zonal_kernel, truncation, len(tokens)),
        in_specs=[pl.BlockSpec(memory_space=pltpu.VMEM)]
        + [pl.BlockSpec(memory_space=pl.ANY)] * (2 + len(tokens)),
        out_specs=pl.BlockSpec(memory_space=pl.ANY),
        out_shape=pltpu.HBM((rows, out_rows, lat_local), jnp.bfloat16),
        scratch_shapes=[
            pltpu.VMEM((2 * rows, longitudes), jnp.bfloat16),
            pltpu.VMEM((rows // SUBLANES, out_rows, SUBLANES, lat_local), jnp.float32),
            pltpu.VMEM((rows, out_rows, lat_local), jnp.bfloat16),
            grid_part,
            grid_part,
            pltpu.SemaphoreType.DMA((groups, 2)),
            pltpu.SemaphoreType.DMA((rows // SUBLANES,)),
        ],
        compiler_params=pltpu.CompilerParams(vmem_limit_bytes=ZONAL_BYTES),
        cost_estimate=pl.CostEstimate(flops=flops, bytes_accessed=moved, transcendentals=0),
        name="zonal",
    )(waves, *in_hbm(velocity, tracer), *tokens)


def forward_kernel(first, block, waves, received, even, odd, *rest):
    out, token = rest[-2:]
    truncation = even.shape[0]
    step = pl.program_id(0)
    per_slot = received.shape[1] // block
    rows = jnp.concatenate([received[g] for g in range(received.shape[0])], axis=-1)
    contract = (((1,), (1,)), ((), ()))
    by_even = lax.dot_general(rows, even[...], contract, preferred_element_type=jnp.float32)
    by_odd = lax.dot_general(rows, odd[...], contract, preferred_element_type=jnp.float32)
    degree = lax.broadcasted_iota(jnp.int32, (per_slot, truncation), 1)
    for slot in range(block):
        wave = waves[first + step * block + slot]
        least = jnp.where(wave < truncation, wave, truncation)
        here = slice(slot * per_slot, (slot + 1) * per_slot)
        chosen = jnp.where(wave % 2 == 1, by_odd[here], by_even[here])
        chosen = jnp.where(degree >= least, chosen, 0.0)
        out[slot] = chosen.astype(out.dtype).reshape(out.shape[1:])
    token[...] = jnp.zeros_like(token)


def forward_transform(waves, first, block, received, even, odd, mem_local, tokens):
    groups, all_rows, lat_local = received.shape
    truncation, latitudes = even.shape
    slots = all_rows // (waves[1] * mem_local)
    out_shape = (slots, mem_local, waves[1], truncation)
    per_block = block * mem_local * waves[1]
    table = pl.BlockSpec(even.shape, lambda step, w: (0, 0))
    return pl.pallas_call(
        functools.partial(forward_kernel, first, block),
        grid_spec=pltpu.PrefetchScalarGridSpec(
            num_scalar_prefetch=1,
            grid=(slots // block,),
            in_specs=[
                pl.BlockSpec((groups, per_block, lat_local), lambda step, w: (0, step, 0)),
                table,
                table,
            ]
            + [pl.BlockSpec(memory_space=pl.ANY)] * len(tokens),
            out_specs=[
                pl.BlockSpec((block,) + out_shape[1:], lambda step, w: (step, 0, 0, 0)),
                pl.BlockSpec(TOKEN, lambda step, w: (0, 0)),
            ],
        ),
        out_shape=[
            pltpu.HBM(out_shape, jnp.bfloat16),
            jax.ShapeDtypeStruct(TOKEN, jnp.float32),
        ],
        compiler_params=pltpu.CompilerParams(vmem_limit_bytes=VMEM_BYTES),
        cost_estimate=pl.CostEstimate(
            flops=4 * all_rows * truncation * latitudes,
            bytes_accessed=2 * (all_rows * latitudes + 2 * even.size + all_rows * truncation),
            transcendentals=0,
        ),
        name="forward",
    )(waves[0], *in_hbm(received), *in_vmem(even, odd), *tokens)


def inverse_kernel(first, block, waves, offsets, low, own, high, noise, even, odd, *rest):
    spectra_out, fourier_out, token = rest[-3:]
    token[...] = jnp.zeros_like(token)
    truncation, latitudes = even.shape
    step = pl.program_id(0)
    mem_local, parts, fields = noise.shape[1:4]
    degree = lax.broadcasted_iota(jnp.int32, (fields, truncation), 1)
    sources = [low[:, m] for m in range(low.shape[1])]
    sources += [own[:, m] for m in range(own.shape[1])]
    sources += [high[:, m] for m in range(high.shape[1])]
    even_rows, odd_rows = [], []
    parents = []
    for child in range(mem_local):
        parent = sources[0]
        for at in range(1, len(sources)):
            parent = jnp.where(offsets[child] == at, sources[at], parent)
        parents.append(parent)
    for slot in range(block):
        wave = waves[first + step * block + slot]
        least = jnp.where(wave < truncation, wave, truncation)
        is_odd = wave % 2 == 1
        active = degree >= least
        for child in range(mem_local):
            parent = parents[child][slot].astype(jnp.float32)
            parent = parent.reshape(parts, fields, truncation)
            added = jnp.where(active[None], noise[slot, child].astype(jnp.float32), 0.0)
            total = parent + added
            spectra_out[slot, child] = total.astype(spectra_out.dtype)
            rows = total.reshape(parts * fields, truncation)
            even_rows.append(jnp.where(is_odd, 0.0, rows).astype(jnp.bfloat16))
            odd_rows.append(jnp.where(is_odd, rows, 0.0).astype(jnp.bfloat16))
    result = jnp.dot(
        jnp.concatenate(even_rows, axis=0), even[...], preferred_element_type=jnp.float32
    )
    result += jnp.dot(
        jnp.concatenate(odd_rows, axis=0), odd[...], preferred_element_type=jnp.float32
    )
    fourier_out[...] = result.reshape(fourier_out.shape).astype(fourier_out.dtype)


def inverse_transform(waves, offsets, first, block, low, own, high, noise, even, odd, outs):
    slots_all, mem_local, parts, fields, truncation = noise.shape
    latitudes = even.shape[1]
    slots = own.shape[0]
    at = first // block
    near = lambda step, w, o: (step, 0, 0, 0)
    far = lambda step, w, o: (at + step, 0, 0, 0, 0)
    table = pl.BlockSpec(even.shape, lambda step, w, o: (0, 0))
    noise_block = pl.BlockSpec((block,) + noise.shape[1:], far)
    fourier_shape = noise.shape[:4] + (latitudes,)
    fourier_block = pl.BlockSpec((block,) + fourier_shape[1:], far)
    operands = [low, *in_hbm(own), high, *in_hbm(noise), *in_vmem(even, odd)]
    in_specs = [pl.BlockSpec((block,) + a.shape[1:], near) for a in operands[:3]]
    in_specs += [noise_block, table, table]
    aliases = {}
    if outs is not None:
        aliases = {8: 0, 9: 1}
        operands += in_hbm(*outs)
        in_specs += [pl.BlockSpec(memory_space=pl.ANY)] * 2
    rows = slots * mem_local * parts * fields
    return pl.pallas_call(
        functools.partial(inverse_kernel, first, block),
        grid_spec=pltpu.PrefetchScalarGridSpec(
            num_scalar_prefetch=2,
            grid=(slots // block,),
            in_specs=in_specs,
            out_specs=[
                noise_block,
                fourier_block,
                pl.BlockSpec(TOKEN, lambda step, w, o: (0, 0)),
            ],
        ),
        out_shape=[
            jax.ShapeDtypeStruct(noise.shape, jnp.bfloat16),
            jax.ShapeDtypeStruct(fourier_shape, jnp.bfloat16),
            jax.ShapeDtypeStruct(TOKEN, jnp.float32),
        ],
        input_output_aliases=aliases,
        compiler_params=pltpu.CompilerParams(vmem_limit_bytes=VMEM_BYTES),
        cost_estimate=pl.CostEstimate(
            flops=4 * rows * truncation * latitudes,
            bytes_accessed=2 * rows * (5 * truncation + latitudes) + 4 * even.size,
            transcendentals=0,
        ),
        name="inverse",
    )(waves, offsets, *operands)


def copy_kernel(offsets, low, own, high, *rest):
    out = rest[-1]
    rows = out.shape[1] // offsets.shape[0]
    for child in range(offsets.shape[0]):
        index, chosen = 0, None
        for source in (low, own, high):
            for at in range(source.shape[1] // rows):
                value = source[:, at * rows : (at + 1) * rows]
                chosen = value if index == 0 else jnp.where(offsets[child] == index, value, chosen)
                index += 1
        out[:, child * rows : (child + 1) * rows] = chosen


def copy_parents(offsets, low, own, high, tokens):
    steps = math.gcd(own.shape[0], 4)
    block = lambda array: pl.BlockSpec(
        (array.shape[0] // steps,) + array.shape[1:], lambda step, o: (step, 0, 0)
    )
    return pl.pallas_call(
        copy_kernel,
        grid_spec=pltpu.PrefetchScalarGridSpec(
            num_scalar_prefetch=1,
            grid=(steps,),
            in_specs=[block(low), block(own), block(high)]
            + [pl.BlockSpec(memory_space=pl.ANY)] * len(tokens),
            out_specs=block(own),
        ),
        out_shape=pltpu.HBM(own.shape, own.dtype),
        compiler_params=pltpu.CompilerParams(vmem_limit_bytes=VMEM_BYTES),
        cost_estimate=pl.CostEstimate(flops=0, bytes_accessed=8 * own.size, transcendentals=0),
        name="parents",
    )(offsets, low, *in_hbm(own), high, *tokens)


def finish_block(first, waves, received, noise, even, odd, spectra_out, fourier_out, ready, store):
    truncation = even.shape[0]
    block, mem_local, parts, fields = noise.shape[:4]
    per_slot = received.shape[1] // block
    rows = jnp.concatenate([received[g] for g in range(received.shape[0])], axis=-1)
    contract = (((1,), (1,)), ((), ()))
    by_even = lax.dot_general(rows, even[...], contract, preferred_element_type=jnp.float32)
    by_odd = lax.dot_general(rows, odd[...], contract, preferred_element_type=jnp.float32)
    degree = lax.broadcasted_iota(jnp.int32, (per_slot, truncation), 1)
    even_rows, odd_rows = [], []
    ready()
    for slot in range(block):
        wave = waves[first + slot]
        least = jnp.where(wave < truncation, wave, truncation)
        is_odd = wave % 2 == 1
        active = degree >= least
        here = slice(slot * per_slot, (slot + 1) * per_slot)
        spectra = jnp.where(is_odd, by_odd[here], by_even[here])
        spectra = spectra.astype(jnp.bfloat16).astype(jnp.float32)
        added = noise[slot].astype(jnp.float32).reshape(per_slot, truncation)
        child = jnp.where(active, spectra + added, 0.0)
        spectra_out[slot] = child.reshape(noise.shape[1:]).astype(spectra_out.dtype)
        even_rows.append(jnp.where(is_odd, 0.0, child).astype(jnp.bfloat16))
        odd_rows.append(jnp.where(is_odd, child, 0.0).astype(jnp.bfloat16))
    store()
    result = jnp.dot(
        jnp.concatenate(even_rows, axis=0), even[...], preferred_element_type=jnp.float32
    )
    result += jnp.dot(
        jnp.concatenate(odd_rows, axis=0), odd[...], preferred_element_type=jnp.float32
    )
    fourier_out[...] = result.reshape(fourier_out.shape).astype(fourier_out.dtype)


def finish_kernel(first, block, waves, received, noise, even, odd, *rest):
    start = first + pl.program_id(0) * block
    nothing = lambda: None
    finish_block(start, waves, received, noise, even, odd, *rest[-2:], nothing, nothing)


def last_kernel(first, waves, received, noise, even, odd, *rest):
    spectra_out, fourier_out, noise_here, spectra_here, fourier_here, sems = rest[-6:]
    part = pl.ds(first, noise_here.shape[0])
    fetch = pltpu.make_async_copy(noise.at[part], noise_here, sems.at[0])
    leave = pltpu.make_async_copy(spectra_here, spectra_out.at[part], sems.at[1])
    leave_too = pltpu.make_async_copy(fourier_here, fourier_out.at[part], sems.at[2])
    fetch.start()
    finish_block(
        first,
        waves,
        received,
        noise_here,
        even,
        odd,
        spectra_here,
        fourier_here,
        fetch.wait,
        leave.start,
    )
    leave_too.start()
    leave.wait()
    leave_too.wait()


def last_transform(waves, first, received, noise, even, odd, outs):
    slots_all, mem_local, parts, fields, truncation = noise.shape
    latitudes = even.shape[1]
    all_rows = received.shape[1]
    block = all_rows // (mem_local * parts * fields)
    fourier_shape = noise.shape[:4] + (latitudes,)
    here = pl.BlockSpec(memory_space=pltpu.VMEM)
    anywhere = pl.BlockSpec(memory_space=pl.ANY)
    return pl.pallas_call(
        functools.partial(last_kernel, first),
        in_specs=[pl.BlockSpec(memory_space=pltpu.SMEM), here, anywhere, here, here]
        + [anywhere] * 2,
        out_specs=[anywhere, anywhere],
        out_shape=[
            jax.ShapeDtypeStruct(noise.shape, jnp.bfloat16),
            jax.ShapeDtypeStruct(fourier_shape, jnp.bfloat16),
        ],
        scratch_shapes=[
            pltpu.VMEM((block,) + noise.shape[1:], jnp.bfloat16),
            pltpu.VMEM((block,) + noise.shape[1:], jnp.bfloat16),
            pltpu.VMEM((block,) + fourier_shape[1:], jnp.bfloat16),
            pltpu.SemaphoreType.DMA((3,)),
        ],
        input_output_aliases={5: 0, 6: 1},
        compiler_params=pltpu.CompilerParams(vmem_limit_bytes=VMEM_BYTES),
        cost_estimate=pl.CostEstimate(
            flops=8 * all_rows * truncation * latitudes,
            bytes_accessed=2 * all_rows * (2 * truncation + 2 * latitudes) + 4 * even.size,
            transcendentals=0,
        ),
        name="last",
    )(waves, received, *in_hbm(noise), *in_vmem(even, odd), *in_hbm(*outs))


def finish_transform(waves, first, block, received, noise, even, odd, outs):
    slots_all, mem_local, parts, fields, truncation = noise.shape
    latitudes = even.shape[1]
    groups, all_rows, lat_local = received.shape
    per_slot = mem_local * parts * fields
    at = first // block
    far = lambda step, w: (at + step, 0, 0, 0, 0)
    table = pl.BlockSpec(even.shape, lambda step, w: (0, 0))
    noise_block = pl.BlockSpec((block,) + noise.shape[1:], far)
    fourier_shape = noise.shape[:4] + (latitudes,)
    fourier_block = pl.BlockSpec((block,) + fourier_shape[1:], far)
    received_block = pl.BlockSpec(
        (groups, block * per_slot, lat_local), lambda step, w: (0, step, 0)
    )
    return pl.pallas_call(
        functools.partial(finish_kernel, first, block),
        grid_spec=pltpu.PrefetchScalarGridSpec(
            num_scalar_prefetch=1,
            grid=(all_rows // (block * per_slot),),
            in_specs=[received_block, noise_block, table, table]
            + [pl.BlockSpec(memory_space=pl.ANY)] * 2,
            out_specs=[noise_block, fourier_block],
        ),
        out_shape=[
            jax.ShapeDtypeStruct(noise.shape, jnp.bfloat16),
            jax.ShapeDtypeStruct(fourier_shape, jnp.bfloat16),
        ],
        input_output_aliases={5: 0, 6: 1},
        compiler_params=pltpu.CompilerParams(vmem_limit_bytes=VMEM_BYTES),
        cost_estimate=pl.CostEstimate(
            flops=8 * all_rows * truncation * latitudes,
            bytes_accessed=2 * all_rows * (2 * truncation + 2 * latitudes) + 4 * even.size,
            transcendentals=0,
        ),
        name="finish",
    )(waves, *in_hbm(received, noise), *in_vmem(even, odd), *in_hbm(*outs))


def chunk_bounds(slots_here, block):
    blocks = slots_here // block
    edges = [0, (blocks * 5 + 10) // 11, (blocks * 10 + 10) // 11, blocks]
    edges = [edge * block for edge in edges]
    return [(start, stop) for start, stop in zip(edges[:-1], edges[1:]) if stop > start]


def per_device(velocity, tracer, wave_slots, parents, noise):
    lat_count = lax.axis_size("lat")
    lat_index = lax.axis_index("lat")
    mem_count = lax.axis_size("member")
    group_index = lax.axis_index("member")
    mem_local, fields, lat_local, longitudes = velocity.shape
    slots_here, truncation = noise.shape[0], noise.shape[-1]
    block = math.gcd(slots_here, 8)
    per_member = 2 * fields
    per_slot = mem_local * per_member
    latitudes = lat_count * lat_local
    own_waves = lax.dynamic_slice_in_dim(wave_slots, lat_index * slots_here, slots_here)
    first_member = group_index * mem_local
    own_parents = lax.dynamic_slice_in_dim(parents, first_member, mem_local)
    offsets = own_parents - first_member + SPREAD
    upward = [(i, i + 1) for i in range(mem_count - 1)]
    downward = [(target, source) for source, target in upward]
    slot_grid = wave_slots.reshape(lat_count, slots_here)
    bounds = chunk_bounds(slots_here, block)
    inner = min(lat_local, LANES)
    starts = jnp.arange(latitudes // inner, dtype=jnp.int32) * inner

    def zonal(at):
        start, stop = bounds[at]
        waves = slot_grid[:, start:stop].reshape(-1, 1)
        return zonal_transform(waves, truncation, velocity, tracer, [])

    def neighbours(rows, per_member):
        low = lax.ppermute(rows[:, rows.shape[1] - SPREAD * per_member :], "member", upward)
        high = lax.ppermute(rows[:, : SPREAD * per_member], "member", downward)
        return low, rows, high

    def exchanged(outgoing):
        outgoing = outgoing.reshape(lat_count, -1, lat_local)
        moved = lax.all_to_all(outgoing, "lat", split_axis=0, concat_axis=0, tiled=True)
        if lat_local % LANES != 0:
            moved = jnp.swapaxes(moved, 0, 1).reshape(1, -1, latitudes)
        return moved

    def copied(at, tokens):
        return copy_parents(offsets, *neighbours(zonal(at), per_member), tokens)

    received = exchanged(zonal(0))
    even, odd = meridional_tables(truncation, latitudes, starts, inner)
    later = [exchanged(copied(1, []))] if len(bounds) > 1 else []
    spectra, _ = forward_transform(
        (own_waves, per_member), 0, block, received, even, odd, mem_local, []
    )
    *outs, token = inverse_transform(
        own_waves, offsets, 0, block, *neighbours(spectra, 1), noise, even, odd, None
    )
    later += [exchanged(copied(at, [token])) for at in range(2, len(bounds))]
    for (start, stop), received in zip(bounds[1:], later):
        if stop - start == block:
            outs = last_transform(own_waves, start, received, noise, even, odd, outs)
        else:
            outs = finish_transform(own_waves, start, block, received, noise, even, odd, outs)
    return tuple(outs)


def solution(mesh):
    in_specs = (
        P("member", None, "lat", None),
        P("member", None, "lat", None),
        P(),
        P(),
        P("lat", "member", None, None, None),
    )
    out_specs = (P("lat", "member", None, None, None), P("lat", "member", None, None, None))
    return jax.shard_map(
        per_device, mesh=mesh, in_specs=in_specs, out_specs=out_specs, check_vma=False
    )
```

```python
import functools
import math

import jax
import jax.numpy as jnp
from jax import lax
from jax.experimental import pallas as pl
from jax.experimental.pallas import tpu as pltpu
from jax.sharding import PartitionSpec as P

SPREAD = 2
VMEM_BYTES = 24 * 1024 * 1024
ZONAL_BYTES = 44 * 1024 * 1024
LANES = 128
SUBLANES = 8
TOKEN = (8, 128)


def in_hbm(*arrays):
    return [pltpu.with_memory_space_constraint(array, pltpu.HBM) for array in arrays]


def in_vmem(*arrays):
    return [pltpu.with_memory_space_constraint(array, pltpu.VMEM) for array in arrays]


def meridional_factors(truncation, latitudes, starts, width):
    degree = jnp.arange(truncation, dtype=jnp.int32)

    def angles(points):
        phase = degree[:, None] * points[None, :] % (4 * latitudes)
        return phase.astype(jnp.float32) * (math.pi / (2 * latitudes))

    coarse = angles(2 * starts)
    fine = angles(2 * jnp.arange(width, dtype=jnp.int32) + 1)
    factor = math.sqrt(2.0 / latitudes)
    return jnp.cos(coarse) * factor, jnp.sin(coarse) * factor, jnp.cos(fine), jnp.sin(fine)


def tables_kernel(cos_c, sin_c, cos_f, sin_f, even, odd, token):
    token[...] = jnp.zeros_like(token)
    width = cos_f.shape[1]
    cos_b, sin_b = cos_f[...], sin_f[...]
    for at in range(cos_c.shape[1]):
        cos_a, sin_a = cos_c[:, at : at + 1], sin_c[:, at : at + 1]
        columns = slice(at * width, (at + 1) * width)
        even[:, columns] = (cos_a * cos_b - sin_a * sin_b).astype(even.dtype)
        odd[:, columns] = (sin_a * cos_b + cos_a * sin_b).astype(odd.dtype)


def meridional_tables(truncation, latitudes, starts, width):
    factors = meridional_factors(truncation, latitudes, starts, width)
    shape = pltpu.VMEM((truncation, starts.shape[0] * width), jnp.bfloat16)
    return pl.pallas_call(
        tables_kernel,
        out_shape=[shape, shape, jax.ShapeDtypeStruct(TOKEN, jnp.float32)],
        compiler_params=pltpu.CompilerParams(vmem_limit_bytes=VMEM_BYTES),
        cost_estimate=pl.CostEstimate(
            flops=6 * truncation * latitudes, bytes_accessed=4 * truncation * latitudes,
            transcendentals=0,
        ),
        name="tables",
    )(*factors)


def zonal_kernel(truncation, tokens, waves, velocity, tracer, *rest):
    out, table, total, turned, velocity_here, tracer_here, sems, out_sems = rest[tokens:]
    members, fields, lat_local, longitudes = velocity.shape
    rows = waves.shape[0]
    groups = velocity_here.shape[0]
    step_fields = velocity_here.shape[1]
    steps = fields // step_fields

    def copies(step):
        part = (step // steps, pl.ds(step % steps * step_fields, step_fields))
        return [
            pltpu.make_async_copy(source.at[part], target.at[step], sems.at[step, at])
            for at, (source, target) in enumerate(
                ((velocity, velocity_here), (tracer, tracer_here))
            )
        ]

    for step in range(groups):
        for copy in copies(step):
            copy.start()

    wave = waves[...]
    weight = jnp.where(wave < truncation, 1.0 / math.sqrt(longitudes), 0.0)

    def cos_sin(count, stride):
        points = lax.broadcasted_iota(jnp.int32, (rows, count), 1) * stride
        phase = lax.rem(wave * points, jnp.full((), longitudes, jnp.int32))
        quarter = longitudes // 4
        turns = lax.div(phase + quarter // 2, jnp.full((), quarter, jnp.int32))
        angle = (phase - turns * quarter).astype(jnp.float32) * (2.0 * math.pi / longitudes)
        square = angle * angle
        cos, sin = 1.0 / 40320, -1.0 / 5040
        for power in (6, 4, 2, 0):
            sign = -1.0 if power % 4 else 1.0
            cos = cos * square + sign / math.factorial(power)
        for power in (5, 3, 1):
            sign = -1.0 if power % 4 == 3 else 1.0
            sin = sin * square + sign / math.factorial(power)
        sin = sin * angle
        swap = turns % 2 == 1
        cos, sin = jnp.where(swap, sin, cos), jnp.where(swap, cos, sin)
        cos = jnp.where((turns == 1) | (turns == 2), -cos, cos)
        sin = jnp.where((turns == 2) | (turns == 3), -sin, sin)
        return cos, sin

    (cos_c, sin_c), (cos_f, sin_f) = cos_sin(longitudes // LANES, LANES), cos_sin(LANES, 1)
    cos_c, sin_c = cos_c * weight, sin_c * weight
    for at in range(longitudes // LANES):
        cos_a, sin_a = cos_c[:, at : at + 1], sin_c[:, at : at + 1]
        columns = slice(at * LANES, (at + 1) * LANES)
        table[:rows, columns] = (cos_a * cos_f - sin_a * sin_f).astype(table.dtype)
        table[rows:, columns] = (-sin_a * cos_f - cos_a * sin_f).astype(table.dtype)

    def body(step, carry):
        for copy in copies(step):
            copy.wait()
        product = velocity_here[step].astype(jnp.float32) * tracer_here[step].astype(jnp.float32)
        product = product.astype(jnp.bfloat16).reshape(step_fields * lat_local, longitudes)
        sums = lax.dot_general(
            table[...], product, (((1,), (1,)), ((), ())), preferred_element_type=jnp.float32
        )
        first = step // steps * 2 * fields + step % steps * step_fields
        for part in range(2):
            for field in range(step_fields):
                block = sums[
                    part * rows : (part + 1) * rows, field * lat_local : (field + 1) * lat_local
                ]
                total[:, first + part * fields + field] = block.reshape(
                    rows // SUBLANES, SUBLANES, lat_local
                )
        return carry

    lax.fori_loop(0, groups, body, 0)

    tiles = rows // SUBLANES
    batch = math.gcd(tiles, 4)

    def leave(at):
        part = pl.ds(pl.multiple_of(at * batch * SUBLANES, SUBLANES), batch * SUBLANES)
        return pltpu.make_async_copy(turned.at[part], out.at[part], out_sems.at[at])

    def turn(at, carry):
        for tile in range(batch):
            first = pl.multiple_of((at * batch + tile) * SUBLANES, SUBLANES)
            tiles_here = jnp.swapaxes(total[at * batch + tile], 0, 1)
            turned[pl.ds(first, SUBLANES)] = tiles_here.astype(out.dtype)
        leave(at).start()
        return carry

    def end(at, carry):
        leave(at).wait()
        return carry

    lax.fori_loop(0, tiles // batch, turn, 0)
    lax.fori_loop(0, tiles // batch, end, 0)


def zonal_transform(waves, truncation, velocity, tracer, tokens):
    mem_local, fields, lat_local, longitudes = velocity.shape
    rows = waves.shape[0]
    fields_step = min(fields, max(1, 512 // lat_local))
    groups = mem_local * (fields // fields_step)
    out_rows = mem_local * 2 * fields
    grid_part = pltpu.VMEM((groups, fields_step, lat_local, longitudes), velocity.dtype)
    flops = 2 * 2 * rows * longitudes * mem_local * fields * lat_local
    moved = 2 * velocity.size * 2 + rows * out_rows * lat_local * 2
    return pl.pallas_call(
        functools.partial(zonal_kernel, truncation, len(tokens)),
        in_specs=[pl.BlockSpec(memory_space=pltpu.VMEM)]
        + [pl.BlockSpec(memory_space=pl.ANY)] * (2 + len(tokens)),
        out_specs=pl.BlockSpec(memory_space=pl.ANY),
        out_shape=pltpu.HBM((rows, out_rows, lat_local), jnp.bfloat16),
        scratch_shapes=[
            pltpu.VMEM((2 * rows, longitudes), jnp.bfloat16),
            pltpu.VMEM((rows // SUBLANES, out_rows, SUBLANES, lat_local), jnp.float32),
            pltpu.VMEM((rows, out_rows, lat_local), jnp.bfloat16),
            grid_part,
            grid_part,
            pltpu.SemaphoreType.DMA((groups, 2)),
            pltpu.SemaphoreType.DMA((rows // SUBLANES,)),
        ],
        compiler_params=pltpu.CompilerParams(vmem_limit_bytes=ZONAL_BYTES),
        cost_estimate=pl.CostEstimate(flops=flops, bytes_accessed=moved, transcendentals=0),
        name="zonal",
    )(waves, *in_hbm(velocity, tracer), *tokens)


def forward_kernel(first, block, waves, received, even, odd, *rest):
    out, token = rest[-2:]
    truncation = even.shape[0]
    step = pl.program_id(0)
    per_slot = received.shape[1] // block
    rows = jnp.concatenate([received[g] for g in range(received.shape[0])], axis=-1)
    contract = (((1,), (1,)), ((), ()))
    by_even = lax.dot_general(rows, even[...], contract, preferred_element_type=jnp.float32)
    by_odd = lax.dot_general(rows, odd[...], contract, preferred_element_type=jnp.float32)
    degree = lax.broadcasted_iota(jnp.int32, (per_slot, truncation), 1)
    for slot in range(block):
        wave = waves[first + step * block + slot]
        least = jnp.where(wave < truncation, wave, truncation)
        here = slice(slot * per_slot, (slot + 1) * per_slot)
        chosen = jnp.where(wave % 2 == 1, by_odd[here], by_even[here])
        chosen = jnp.where(degree >= least, chosen, 0.0)
        out[slot] = chosen.astype(out.dtype).reshape(out.shape[1:])
    token[...] = jnp.zeros_like(token)


def forward_transform(waves, first, block, received, even, odd, mem_local, tokens):
    groups, all_rows, lat_local = received.shape
    truncation, latitudes = even.shape
    slots = all_rows // (waves[1] * mem_local)
    out_shape = (slots, mem_local, waves[1], truncation)
    per_block = block * mem_local * waves[1]
    table = pl.BlockSpec(even.shape, lambda step, w: (0, 0))
    return pl.pallas_call(
        functools.partial(forward_kernel, first, block),
        grid_spec=pltpu.PrefetchScalarGridSpec(
            num_scalar_prefetch=1,
            grid=(slots // block,),
            in_specs=[
                pl.BlockSpec((groups, per_block, lat_local), lambda step, w: (0, step, 0)),
                table,
                table,
            ]
            + [pl.BlockSpec(memory_space=pl.ANY)] * len(tokens),
            out_specs=[
                pl.BlockSpec((block,) + out_shape[1:], lambda step, w: (step, 0, 0, 0)),
                pl.BlockSpec(TOKEN, lambda step, w: (0, 0)),
            ],
        ),
        out_shape=[
            pltpu.HBM(out_shape, jnp.bfloat16),
            jax.ShapeDtypeStruct(TOKEN, jnp.float32),
        ],
        compiler_params=pltpu.CompilerParams(vmem_limit_bytes=VMEM_BYTES),
        cost_estimate=pl.CostEstimate(
            flops=4 * all_rows * truncation * latitudes,
            bytes_accessed=2 * (all_rows * latitudes + 2 * even.size + all_rows * truncation),
            transcendentals=0,
        ),
        name="forward",
    )(waves[0], *in_hbm(received), *in_vmem(even, odd), *tokens)


def inverse_kernel(first, block, waves, offsets, low, own, high, noise, even, odd, *rest):
    spectra_out, fourier_out, token = rest[-3:]
    token[...] = jnp.zeros_like(token)
    truncation, latitudes = even.shape
    step = pl.program_id(0)
    mem_local, parts, fields = noise.shape[1:4]
    degree = lax.broadcasted_iota(jnp.int32, (fields, truncation), 1)
    sources = [low[:, m] for m in range(low.shape[1])]
    sources += [own[:, m] for m in range(own.shape[1])]
    sources += [high[:, m] for m in range(high.shape[1])]
    even_rows, odd_rows = [], []
    parents = []
    for child in range(mem_local):
        parent = sources[0]
        for at in range(1, len(sources)):
            parent = jnp.where(offsets[child] == at, sources[at], parent)
        parents.append(parent)
    for slot in range(block):
        wave = waves[first + step * block + slot]
        least = jnp.where(wave < truncation, wave, truncation)
        is_odd = wave % 2 == 1
        active = degree >= least
        for child in range(mem_local):
            parent = parents[child][slot].astype(jnp.float32)
            parent = parent.reshape(parts, fields, truncation)
            added = jnp.where(active[None], noise[slot, child].astype(jnp.float32), 0.0)
            total = parent + added
            spectra_out[slot, child] = total.astype(spectra_out.dtype)
            rows = total.reshape(parts * fields, truncation)
            even_rows.append(jnp.where(is_odd, 0.0, rows).astype(jnp.bfloat16))
            odd_rows.append(jnp.where(is_odd, rows, 0.0).astype(jnp.bfloat16))
    result = jnp.dot(
        jnp.concatenate(even_rows, axis=0), even[...], preferred_element_type=jnp.float32
    )
    result += jnp.dot(
        jnp.concatenate(odd_rows, axis=0), odd[...], preferred_element_type=jnp.float32
    )
    fourier_out[...] = result.reshape(fourier_out.shape).astype(fourier_out.dtype)


def inverse_transform(waves, offsets, first, block, low, own, high, noise, even, odd, outs):
    slots_all, mem_local, parts, fields, truncation = noise.shape
    latitudes = even.shape[1]
    slots = own.shape[0]
    at = first // block
    near = lambda step, w, o: (step, 0, 0, 0)
    far = lambda step, w, o: (at + step, 0, 0, 0, 0)
    table = pl.BlockSpec(even.shape, lambda step, w, o: (0, 0))
    noise_block = pl.BlockSpec((block,) + noise.shape[1:], far)
    fourier_shape = noise.shape[:4] + (latitudes,)
    fourier_block = pl.BlockSpec((block,) + fourier_shape[1:], far)
    operands = [low, *in_hbm(own), high, *in_hbm(noise), *in_vmem(even, odd)]
    in_specs = [pl.BlockSpec((block,) + a.shape[1:], near) for a in operands[:3]]
    in_specs += [noise_block, table, table]
    aliases = {}
    if outs is not None:
        aliases = {8: 0, 9: 1}
        operands += in_hbm(*outs)
        in_specs += [pl.BlockSpec(memory_space=pl.ANY)] * 2
    rows = slots * mem_local * parts * fields
    return pl.pallas_call(
        functools.partial(inverse_kernel, first, block),
        grid_spec=pltpu.PrefetchScalarGridSpec(
            num_scalar_prefetch=2,
            grid=(slots // block,),
            in_specs=in_specs,
            out_specs=[
                noise_block,
                fourier_block,
                pl.BlockSpec(TOKEN, lambda step, w, o: (0, 0)),
            ],
        ),
        out_shape=[
            jax.ShapeDtypeStruct(noise.shape, jnp.bfloat16),
            jax.ShapeDtypeStruct(fourier_shape, jnp.bfloat16),
            jax.ShapeDtypeStruct(TOKEN, jnp.float32),
        ],
        input_output_aliases=aliases,
        compiler_params=pltpu.CompilerParams(vmem_limit_bytes=VMEM_BYTES),
        cost_estimate=pl.CostEstimate(
            flops=4 * rows * truncation * latitudes,
            bytes_accessed=2 * rows * (5 * truncation + latitudes) + 4 * even.size,
            transcendentals=0,
        ),
        name="inverse",
    )(waves, offsets, *operands)


def copy_kernel(offsets, low, own, high, *rest):
    out = rest[-1]
    rows = out.shape[1] // offsets.shape[0]
    for child in range(offsets.shape[0]):
        index, chosen = 0, None
        for source in (low, own, high):
            for at in range(source.shape[1] // rows):
                value = source[:, at * rows : (at + 1) * rows]
                chosen = value if index == 0 else jnp.where(offsets[child] == index, value, chosen)
                index += 1
        out[:, child * rows : (child + 1) * rows] = chosen


def copy_parents(offsets, low, own, high, tokens):
    steps = math.gcd(own.shape[0], 4)
    block = lambda array: pl.BlockSpec(
        (array.shape[0] // steps,) + array.shape[1:], lambda step, o: (step, 0, 0)
    )
    return pl.pallas_call(
        copy_kernel,
        grid_spec=pltpu.PrefetchScalarGridSpec(
            num_scalar_prefetch=1,
            grid=(steps,),
            in_specs=[block(low), block(own), block(high)]
            + [pl.BlockSpec(memory_space=pl.ANY)] * len(tokens),
            out_specs=block(own),
        ),
        out_shape=pltpu.HBM(own.shape, own.dtype),
        compiler_params=pltpu.CompilerParams(vmem_limit_bytes=VMEM_BYTES),
        cost_estimate=pl.CostEstimate(flops=0, bytes_accessed=8 * own.size, transcendentals=0),
        name="parents",
    )(offsets, low, *in_hbm(own), high, *tokens)


def finish_block(first, waves, received, noise, even, odd, spectra_out, fourier_out, ready, store):
    truncation = even.shape[0]
    block, mem_local, parts, fields = noise.shape[:4]
    per_slot = received.shape[1] // block
    rows = jnp.concatenate([received[g] for g in range(received.shape[0])], axis=-1)
    contract = (((1,), (1,)), ((), ()))
    by_even = lax.dot_general(rows, even[...], contract, preferred_element_type=jnp.float32)
    by_odd = lax.dot_general(rows, odd[...], contract, preferred_element_type=jnp.float32)
    degree = lax.broadcasted_iota(jnp.int32, (per_slot, truncation), 1)
    even_rows, odd_rows = [], []
    ready()
    for slot in range(block):
        wave = waves[first + slot]
        least = jnp.where(wave < truncation, wave, truncation)
        is_odd = wave % 2 == 1
        active = degree >= least
        here = slice(slot * per_slot, (slot + 1) * per_slot)
        spectra = jnp.where(is_odd, by_odd[here], by_even[here])
        spectra = spectra.astype(jnp.bfloat16).astype(jnp.float32)
        added = noise[slot].astype(jnp.float32).reshape(per_slot, truncation)
        child = jnp.where(active, spectra + added, 0.0)
        spectra_out[slot] = child.reshape(noise.shape[1:]).astype(spectra_out.dtype)
        even_rows.append(jnp.where(is_odd, 0.0, child).astype(jnp.bfloat16))
        odd_rows.append(jnp.where(is_odd, child, 0.0).astype(jnp.bfloat16))
    store()
    result = jnp.dot(
        jnp.concatenate(even_rows, axis=0), even[...], preferred_element_type=jnp.float32
    )
    result += jnp.dot(
        jnp.concatenate(odd_rows, axis=0), odd[...], preferred_element_type=jnp.float32
    )
    fourier_out[...] = result.reshape(fourier_out.shape).astype(fourier_out.dtype)


def finish_kernel(first, block, waves, received, noise, even, odd, *rest):
    start = first + pl.program_id(0) * block
    nothing = lambda: None
    finish_block(start, waves, received, noise, even, odd, *rest[-2:], nothing, nothing)


def last_kernel(first, waves, received, noise, even, odd, *rest):
    spectra_out, fourier_out, noise_here, spectra_here, fourier_here, sems = rest[-6:]
    part = pl.ds(first, noise_here.shape[0])
    fetch = pltpu.make_async_copy(noise.at[part], noise_here, sems.at[0])
    leave = pltpu.make_async_copy(spectra_here, spectra_out.at[part], sems.at[1])
    leave_too = pltpu.make_async_copy(fourier_here, fourier_out.at[part], sems.at[2])
    fetch.start()
    finish_block(
        first,
        waves,
        received,
        noise_here,
        even,
        odd,
        spectra_here,
        fourier_here,
        fetch.wait,
        leave.start,
    )
    leave_too.start()
    leave.wait()
    leave_too.wait()


def last_transform(waves, first, received, noise, even, odd, outs):
    slots_all, mem_local, parts, fields, truncation = noise.shape
    latitudes = even.shape[1]
    all_rows = received.shape[1]
    block = all_rows // (mem_local * parts * fields)
    fourier_shape = noise.shape[:4] + (latitudes,)
    here = pl.BlockSpec(memory_space=pltpu.VMEM)
    anywhere = pl.BlockSpec(memory_space=pl.ANY)
    return pl.pallas_call(
        functools.partial(last_kernel, first),
        in_specs=[pl.BlockSpec(memory_space=pltpu.SMEM), here, anywhere, here, here]
        + [anywhere] * 2,
        out_specs=[anywhere, anywhere],
        out_shape=[
            jax.ShapeDtypeStruct(noise.shape, jnp.bfloat16),
            jax.ShapeDtypeStruct(fourier_shape, jnp.bfloat16),
        ],
        scratch_shapes=[
            pltpu.VMEM((block,) + noise.shape[1:], jnp.bfloat16),
            pltpu.VMEM((block,) + noise.shape[1:], jnp.bfloat16),
            pltpu.VMEM((block,) + fourier_shape[1:], jnp.bfloat16),
            pltpu.SemaphoreType.DMA((3,)),
        ],
        input_output_aliases={5: 0, 6: 1},
        compiler_params=pltpu.CompilerParams(vmem_limit_bytes=VMEM_BYTES),
        cost_estimate=pl.CostEstimate(
            flops=8 * all_rows * truncation * latitudes,
            bytes_accessed=2 * all_rows * (2 * truncation + 2 * latitudes) + 4 * even.size,
            transcendentals=0,
        ),
        name="last",
    )(waves, received, *in_hbm(noise), *in_vmem(even, odd), *in_hbm(*outs))


def finish_transform(waves, first, block, received, noise, even, odd, outs):
    slots_all, mem_local, parts, fields, truncation = noise.shape
    latitudes = even.shape[1]
    groups, all_rows, lat_local = received.shape
    per_slot = mem_local * parts * fields
    at = first // block
    far = lambda step, w: (at + step, 0, 0, 0, 0)
    table = pl.BlockSpec(even.shape, lambda step, w: (0, 0))
    noise_block = pl.BlockSpec((block,) + noise.shape[1:], far)
    fourier_shape = noise.shape[:4] + (latitudes,)
    fourier_block = pl.BlockSpec((block,) + fourier_shape[1:], far)
    received_block = pl.BlockSpec(
        (groups, block * per_slot, lat_local), lambda step, w: (0, step, 0)
    )
    return pl.pallas_call(
        functools.partial(finish_kernel, first, block),
        grid_spec=pltpu.PrefetchScalarGridSpec(
            num_scalar_prefetch=1,
            grid=(all_rows // (block * per_slot),),
            in_specs=[received_block, noise_block, table, table]
            + [pl.BlockSpec(memory_space=pl.ANY)] * 2,
            out_specs=[noise_block, fourier_block],
        ),
        out_shape=[
            jax.ShapeDtypeStruct(noise.shape, jnp.bfloat16),
            jax.ShapeDtypeStruct(fourier_shape, jnp.bfloat16),
        ],
        input_output_aliases={5: 0, 6: 1},
        compiler_params=pltpu.CompilerParams(vmem_limit_bytes=VMEM_BYTES),
        cost_estimate=pl.CostEstimate(
            flops=8 * all_rows * truncation * latitudes,
            bytes_accessed=2 * all_rows * (2 * truncation + 2 * latitudes) + 4 * even.size,
            transcendentals=0,
        ),
        name="finish",
    )(waves, *in_hbm(received, noise), *in_vmem(even, odd), *in_hbm(*outs))


def chunk_bounds(slots_here, block):
    blocks = slots_here // block
    edges = [0, (blocks * 5 + 10) // 11, (blocks * 10 + 10) // 11, blocks]
    edges = [edge * block for edge in edges]
    return [(start, stop) for start, stop in zip(edges[:-1], edges[1:]) if stop > start]


def per_device(velocity, tracer, wave_slots, parents, noise):
    lat_count = lax.axis_size("lat")
    lat_index = lax.axis_index("lat")
    mem_count = lax.axis_size("member")
    group_index = lax.axis_index("member")
    mem_local, fields, lat_local, longitudes = velocity.shape
    slots_here, truncation = noise.shape[0], noise.shape[-1]
    block = math.gcd(slots_here, 8)
    per_member = 2 * fields
    per_slot = mem_local * per_member
    latitudes = lat_count * lat_local
    own_waves = lax.dynamic_slice_in_dim(wave_slots, lat_index * slots_here, slots_here)
    first_member = group_index * mem_local
    own_parents = lax.dynamic_slice_in_dim(parents, first_member, mem_local)
    offsets = own_parents - first_member + SPREAD
    upward = [(i, i + 1) for i in range(mem_count - 1)]
    downward = [(target, source) for source, target in upward]
    slot_grid = wave_slots.reshape(lat_count, slots_here)
    bounds = chunk_bounds(slots_here, block)
    inner = min(lat_local, LANES)
    starts = jnp.arange(latitudes // inner, dtype=jnp.int32) * inner

    def zonal(at):
        start, stop = bounds[at]
        waves = slot_grid[:, start:stop].reshape(-1, 1)
        return zonal_transform(waves, truncation, velocity, tracer, [])

    def neighbours(rows, per_member):
        low = lax.ppermute(rows[:, rows.shape[1] - SPREAD * per_member :], "member", upward)
        high = lax.ppermute(rows[:, : SPREAD * per_member], "member", downward)
        return low, rows, high

    def exchanged(outgoing):
        outgoing = outgoing.reshape(lat_count, -1, lat_local)
        moved = lax.all_to_all(outgoing, "lat", split_axis=0, concat_axis=0, tiled=True)
        if lat_local % LANES != 0:
            moved = jnp.swapaxes(moved, 0, 1).reshape(1, -1, latitudes)
        return moved

    def exchanged_in_two(outgoing, token):
        outgoing = outgoing.reshape(lat_count // 2, 2, -1, lat_local)
        side = lat_index % 2
        kept = lax.dynamic_index_in_dim(outgoing, side, 1, keepdims=False)
        sent = lax.dynamic_index_in_dim(outgoing, 1 - side, 1, keepdims=False)
        swapped = lax.ppermute(sent, "lat", [(i, i ^ 1) for i in range(lat_count)])
        side = side + token[0, 0].astype(jnp.int32)
        pair = jnp.where(side == 0, jnp.stack([kept, swapped], 1), jnp.stack([swapped, kept], 1))
        groups = [list(range(first, lat_count, 2)) for first in range(2)]
        moved = lax.all_to_all(
            pair, "lat", split_axis=0, concat_axis=0, axis_index_groups=groups, tiled=True
        )
        return moved.reshape(lat_count, -1, lat_local)

    received = exchanged(zonal(0))
    even, odd, made = meridional_tables(truncation, latitudes, starts, inner)
    sides = [neighbours(zonal(at), per_member) for at in range(1, len(bounds))]
    tokens = [made] + [part for low, _, high in sides[1:] for part in (low, high)]
    later = [exchanged(copy_parents(offsets, *side, tokens)) for side in sides[:1]]
    picked = [copy_parents(offsets, *side, []) for side in sides[1:]]
    spectra, _ = forward_transform(
        (own_waves, per_member), 0, block, received, even, odd, mem_local, []
    )
    *outs, token = inverse_transform(
        own_waves, offsets, 0, block, *neighbours(spectra, 1), noise, even, odd, None
    )
    for outgoing in picked:
        if lat_count % 2 == 0 and lat_local % LANES == 0:
            later.append(exchanged_in_two(outgoing, token))
        else:
            later.append(exchanged(outgoing))
    for (start, stop), received in zip(bounds[1:], later):
        if stop - start == block:
            outs = last_transform(own_waves, start, received, noise, even, odd, outs)
        else:
            outs = finish_transform(own_waves, start, block, received, noise, even, odd, outs)
    return tuple(outs)


def solution(mesh):
    in_specs = (
        P("member", None, "lat", None),
        P("member", None, "lat", None),
        P(),
        P(),
        P("lat", "member", None, None, None),
    )
    out_specs = (P("lat", "member", None, None, None), P("lat", "member", None, None, None))
    return jax.shard_map(
        per_device, mesh=mesh, in_specs=in_specs, out_specs=out_specs, check_vma=False
    )
```

```python
import functools
import math

import jax
import jax.numpy as jnp
from jax import lax
from jax.experimental import pallas as pl
from jax.experimental.pallas import tpu as pltpu
from jax.sharding import PartitionSpec as P

SPREAD = 2
VMEM_BYTES = 24 * 1024 * 1024
ZONAL_BYTES = 44 * 1024 * 1024
LANES = 128
SUBLANES = 8
TOKEN = (8, 128)


def in_hbm(*arrays):
    return [pltpu.with_memory_space_constraint(array, pltpu.HBM) for array in arrays]


def in_vmem(*arrays):
    return [pltpu.with_memory_space_constraint(array, pltpu.VMEM) for array in arrays]


def meridional_factors(truncation, latitudes, starts, width):
    degree = jnp.arange(truncation, dtype=jnp.int32)

    def angles(points):
        phase = degree[:, None] * points[None, :] % (4 * latitudes)
        return phase.astype(jnp.float32) * (math.pi / (2 * latitudes))

    coarse = angles(2 * starts)
    fine = angles(2 * jnp.arange(width, dtype=jnp.int32) + 1)
    factor = math.sqrt(2.0 / latitudes)
    return jnp.cos(coarse) * factor, jnp.sin(coarse) * factor, jnp.cos(fine), jnp.sin(fine)


def tables_kernel(cos_c, sin_c, cos_f, sin_f, even, odd, token):
    token[...] = jnp.zeros_like(token)
    width = cos_f.shape[1]
    cos_b, sin_b = cos_f[...], sin_f[...]
    for at in range(cos_c.shape[1]):
        cos_a, sin_a = cos_c[:, at : at + 1], sin_c[:, at : at + 1]
        columns = slice(at * width, (at + 1) * width)
        even[:, columns] = (cos_a * cos_b - sin_a * sin_b).astype(even.dtype)
        odd[:, columns] = (sin_a * cos_b + cos_a * sin_b).astype(odd.dtype)


def meridional_tables(truncation, latitudes, starts, width):
    factors = meridional_factors(truncation, latitudes, starts, width)
    shape = pltpu.VMEM((truncation, starts.shape[0] * width), jnp.bfloat16)
    return pl.pallas_call(
        tables_kernel,
        out_shape=[shape, shape, jax.ShapeDtypeStruct(TOKEN, jnp.float32)],
        compiler_params=pltpu.CompilerParams(vmem_limit_bytes=VMEM_BYTES),
        cost_estimate=pl.CostEstimate(
            flops=6 * truncation * latitudes, bytes_accessed=4 * truncation * latitudes,
            transcendentals=0,
        ),
        name="tables",
    )(*factors)


def zonal_kernel(truncation, tokens, waves, velocity, tracer, *rest):
    out, table, total, turned, velocity_here, tracer_here, sems, out_sems = rest[tokens:]
    members, fields, lat_local, longitudes = velocity.shape
    rows = waves.shape[0]
    groups = velocity_here.shape[0]
    step_fields = velocity_here.shape[1]
    steps = fields // step_fields

    def copies(step):
        part = (step // steps, pl.ds(step % steps * step_fields, step_fields))
        return [
            pltpu.make_async_copy(source.at[part], target.at[step], sems.at[step, at])
            for at, (source, target) in enumerate(
                ((velocity, velocity_here), (tracer, tracer_here))
            )
        ]

    for step in range(groups):
        for copy in copies(step):
            copy.start()

    wave = waves[...]
    weight = jnp.where(wave < truncation, 1.0 / math.sqrt(longitudes), 0.0)

    def cos_sin(count, stride):
        points = lax.broadcasted_iota(jnp.int32, (rows, count), 1) * stride
        phase = lax.rem(wave * points, jnp.full((), longitudes, jnp.int32))
        quarter = longitudes // 4
        turns = lax.div(phase + quarter // 2, jnp.full((), quarter, jnp.int32))
        angle = (phase - turns * quarter).astype(jnp.float32) * (2.0 * math.pi / longitudes)
        square = angle * angle
        cos, sin = 1.0 / 40320, -1.0 / 5040
        for power in (6, 4, 2, 0):
            sign = -1.0 if power % 4 else 1.0
            cos = cos * square + sign / math.factorial(power)
        for power in (5, 3, 1):
            sign = -1.0 if power % 4 == 3 else 1.0
            sin = sin * square + sign / math.factorial(power)
        sin = sin * angle
        swap = turns % 2 == 1
        cos, sin = jnp.where(swap, sin, cos), jnp.where(swap, cos, sin)
        cos = jnp.where((turns == 1) | (turns == 2), -cos, cos)
        sin = jnp.where((turns == 2) | (turns == 3), -sin, sin)
        return cos, sin

    (cos_c, sin_c), (cos_f, sin_f) = cos_sin(longitudes // LANES, LANES), cos_sin(LANES, 1)
    cos_c, sin_c = cos_c * weight, sin_c * weight
    for at in range(longitudes // LANES):
        cos_a, sin_a = cos_c[:, at : at + 1], sin_c[:, at : at + 1]
        columns = slice(at * LANES, (at + 1) * LANES)
        table[:rows, columns] = (cos_a * cos_f - sin_a * sin_f).astype(table.dtype)
        table[rows:, columns] = (-sin_a * cos_f - cos_a * sin_f).astype(table.dtype)

    def body(step, carry):
        for copy in copies(step):
            copy.wait()
        product = velocity_here[step].astype(jnp.float32) * tracer_here[step].astype(jnp.float32)
        product = product.astype(jnp.bfloat16).reshape(step_fields * lat_local, longitudes)
        sums = lax.dot_general(
            table[...], product, (((1,), (1,)), ((), ())), preferred_element_type=jnp.float32
        )
        first = step // steps * 2 * fields + step % steps * step_fields
        for part in range(2):
            for field in range(step_fields):
                block = sums[
                    part * rows : (part + 1) * rows, field * lat_local : (field + 1) * lat_local
                ]
                total[:, first + part * fields + field] = block.reshape(
                    rows // SUBLANES, SUBLANES, lat_local
                )
        return carry

    lax.fori_loop(0, groups, body, 0)

    tiles = rows // SUBLANES
    batch = math.gcd(tiles, 4)

    def leave(at):
        part = pl.ds(pl.multiple_of(at * batch * SUBLANES, SUBLANES), batch * SUBLANES)
        return pltpu.make_async_copy(turned.at[part], out.at[part], out_sems.at[at])

    def turn(at, carry):
        for tile in range(batch):
            first = pl.multiple_of((at * batch + tile) * SUBLANES, SUBLANES)
            tiles_here = jnp.swapaxes(total[at * batch + tile], 0, 1)
            turned[pl.ds(first, SUBLANES)] = tiles_here.astype(out.dtype)
        leave(at).start()
        return carry

    def end(at, carry):
        leave(at).wait()
        return carry

    lax.fori_loop(0, tiles // batch, turn, 0)
    lax.fori_loop(0, tiles // batch, end, 0)


def zonal_transform(waves, truncation, velocity, tracer, tokens):
    mem_local, fields, lat_local, longitudes = velocity.shape
    rows = waves.shape[0]
    fields_step = min(fields, max(1, 512 // lat_local))
    groups = mem_local * (fields // fields_step)
    out_rows = mem_local * 2 * fields
    grid_part = pltpu.VMEM((groups, fields_step, lat_local, longitudes), velocity.dtype)
    flops = 2 * 2 * rows * longitudes * mem_local * fields * lat_local
    moved = 2 * velocity.size * 2 + rows * out_rows * lat_local * 2
    return pl.pallas_call(
        functools.partial(zonal_kernel, truncation, len(tokens)),
        in_specs=[pl.BlockSpec(memory_space=pltpu.VMEM)]
        + [pl.BlockSpec(memory_space=pl.ANY)] * (2 + len(tokens)),
        out_specs=pl.BlockSpec(memory_space=pl.ANY),
        out_shape=pltpu.HBM((rows, out_rows, lat_local), jnp.bfloat16),
        scratch_shapes=[
            pltpu.VMEM((2 * rows, longitudes), jnp.bfloat16),
            pltpu.VMEM((rows // SUBLANES, out_rows, SUBLANES, lat_local), jnp.float32),
            pltpu.VMEM((rows, out_rows, lat_local), jnp.bfloat16),
            grid_part,
            grid_part,
            pltpu.SemaphoreType.DMA((groups, 2)),
            pltpu.SemaphoreType.DMA((rows // SUBLANES,)),
        ],
        compiler_params=pltpu.CompilerParams(vmem_limit_bytes=ZONAL_BYTES),
        cost_estimate=pl.CostEstimate(flops=flops, bytes_accessed=moved, transcendentals=0),
        name="zonal",
    )(waves, *in_hbm(velocity, tracer), *tokens)


def forward_kernel(first, block, waves, received, even, odd, *rest):
    out, token = rest[-2:]
    truncation = even.shape[0]
    step = pl.program_id(0)
    per_slot = received.shape[1] // block
    rows = jnp.concatenate([received[g] for g in range(received.shape[0])], axis=-1)
    contract = (((1,), (1,)), ((), ()))
    by_even = lax.dot_general(rows, even[...], contract, preferred_element_type=jnp.float32)
    by_odd = lax.dot_general(rows, odd[...], contract, preferred_element_type=jnp.float32)
    degree = lax.broadcasted_iota(jnp.int32, (per_slot, truncation), 1)
    for slot in range(block):
        wave = waves[first + step * block + slot]
        least = jnp.where(wave < truncation, wave, truncation)
        here = slice(slot * per_slot, (slot + 1) * per_slot)
        chosen = jnp.where(wave % 2 == 1, by_odd[here], by_even[here])
        chosen = jnp.where(degree >= least, chosen, 0.0)
        out[slot] = chosen.astype(out.dtype).reshape(out.shape[1:])
    token[...] = jnp.zeros_like(token)


def forward_transform(waves, first, block, received, even, odd, mem_local, tokens):
    groups, all_rows, lat_local = received.shape
    truncation, latitudes = even.shape
    slots = all_rows // (waves[1] * mem_local)
    out_shape = (slots, mem_local, waves[1], truncation)
    per_block = block * mem_local * waves[1]
    table = pl.BlockSpec(even.shape, lambda step, w: (0, 0))
    return pl.pallas_call(
        functools.partial(forward_kernel, first, block),
        grid_spec=pltpu.PrefetchScalarGridSpec(
            num_scalar_prefetch=1,
            grid=(slots // block,),
            in_specs=[
                pl.BlockSpec((groups, per_block, lat_local), lambda step, w: (0, step, 0)),
                table,
                table,
            ]
            + [pl.BlockSpec(memory_space=pl.ANY)] * len(tokens),
            out_specs=[
                pl.BlockSpec((block,) + out_shape[1:], lambda step, w: (step, 0, 0, 0)),
                pl.BlockSpec(TOKEN, lambda step, w: (0, 0)),
            ],
        ),
        out_shape=[
            pltpu.HBM(out_shape, jnp.bfloat16),
            jax.ShapeDtypeStruct(TOKEN, jnp.float32),
        ],
        compiler_params=pltpu.CompilerParams(vmem_limit_bytes=VMEM_BYTES),
        cost_estimate=pl.CostEstimate(
            flops=4 * all_rows * truncation * latitudes,
            bytes_accessed=2 * (all_rows * latitudes + 2 * even.size + all_rows * truncation),
            transcendentals=0,
        ),
        name="forward",
    )(waves[0], *in_hbm(received), *in_vmem(even, odd), *tokens)


def inverse_kernel(first, block, waves, offsets, low, own, high, noise, even, odd, *rest):
    spectra_out, fourier_out, token = rest[-3:]
    token[...] = jnp.zeros_like(token)
    truncation, latitudes = even.shape
    step = pl.program_id(0)
    mem_local, parts, fields = noise.shape[1:4]
    degree = lax.broadcasted_iota(jnp.int32, (fields, truncation), 1)
    sources = [low[:, m] for m in range(low.shape[1])]
    sources += [own[:, m] for m in range(own.shape[1])]
    sources += [high[:, m] for m in range(high.shape[1])]
    even_rows, odd_rows = [], []
    parents = []
    for child in range(mem_local):
        parent = sources[0]
        for at in range(1, len(sources)):
            parent = jnp.where(offsets[child] == at, sources[at], parent)
        parents.append(parent)
    for slot in range(block):
        wave = waves[first + step * block + slot]
        least = jnp.where(wave < truncation, wave, truncation)
        is_odd = wave % 2 == 1
        active = degree >= least
        for child in range(mem_local):
            parent = parents[child][slot].astype(jnp.float32)
            parent = parent.reshape(parts, fields, truncation)
            added = jnp.where(active[None], noise[slot, child].astype(jnp.float32), 0.0)
            total = parent + added
            spectra_out[slot, child] = total.astype(spectra_out.dtype)
            rows = total.reshape(parts * fields, truncation)
            even_rows.append(jnp.where(is_odd, 0.0, rows).astype(jnp.bfloat16))
            odd_rows.append(jnp.where(is_odd, rows, 0.0).astype(jnp.bfloat16))
    result = jnp.dot(
        jnp.concatenate(even_rows, axis=0), even[...], preferred_element_type=jnp.float32
    )
    result += jnp.dot(
        jnp.concatenate(odd_rows, axis=0), odd[...], preferred_element_type=jnp.float32
    )
    fourier_out[...] = result.reshape(fourier_out.shape).astype(fourier_out.dtype)


def inverse_transform(waves, offsets, first, block, low, own, high, noise, even, odd, outs):
    slots_all, mem_local, parts, fields, truncation = noise.shape
    latitudes = even.shape[1]
    slots = own.shape[0]
    at = first // block
    near = lambda step, w, o: (step, 0, 0, 0)
    far = lambda step, w, o: (at + step, 0, 0, 0, 0)
    table = pl.BlockSpec(even.shape, lambda step, w, o: (0, 0))
    noise_block = pl.BlockSpec((block,) + noise.shape[1:], far)
    fourier_shape = noise.shape[:4] + (latitudes,)
    fourier_block = pl.BlockSpec((block,) + fourier_shape[1:], far)
    operands = [low, *in_hbm(own), high, *in_hbm(noise), *in_vmem(even, odd)]
    in_specs = [pl.BlockSpec((block,) + a.shape[1:], near) for a in operands[:3]]
    in_specs += [noise_block, table, table]
    aliases = {}
    if outs is not None:
        aliases = {8: 0, 9: 1}
        operands += in_hbm(*outs)
        in_specs += [pl.BlockSpec(memory_space=pl.ANY)] * 2
    rows = slots * mem_local * parts * fields
    return pl.pallas_call(
        functools.partial(inverse_kernel, first, block),
        grid_spec=pltpu.PrefetchScalarGridSpec(
            num_scalar_prefetch=2,
            grid=(slots // block,),
            in_specs=in_specs,
            out_specs=[
                noise_block,
                fourier_block,
                pl.BlockSpec(TOKEN, lambda step, w, o: (0, 0)),
            ],
        ),
        out_shape=[
            jax.ShapeDtypeStruct(noise.shape, jnp.bfloat16),
            jax.ShapeDtypeStruct(fourier_shape, jnp.bfloat16),
            jax.ShapeDtypeStruct(TOKEN, jnp.float32),
        ],
        input_output_aliases=aliases,
        compiler_params=pltpu.CompilerParams(vmem_limit_bytes=VMEM_BYTES),
        cost_estimate=pl.CostEstimate(
            flops=4 * rows * truncation * latitudes,
            bytes_accessed=2 * rows * (5 * truncation + latitudes) + 4 * even.size,
            transcendentals=0,
        ),
        name="inverse",
    )(waves, offsets, *operands)


def copy_kernel(offsets, low, own, high, *rest):
    out = rest[-1]
    rows = out.shape[1] // offsets.shape[0]
    for child in range(offsets.shape[0]):
        index, chosen = 0, None
        for source in (low, own, high):
            for at in range(source.shape[1] // rows):
                value = source[:, at * rows : (at + 1) * rows]
                chosen = value if index == 0 else jnp.where(offsets[child] == index, value, chosen)
                index += 1
        out[:, child * rows : (child + 1) * rows] = chosen


def copy_parents(offsets, low, own, high, tokens):
    steps = math.gcd(own.shape[0], 4)
    block = lambda array: pl.BlockSpec(
        (array.shape[0] // steps,) + array.shape[1:], lambda step, o: (step, 0, 0)
    )
    return pl.pallas_call(
        copy_kernel,
        grid_spec=pltpu.PrefetchScalarGridSpec(
            num_scalar_prefetch=1,
            grid=(steps,),
            in_specs=[block(low), block(own), block(high)]
            + [pl.BlockSpec(memory_space=pl.ANY)] * len(tokens),
            out_specs=block(own),
        ),
        out_shape=pltpu.HBM(own.shape, own.dtype),
        compiler_params=pltpu.CompilerParams(vmem_limit_bytes=VMEM_BYTES),
        cost_estimate=pl.CostEstimate(flops=0, bytes_accessed=8 * own.size, transcendentals=0),
        name="parents",
    )(offsets, low, *in_hbm(own), high, *tokens)


def finish_block(first, waves, received, noise, even, odd, spectra_out, fourier_out, ready, store):
    truncation = even.shape[0]
    block, mem_local, parts, fields = noise.shape[:4]
    per_slot = received.shape[1] // block
    rows = jnp.concatenate([received[g] for g in range(received.shape[0])], axis=-1)
    contract = (((1,), (1,)), ((), ()))
    by_even = lax.dot_general(rows, even[...], contract, preferred_element_type=jnp.float32)
    by_odd = lax.dot_general(rows, odd[...], contract, preferred_element_type=jnp.float32)
    degree = lax.broadcasted_iota(jnp.int32, (per_slot, truncation), 1)
    even_rows, odd_rows = [], []
    ready()
    for slot in range(block):
        wave = waves[first + slot]
        least = jnp.where(wave < truncation, wave, truncation)
        is_odd = wave % 2 == 1
        active = degree >= least
        here = slice(slot * per_slot, (slot + 1) * per_slot)
        spectra = jnp.where(is_odd, by_odd[here], by_even[here])
        spectra = spectra.astype(jnp.bfloat16).astype(jnp.float32)
        added = noise[slot].astype(jnp.float32).reshape(per_slot, truncation)
        child = jnp.where(active, spectra + added, 0.0)
        spectra_out[slot] = child.reshape(noise.shape[1:]).astype(spectra_out.dtype)
        even_rows.append(jnp.where(is_odd, 0.0, child).astype(jnp.bfloat16))
        odd_rows.append(jnp.where(is_odd, child, 0.0).astype(jnp.bfloat16))
    store()
    result = jnp.dot(
        jnp.concatenate(even_rows, axis=0), even[...], preferred_element_type=jnp.float32
    )
    result += jnp.dot(
        jnp.concatenate(odd_rows, axis=0), odd[...], preferred_element_type=jnp.float32
    )
    fourier_out[...] = result.reshape(fourier_out.shape).astype(fourier_out.dtype)


def finish_kernel(first, block, waves, received, noise, even, odd, *rest):
    start = first + pl.program_id(0) * block
    nothing = lambda: None
    finish_block(start, waves, received, noise, even, odd, *rest[-2:], nothing, nothing)


def last_kernel(first, waves, received, noise, even, odd, *rest):
    spectra_out, fourier_out, noise_here, spectra_here, fourier_here, sems = rest[-6:]
    part = pl.ds(first, noise_here.shape[0])
    fetch = pltpu.make_async_copy(noise.at[part], noise_here, sems.at[0])
    leave = pltpu.make_async_copy(spectra_here, spectra_out.at[part], sems.at[1])
    leave_too = pltpu.make_async_copy(fourier_here, fourier_out.at[part], sems.at[2])
    fetch.start()
    finish_block(
        first,
        waves,
        received,
        noise_here,
        even,
        odd,
        spectra_here,
        fourier_here,
        fetch.wait,
        leave.start,
    )
    leave_too.start()
    leave.wait()
    leave_too.wait()


def last_transform(waves, first, received, noise, even, odd, outs):
    slots_all, mem_local, parts, fields, truncation = noise.shape
    latitudes = even.shape[1]
    all_rows = received.shape[1]
    block = all_rows // (mem_local * parts * fields)
    fourier_shape = noise.shape[:4] + (latitudes,)
    here = pl.BlockSpec(memory_space=pltpu.VMEM)
    anywhere = pl.BlockSpec(memory_space=pl.ANY)
    return pl.pallas_call(
        functools.partial(last_kernel, first),
        in_specs=[pl.BlockSpec(memory_space=pltpu.SMEM), here, anywhere, here, here]
        + [anywhere] * 2,
        out_specs=[anywhere, anywhere],
        out_shape=[
            jax.ShapeDtypeStruct(noise.shape, jnp.bfloat16),
            jax.ShapeDtypeStruct(fourier_shape, jnp.bfloat16),
        ],
        scratch_shapes=[
            pltpu.VMEM((block,) + noise.shape[1:], jnp.bfloat16),
            pltpu.VMEM((block,) + noise.shape[1:], jnp.bfloat16),
            pltpu.VMEM((block,) + fourier_shape[1:], jnp.bfloat16),
            pltpu.SemaphoreType.DMA((3,)),
        ],
        input_output_aliases={5: 0, 6: 1},
        compiler_params=pltpu.CompilerParams(vmem_limit_bytes=VMEM_BYTES),
        cost_estimate=pl.CostEstimate(
            flops=8 * all_rows * truncation * latitudes,
            bytes_accessed=2 * all_rows * (2 * truncation + 2 * latitudes) + 4 * even.size,
            transcendentals=0,
        ),
        name="last",
    )(waves, received, *in_hbm(noise), *in_vmem(even, odd), *in_hbm(*outs))


def finish_transform(waves, first, block, received, noise, even, odd, outs):
    slots_all, mem_local, parts, fields, truncation = noise.shape
    latitudes = even.shape[1]
    groups, all_rows, lat_local = received.shape
    per_slot = mem_local * parts * fields
    at = first // block
    far = lambda step, w: (at + step, 0, 0, 0, 0)
    table = pl.BlockSpec(even.shape, lambda step, w: (0, 0))
    noise_block = pl.BlockSpec((block,) + noise.shape[1:], far)
    fourier_shape = noise.shape[:4] + (latitudes,)
    fourier_block = pl.BlockSpec((block,) + fourier_shape[1:], far)
    received_block = pl.BlockSpec(
        (groups, block * per_slot, lat_local), lambda step, w: (0, step, 0)
    )
    return pl.pallas_call(
        functools.partial(finish_kernel, first, block),
        grid_spec=pltpu.PrefetchScalarGridSpec(
            num_scalar_prefetch=1,
            grid=(all_rows // (block * per_slot),),
            in_specs=[received_block, noise_block, table, table]
            + [pl.BlockSpec(memory_space=pl.ANY)] * 2,
            out_specs=[noise_block, fourier_block],
        ),
        out_shape=[
            jax.ShapeDtypeStruct(noise.shape, jnp.bfloat16),
            jax.ShapeDtypeStruct(fourier_shape, jnp.bfloat16),
        ],
        input_output_aliases={5: 0, 6: 1},
        compiler_params=pltpu.CompilerParams(vmem_limit_bytes=VMEM_BYTES),
        cost_estimate=pl.CostEstimate(
            flops=8 * all_rows * truncation * latitudes,
            bytes_accessed=2 * all_rows * (2 * truncation + 2 * latitudes) + 4 * even.size,
            transcendentals=0,
        ),
        name="finish",
    )(waves, *in_hbm(received, noise), *in_vmem(even, odd), *in_hbm(*outs))


def chunk_bounds(slots_here, block):
    blocks = slots_here // block
    edges = [0, (blocks * 5 + 10) // 11, (blocks * 10 + 10) // 11, blocks]
    edges = [edge * block for edge in edges]
    return [(start, stop) for start, stop in zip(edges[:-1], edges[1:]) if stop > start]


def per_device(velocity, tracer, wave_slots, parents, noise):
    lat_count = lax.axis_size("lat")
    lat_index = lax.axis_index("lat")
    mem_count = lax.axis_size("member")
    group_index = lax.axis_index("member")
    mem_local, fields, lat_local, longitudes = velocity.shape
    slots_here, truncation = noise.shape[0], noise.shape[-1]
    block = math.gcd(slots_here, 8)
    per_member = 2 * fields
    per_slot = mem_local * per_member
    latitudes = lat_count * lat_local
    own_waves = lax.dynamic_slice_in_dim(wave_slots, lat_index * slots_here, slots_here)
    first_member = group_index * mem_local
    own_parents = lax.dynamic_slice_in_dim(parents, first_member, mem_local)
    offsets = own_parents - first_member + SPREAD
    upward = [(i, i + 1) for i in range(mem_count - 1)]
    downward = [(target, source) for source, target in upward]
    slot_grid = wave_slots.reshape(lat_count, slots_here)
    bounds = chunk_bounds(slots_here, block)
    inner = min(lat_local, LANES)
    starts = jnp.arange(latitudes // inner, dtype=jnp.int32) * inner

    def zonal(at):
        start, stop = bounds[at]
        waves = slot_grid[:, start:stop].reshape(-1, 1)
        return zonal_transform(waves, truncation, velocity, tracer, [])

    def neighbours(rows, per_member):
        low = lax.ppermute(rows[:, rows.shape[1] - SPREAD * per_member :], "member", upward)
        high = lax.ppermute(rows[:, : SPREAD * per_member], "member", downward)
        return low, rows, high

    def exchanged(outgoing):
        outgoing = outgoing.reshape(lat_count, -1, lat_local)
        moved = lax.all_to_all(outgoing, "lat", split_axis=0, concat_axis=0, tiled=True)
        if lat_local % LANES != 0:
            moved = jnp.swapaxes(moved, 0, 1).reshape(1, -1, latitudes)
        return moved

    received = exchanged(zonal(0))
    even, odd, made = meridional_tables(truncation, latitudes, starts, inner)
    sides = [neighbours(zonal(at), per_member) for at in range(1, len(bounds))]
    tokens = [made] + [part for low, _, high in sides[1:] for part in (low, high)]
    later = [exchanged(copy_parents(offsets, *side, tokens)) for side in sides[:1]]
    spectra, _ = forward_transform(
        (own_waves, per_member), 0, block, received, even, odd, mem_local, []
    )
    *outs, token = inverse_transform(
        own_waves, offsets, 0, block, *neighbours(spectra, 1), noise, even, odd, None
    )
    later += [exchanged(copy_parents(offsets, *side, [token])) for side in sides[1:]]
    for (start, stop), received in zip(bounds[1:], later):
        if stop - start == block:
            outs = last_transform(own_waves, start, received, noise, even, odd, outs)
        else:
            outs = finish_transform(own_waves, start, block, received, noise, even, odd, outs)
    return tuple(outs)


def solution(mesh):
    in_specs = (
        P("member", None, "lat", None),
        P("member", None, "lat", None),
        P(),
        P(),
        P("lat", "member", None, None, None),
    )
    out_specs = (P("lat", "member", None, None, None), P("lat", "member", None, None, None))
    return jax.shard_map(
        per_device, mesh=mesh, in_specs=in_specs, out_specs=out_specs, check_vma=False
    )
```

```python
import functools
import math

import jax
import jax.numpy as jnp
from jax import lax
from jax.experimental import pallas as pl
from jax.experimental.pallas import tpu as pltpu
from jax.sharding import PartitionSpec as P

SPREAD = 2
VMEM_BYTES = 24 * 1024 * 1024
ZONAL_BYTES = 44 * 1024 * 1024
LANES = 128
SUBLANES = 8
TOKEN = (8, 128)


def in_hbm(*arrays):
    return [pltpu.with_memory_space_constraint(array, pltpu.HBM) for array in arrays]


def in_vmem(*arrays):
    return [pltpu.with_memory_space_constraint(array, pltpu.VMEM) for array in arrays]


def meridional_factors(truncation, latitudes, starts, width):
    degree = jnp.arange(truncation, dtype=jnp.int32)

    def angles(points):
        phase = degree[:, None] * points[None, :] % (4 * latitudes)
        return phase.astype(jnp.float32) * (math.pi / (2 * latitudes))

    coarse = angles(2 * starts)
    fine = angles(2 * jnp.arange(width, dtype=jnp.int32) + 1)
    factor = math.sqrt(2.0 / latitudes)
    return jnp.cos(coarse) * factor, jnp.sin(coarse) * factor, jnp.cos(fine), jnp.sin(fine)


def tables_kernel(cos_c, sin_c, cos_f, sin_f, even, odd):
    width = cos_f.shape[1]
    cos_b, sin_b = cos_f[...], sin_f[...]
    for at in range(cos_c.shape[1]):
        cos_a, sin_a = cos_c[:, at : at + 1], sin_c[:, at : at + 1]
        columns = slice(at * width, (at + 1) * width)
        even[:, columns] = (cos_a * cos_b - sin_a * sin_b).astype(even.dtype)
        odd[:, columns] = (sin_a * cos_b + cos_a * sin_b).astype(odd.dtype)


def meridional_tables(truncation, latitudes, starts, width):
    factors = meridional_factors(truncation, latitudes, starts, width)
    shape = pltpu.VMEM((truncation, starts.shape[0] * width), jnp.bfloat16)
    return pl.pallas_call(
        tables_kernel,
        out_shape=[shape, shape],
        compiler_params=pltpu.CompilerParams(vmem_limit_bytes=VMEM_BYTES),
        cost_estimate=pl.CostEstimate(
            flops=6 * truncation * latitudes, bytes_accessed=4 * truncation * latitudes,
            transcendentals=0,
        ),
        name="tables",
    )(*factors)


def zonal_kernel(truncation, tokens, waves, velocity, tracer, *rest):
    out, table, total, turned, velocity_here, tracer_here, sems, out_sems = rest[tokens:]
    members, fields, lat_local, longitudes = velocity.shape
    rows = waves.shape[0]
    groups = velocity_here.shape[0]
    step_fields = velocity_here.shape[1]
    steps = fields // step_fields

    def copies(step):
        part = (step // steps, pl.ds(step % steps * step_fields, step_fields))
        return [
            pltpu.make_async_copy(source.at[part], target.at[step], sems.at[step, at])
            for at, (source, target) in enumerate(
                ((velocity, velocity_here), (tracer, tracer_here))
            )
        ]

    for step in range(groups):
        for copy in copies(step):
            copy.start()

    wave = waves[...]
    weight = jnp.where(wave < truncation, 1.0 / math.sqrt(longitudes), 0.0)

    def cos_sin(count, stride):
        points = lax.broadcasted_iota(jnp.int32, (rows, count), 1) * stride
        phase = lax.rem(wave * points, jnp.full((), longitudes, jnp.int32))
        quarter = longitudes // 4
        turns = lax.div(phase + quarter // 2, jnp.full((), quarter, jnp.int32))
        angle = (phase - turns * quarter).astype(jnp.float32) * (2.0 * math.pi / longitudes)
        square = angle * angle
        cos, sin = 1.0 / 40320, -1.0 / 5040
        for power in (6, 4, 2, 0):
            sign = -1.0 if power % 4 else 1.0
            cos = cos * square + sign / math.factorial(power)
        for power in (5, 3, 1):
            sign = -1.0 if power % 4 == 3 else 1.0
            sin = sin * square + sign / math.factorial(power)
        sin = sin * angle
        swap = turns % 2 == 1
        cos, sin = jnp.where(swap, sin, cos), jnp.where(swap, cos, sin)
        cos = jnp.where((turns == 1) | (turns == 2), -cos, cos)
        sin = jnp.where((turns == 2) | (turns == 3), -sin, sin)
        return cos, sin

    (cos_c, sin_c), (cos_f, sin_f) = cos_sin(longitudes // LANES, LANES), cos_sin(LANES, 1)
    cos_c, sin_c = cos_c * weight, sin_c * weight
    for at in range(longitudes // LANES):
        cos_a, sin_a = cos_c[:, at : at + 1], sin_c[:, at : at + 1]
        columns = slice(at * LANES, (at + 1) * LANES)
        table[:rows, columns] = (cos_a * cos_f - sin_a * sin_f).astype(table.dtype)
        table[rows:, columns] = (-sin_a * cos_f - cos_a * sin_f).astype(table.dtype)

    def body(step, carry):
        for copy in copies(step):
            copy.wait()
        product = velocity_here[step].astype(jnp.float32) * tracer_here[step].astype(jnp.float32)
        product = product.astype(jnp.bfloat16).reshape(step_fields * lat_local, longitudes)
        sums = lax.dot_general(
            table[...], product, (((1,), (1,)), ((), ())), preferred_element_type=jnp.float32
        )
        first = step // steps * 2 * fields + step % steps * step_fields
        for part in range(2):
            for field in range(step_fields):
                block = sums[
                    part * rows : (part + 1) * rows, field * lat_local : (field + 1) * lat_local
                ]
                total[:, first + part * fields + field] = block.reshape(
                    rows // SUBLANES, SUBLANES, lat_local
                )
        return carry

    lax.fori_loop(0, groups, body, 0)

    tiles = rows // SUBLANES
    batch = math.gcd(tiles, 4)

    def leave(at):
        part = pl.ds(pl.multiple_of(at * batch * SUBLANES, SUBLANES), batch * SUBLANES)
        return pltpu.make_async_copy(turned.at[part], out.at[part], out_sems.at[at])

    def turn(at, carry):
        for tile in range(batch):
            first = pl.multiple_of((at * batch + tile) * SUBLANES, SUBLANES)
            tiles_here = jnp.swapaxes(total[at * batch + tile], 0, 1)
            turned[pl.ds(first, SUBLANES)] = tiles_here.astype(out.dtype)
        leave(at).start()
        return carry

    def end(at, carry):
        leave(at).wait()
        return carry

    lax.fori_loop(0, tiles // batch, turn, 0)
    lax.fori_loop(0, tiles // batch, end, 0)


def zonal_transform(waves, truncation, velocity, tracer, tokens):
    mem_local, fields, lat_local, longitudes = velocity.shape
    rows = waves.shape[0]
    fields_step = min(fields, max(1, 512 // lat_local))
    groups = mem_local * (fields // fields_step)
    out_rows = mem_local * 2 * fields
    grid_part = pltpu.VMEM((groups, fields_step, lat_local, longitudes), velocity.dtype)
    flops = 2 * 2 * rows * longitudes * mem_local * fields * lat_local
    moved = 2 * velocity.size * 2 + rows * out_rows * lat_local * 2
    return pl.pallas_call(
        functools.partial(zonal_kernel, truncation, len(tokens)),
        in_specs=[pl.BlockSpec(memory_space=pltpu.VMEM)]
        + [pl.BlockSpec(memory_space=pl.ANY)] * (2 + len(tokens)),
        out_specs=pl.BlockSpec(memory_space=pl.ANY),
        out_shape=pltpu.HBM((rows, out_rows, lat_local), jnp.bfloat16),
        scratch_shapes=[
            pltpu.VMEM((2 * rows, longitudes), jnp.bfloat16),
            pltpu.VMEM((rows // SUBLANES, out_rows, SUBLANES, lat_local), jnp.float32),
            pltpu.VMEM((rows, out_rows, lat_local), jnp.bfloat16),
            grid_part,
            grid_part,
            pltpu.SemaphoreType.DMA((groups, 2)),
            pltpu.SemaphoreType.DMA((rows // SUBLANES,)),
        ],
        compiler_params=pltpu.CompilerParams(vmem_limit_bytes=ZONAL_BYTES),
        cost_estimate=pl.CostEstimate(flops=flops, bytes_accessed=moved, transcendentals=0),
        name="zonal",
    )(waves, *in_hbm(velocity, tracer), *tokens)


def forward_kernel(first, block, waves, received, even, odd, *rest):
    out, token = rest[-2:]
    truncation = even.shape[0]
    step = pl.program_id(0)
    per_slot = received.shape[1] // block
    rows = jnp.concatenate([received[g] for g in range(received.shape[0])], axis=-1)
    contract = (((1,), (1,)), ((), ()))
    by_even = lax.dot_general(rows, even[...], contract, preferred_element_type=jnp.float32)
    by_odd = lax.dot_general(rows, odd[...], contract, preferred_element_type=jnp.float32)
    degree = lax.broadcasted_iota(jnp.int32, (per_slot, truncation), 1)
    for slot in range(block):
        wave = waves[first + step * block + slot]
        least = jnp.where(wave < truncation, wave, truncation)
        here = slice(slot * per_slot, (slot + 1) * per_slot)
        chosen = jnp.where(wave % 2 == 1, by_odd[here], by_even[here])
        chosen = jnp.where(degree >= least, chosen, 0.0)
        out[slot] = chosen.astype(out.dtype).reshape(out.shape[1:])
    token[...] = jnp.zeros_like(token)


def forward_transform(waves, first, block, received, even, odd, mem_local, tokens):
    groups, all_rows, lat_local = received.shape
    truncation, latitudes = even.shape
    slots = all_rows // (waves[1] * mem_local)
    out_shape = (slots, mem_local, waves[1], truncation)
    per_block = block * mem_local * waves[1]
    table = pl.BlockSpec(even.shape, lambda step, w: (0, 0))
    return pl.pallas_call(
        functools.partial(forward_kernel, first, block),
        grid_spec=pltpu.PrefetchScalarGridSpec(
            num_scalar_prefetch=1,
            grid=(slots // block,),
            in_specs=[
                pl.BlockSpec((groups, per_block, lat_local), lambda step, w: (0, step, 0)),
                table,
                table,
            ]
            + [pl.BlockSpec(memory_space=pl.ANY)] * len(tokens),
            out_specs=[
                pl.BlockSpec((block,) + out_shape[1:], lambda step, w: (step, 0, 0, 0)),
                pl.BlockSpec(TOKEN, lambda step, w: (0, 0)),
            ],
        ),
        out_shape=[
            pltpu.HBM(out_shape, jnp.bfloat16),
            jax.ShapeDtypeStruct(TOKEN, jnp.float32),
        ],
        compiler_params=pltpu.CompilerParams(vmem_limit_bytes=VMEM_BYTES),
        cost_estimate=pl.CostEstimate(
            flops=4 * all_rows * truncation * latitudes,
            bytes_accessed=2 * (all_rows * latitudes + 2 * even.size + all_rows * truncation),
            transcendentals=0,
        ),
        name="forward",
    )(waves[0], *in_hbm(received), *in_vmem(even, odd), *tokens)


def inverse_kernel(first, block, waves, offsets, low, own, high, noise, even, odd, *rest):
    spectra_out, fourier_out, token = rest[-3:]
    token[...] = jnp.zeros_like(token)
    truncation, latitudes = even.shape
    step = pl.program_id(0)
    mem_local, parts, fields = noise.shape[1:4]
    degree = lax.broadcasted_iota(jnp.int32, (fields, truncation), 1)
    sources = [low[:, m] for m in range(low.shape[1])]
    sources += [own[:, m] for m in range(own.shape[1])]
    sources += [high[:, m] for m in range(high.shape[1])]
    even_rows, odd_rows = [], []
    parents = []
    for child in range(mem_local):
        parent = sources[0]
        for at in range(1, len(sources)):
            parent = jnp.where(offsets[child] == at, sources[at], parent)
        parents.append(parent)
    for slot in range(block):
        wave = waves[first + step * block + slot]
        least = jnp.where(wave < truncation, wave, truncation)
        is_odd = wave % 2 == 1
        active = degree >= least
        for child in range(mem_local):
            parent = parents[child][slot].astype(jnp.float32)
            parent = parent.reshape(parts, fields, truncation)
            added = jnp.where(active[None], noise[slot, child].astype(jnp.float32), 0.0)
            total = parent + added
            spectra_out[slot, child] = total.astype(spectra_out.dtype)
            rows = total.reshape(parts * fields, truncation)
            even_rows.append(jnp.where(is_odd, 0.0, rows).astype(jnp.bfloat16))
            odd_rows.append(jnp.where(is_odd, rows, 0.0).astype(jnp.bfloat16))
    result = jnp.dot(
        jnp.concatenate(even_rows, axis=0), even[...], preferred_element_type=jnp.float32
    )
    result += jnp.dot(
        jnp.concatenate(odd_rows, axis=0), odd[...], preferred_element_type=jnp.float32
    )
    fourier_out[...] = result.reshape(fourier_out.shape).astype(fourier_out.dtype)


def inverse_transform(waves, offsets, first, block, low, own, high, noise, even, odd, outs):
    slots_all, mem_local, parts, fields, truncation = noise.shape
    latitudes = even.shape[1]
    slots = own.shape[0]
    at = first // block
    near = lambda step, w, o: (step, 0, 0, 0)
    far = lambda step, w, o: (at + step, 0, 0, 0, 0)
    table = pl.BlockSpec(even.shape, lambda step, w, o: (0, 0))
    noise_block = pl.BlockSpec((block,) + noise.shape[1:], far)
    fourier_shape = noise.shape[:4] + (latitudes,)
    fourier_block = pl.BlockSpec((block,) + fourier_shape[1:], far)
    operands = [low, *in_hbm(own), high, *in_hbm(noise), *in_vmem(even, odd)]
    in_specs = [pl.BlockSpec((block,) + a.shape[1:], near) for a in operands[:3]]
    in_specs += [noise_block, table, table]
    aliases = {}
    if outs is not None:
        aliases = {8: 0, 9: 1}
        operands += in_hbm(*outs)
        in_specs += [pl.BlockSpec(memory_space=pl.ANY)] * 2
    rows = slots * mem_local * parts * fields
    return pl.pallas_call(
        functools.partial(inverse_kernel, first, block),
        grid_spec=pltpu.PrefetchScalarGridSpec(
            num_scalar_prefetch=2,
            grid=(slots // block,),
            in_specs=in_specs,
            out_specs=[
                noise_block,
                fourier_block,
                pl.BlockSpec(TOKEN, lambda step, w, o: (0, 0)),
            ],
        ),
        out_shape=[
            jax.ShapeDtypeStruct(noise.shape, jnp.bfloat16),
            jax.ShapeDtypeStruct(fourier_shape, jnp.bfloat16),
            jax.ShapeDtypeStruct(TOKEN, jnp.float32),
        ],
        input_output_aliases=aliases,
        compiler_params=pltpu.CompilerParams(vmem_limit_bytes=VMEM_BYTES),
        cost_estimate=pl.CostEstimate(
            flops=4 * rows * truncation * latitudes,
            bytes_accessed=2 * rows * (5 * truncation + latitudes) + 4 * even.size,
            transcendentals=0,
        ),
        name="inverse",
    )(waves, offsets, *operands)


def copy_kernel(offsets, low, own, high, *rest):
    out = rest[-1]
    rows = out.shape[1] // offsets.shape[0]
    for child in range(offsets.shape[0]):
        index, chosen = 0, None
        for source in (low, own, high):
            for at in range(source.shape[1] // rows):
                value = source[:, at * rows : (at + 1) * rows]
                chosen = value if index == 0 else jnp.where(offsets[child] == index, value, chosen)
                index += 1
        out[:, child * rows : (child + 1) * rows] = chosen


def copy_parents(offsets, low, own, high, tokens):
    steps = math.gcd(own.shape[0], 4)
    block = lambda array: pl.BlockSpec(
        (array.shape[0] // steps,) + array.shape[1:], lambda step, o: (step, 0, 0)
    )
    return pl.pallas_call(
        copy_kernel,
        grid_spec=pltpu.PrefetchScalarGridSpec(
            num_scalar_prefetch=1,
            grid=(steps,),
            in_specs=[block(low), block(own), block(high)]
            + [pl.BlockSpec(memory_space=pl.ANY)] * len(tokens),
            out_specs=block(own),
        ),
        out_shape=pltpu.HBM(own.shape, own.dtype),
        compiler_params=pltpu.CompilerParams(vmem_limit_bytes=VMEM_BYTES),
        cost_estimate=pl.CostEstimate(flops=0, bytes_accessed=8 * own.size, transcendentals=0),
        name="parents",
    )(offsets, low, *in_hbm(own), high, *tokens)


def finish_block(first, waves, received, noise, even, odd, spectra_out, fourier_out, ready, store, cuts):
    truncation = even.shape[0]
    block, mem_local, parts, fields = noise.shape[:4]
    per_slot = received.shape[1] // block
    rows = jnp.concatenate([received[g] for g in range(received.shape[0])], axis=-1)
    contract = (((1,), (1,)), ((), ()))
    by_even = lax.dot_general(rows, even[...], contract, preferred_element_type=jnp.float32)
    by_odd = lax.dot_general(rows, odd[...], contract, preferred_element_type=jnp.float32)
    degree = lax.broadcasted_iota(jnp.int32, (per_slot, truncation), 1)
    even_rows, odd_rows = [], []
    ready()
    for slot in range(block):
        wave = waves[first + slot]
        least = jnp.where(wave < truncation, wave, truncation)
        is_odd = wave % 2 == 1
        active = degree >= least
        here = slice(slot * per_slot, (slot + 1) * per_slot)
        spectra = jnp.where(is_odd, by_odd[here], by_even[here])
        spectra = spectra.astype(jnp.bfloat16).astype(jnp.float32)
        added = noise[slot].astype(jnp.float32).reshape(per_slot, truncation)
        child = jnp.where(active, spectra + added, 0.0)
        spectra_out[slot] = child.reshape(noise.shape[1:]).astype(spectra_out.dtype)
        even_rows.append(jnp.where(is_odd, 0.0, child).astype(jnp.bfloat16))
        odd_rows.append(jnp.where(is_odd, child, 0.0).astype(jnp.bfloat16))
    store()
    even_rows, odd_rows = jnp.concatenate(even_rows, axis=0), jnp.concatenate(odd_rows, axis=0)
    for columns, leave in cuts:
        result = jnp.dot(even_rows, even[:, columns], preferred_element_type=jnp.float32)
        result += jnp.dot(odd_rows, odd[:, columns], preferred_element_type=jnp.float32)
        shape = fourier_out.shape[:-1] + (result.shape[1],)
        fourier_out[..., columns] = result.reshape(shape).astype(fourier_out.dtype)
        leave()


def finish_kernel(first, block, waves, received, noise, even, odd, *rest):
    start = first + pl.program_id(0) * block
    nothing = lambda: None
    cuts = [(slice(0, even.shape[1]), nothing)]
    finish_block(start, waves, received, noise, even, odd, *rest[-2:], nothing, nothing, cuts)


def last_kernel(first, waves, received, noise, even, odd, *rest):
    spectra_out, fourier_out, noise_here, spectra_here, fourier_here, sems = rest[-6:]
    part = pl.ds(first, noise_here.shape[0])
    fetch = pltpu.make_async_copy(noise.at[part], noise_here, sems.at[0])
    leave = pltpu.make_async_copy(spectra_here, spectra_out.at[part], sems.at[1])
    width = even.shape[1] // 2
    cuts = [slice(0, width), slice(width, 2 * width)]
    halves = [
        pltpu.make_async_copy(
            fourier_here.at[:, :, :, :, pl.ds(at * width, width)],
            fourier_out.at[part, :, :, :, pl.ds(at * width, width)],
            sems.at[2 + at],
        )
        for at in range(2)
    ]
    fetch.start()
    finish_block(
        first,
        waves,
        received,
        noise_here,
        even,
        odd,
        spectra_here,
        fourier_here,
        fetch.wait,
        leave.start,
        [(columns, half.start) for columns, half in zip(cuts, halves)],
    )
    leave.wait()
    for half in halves:
        half.wait()


def last_transform(waves, first, received, noise, even, odd, outs):
    slots_all, mem_local, parts, fields, truncation = noise.shape
    latitudes = even.shape[1]
    all_rows = received.shape[1]
    block = all_rows // (mem_local * parts * fields)
    fourier_shape = noise.shape[:4] + (latitudes,)
    here = pl.BlockSpec(memory_space=pltpu.VMEM)
    anywhere = pl.BlockSpec(memory_space=pl.ANY)
    return pl.pallas_call(
        functools.partial(last_kernel, first),
        in_specs=[pl.BlockSpec(memory_space=pltpu.SMEM), here, anywhere, here, here]
        + [anywhere] * 2,
        out_specs=[anywhere, anywhere],
        out_shape=[
            jax.ShapeDtypeStruct(noise.shape, jnp.bfloat16),
            jax.ShapeDtypeStruct(fourier_shape, jnp.bfloat16),
        ],
        scratch_shapes=[
            pltpu.VMEM((block,) + noise.shape[1:], jnp.bfloat16),
            pltpu.VMEM((block,) + noise.shape[1:], jnp.bfloat16),
            pltpu.VMEM((block,) + fourier_shape[1:], jnp.bfloat16),
            pltpu.SemaphoreType.DMA((4,)),
        ],
        input_output_aliases={5: 0, 6: 1},
        compiler_params=pltpu.CompilerParams(vmem_limit_bytes=VMEM_BYTES),
        cost_estimate=pl.CostEstimate(
            flops=8 * all_rows * truncation * latitudes,
            bytes_accessed=2 * all_rows * (2 * truncation + 2 * latitudes) + 4 * even.size,
            transcendentals=0,
        ),
        name="last",
    )(waves, received, *in_hbm(noise), *in_vmem(even, odd), *in_hbm(*outs))


def finish_transform(waves, first, block, received, noise, even, odd, outs):
    slots_all, mem_local, parts, fields, truncation = noise.shape
    latitudes = even.shape[1]
    groups, all_rows, lat_local = received.shape
    per_slot = mem_local * parts * fields
    at = first // block
    far = lambda step, w: (at + step, 0, 0, 0, 0)
    table = pl.BlockSpec(even.shape, lambda step, w: (0, 0))
    noise_block = pl.BlockSpec((block,) + noise.shape[1:], far)
    fourier_shape = noise.shape[:4] + (latitudes,)
    fourier_block = pl.BlockSpec((block,) + fourier_shape[1:], far)
    received_block = pl.BlockSpec(
        (groups, block * per_slot, lat_local), lambda step, w: (0, step, 0)
    )
    return pl.pallas_call(
        functools.partial(finish_kernel, first, block),
        grid_spec=pltpu.PrefetchScalarGridSpec(
            num_scalar_prefetch=1,
            grid=(all_rows // (block * per_slot),),
            in_specs=[received_block, noise_block, table, table]
            + [pl.BlockSpec(memory_space=pl.ANY)] * 2,
            out_specs=[noise_block, fourier_block],
        ),
        out_shape=[
            jax.ShapeDtypeStruct(noise.shape, jnp.bfloat16),
            jax.ShapeDtypeStruct(fourier_shape, jnp.bfloat16),
        ],
        input_output_aliases={5: 0, 6: 1},
        compiler_params=pltpu.CompilerParams(vmem_limit_bytes=VMEM_BYTES),
        cost_estimate=pl.CostEstimate(
            flops=8 * all_rows * truncation * latitudes,
            bytes_accessed=2 * all_rows * (2 * truncation + 2 * latitudes) + 4 * even.size,
            transcendentals=0,
        ),
        name="finish",
    )(waves, *in_hbm(received, noise), *in_vmem(even, odd), *in_hbm(*outs))


def chunk_bounds(slots_here, block):
    blocks = slots_here // block
    edges = [0, (blocks * 5 + 10) // 11, (blocks * 10 + 10) // 11, blocks]
    edges = [edge * block for edge in edges]
    return [(start, stop) for start, stop in zip(edges[:-1], edges[1:]) if stop > start]


def per_device(velocity, tracer, wave_slots, parents, noise):
    lat_count = lax.axis_size("lat")
    lat_index = lax.axis_index("lat")
    mem_count = lax.axis_size("member")
    group_index = lax.axis_index("member")
    mem_local, fields, lat_local, longitudes = velocity.shape
    slots_here, truncation = noise.shape[0], noise.shape[-1]
    block = math.gcd(slots_here, 8)
    per_member = 2 * fields
    per_slot = mem_local * per_member
    latitudes = lat_count * lat_local
    own_waves = lax.dynamic_slice_in_dim(wave_slots, lat_index * slots_here, slots_here)
    first_member = group_index * mem_local
    own_parents = lax.dynamic_slice_in_dim(parents, first_member, mem_local)
    offsets = own_parents - first_member + SPREAD
    upward = [(i, i + 1) for i in range(mem_count - 1)]
    downward = [(target, source) for source, target in upward]
    slot_grid = wave_slots.reshape(lat_count, slots_here)
    bounds = chunk_bounds(slots_here, block)
    inner = min(lat_local, LANES)
    starts = jnp.arange(latitudes // inner, dtype=jnp.int32) * inner

    def zonal(at):
        start, stop = bounds[at]
        waves = slot_grid[:, start:stop].reshape(-1, 1)
        return zonal_transform(waves, truncation, velocity, tracer, [])

    def neighbours(rows, per_member):
        low = lax.ppermute(rows[:, rows.shape[1] - SPREAD * per_member :], "member", upward)
        high = lax.ppermute(rows[:, : SPREAD * per_member], "member", downward)
        return low, rows, high

    def exchanged(outgoing):
        outgoing = outgoing.reshape(lat_count, -1, lat_local)
        moved = lax.all_to_all(outgoing, "lat", split_axis=0, concat_axis=0, tiled=True)
        if lat_local % LANES != 0:
            moved = jnp.swapaxes(moved, 0, 1).reshape(1, -1, latitudes)
        return moved

    def copied(at, tokens):
        return copy_parents(offsets, *neighbours(zonal(at), per_member), tokens)

    received = exchanged(zonal(0))
    even, odd = meridional_tables(truncation, latitudes, starts, inner)
    later = [exchanged(copied(1, []))] if len(bounds) > 1 else []
    spectra, _ = forward_transform(
        (own_waves, per_member), 0, block, received, even, odd, mem_local, []
    )
    *outs, token = inverse_transform(
        own_waves, offsets, 0, block, *neighbours(spectra, 1), noise, even, odd, None
    )
    later += [exchanged(copied(at, [token])) for at in range(2, len(bounds))]
    for (start, stop), received in zip(bounds[1:], later):
        if stop - start == block:
            outs = last_transform(own_waves, start, received, noise, even, odd, outs)
        else:
            outs = finish_transform(own_waves, start, block, received, noise, even, odd, outs)
    return tuple(outs)


def solution(mesh):
    in_specs = (
        P("member", None, "lat", None),
        P("member", None, "lat", None),
        P(),
        P(),
        P("lat", "member", None, None, None),
    )
    out_specs = (P("lat", "member", None, None, None), P("lat", "member", None, None, None))
    return jax.shard_map(
        per_device, mesh=mesh, in_specs=in_specs, out_specs=out_specs, check_vma=False
    )
```

```python
import functools
import math

import jax
import jax.numpy as jnp
from jax import lax
from jax.experimental import pallas as pl
from jax.experimental.pallas import tpu as pltpu
from jax.sharding import PartitionSpec as P

SPREAD = 2
VMEM_BYTES = 24 * 1024 * 1024
ZONAL_BYTES = 44 * 1024 * 1024
LANES = 128
SUBLANES = 8
TOKEN = (8, 128)


def in_hbm(*arrays):
    return [pltpu.with_memory_space_constraint(array, pltpu.HBM) for array in arrays]


def in_vmem(*arrays):
    return [pltpu.with_memory_space_constraint(array, pltpu.VMEM) for array in arrays]


def meridional_factors(truncation, latitudes, starts, width):
    degree = jnp.arange(truncation, dtype=jnp.int32)

    def angles(points):
        phase = degree[:, None] * points[None, :] % (4 * latitudes)
        return phase.astype(jnp.float32) * (math.pi / (2 * latitudes))

    coarse = angles(2 * starts)
    fine = angles(2 * jnp.arange(width, dtype=jnp.int32) + 1)
    factor = math.sqrt(2.0 / latitudes)
    return jnp.cos(coarse) * factor, jnp.sin(coarse) * factor, jnp.cos(fine), jnp.sin(fine)


def tables_kernel(cos_c, sin_c, cos_f, sin_f, even, odd):
    width = cos_f.shape[1]
    cos_b, sin_b = cos_f[...], sin_f[...]
    for at in range(cos_c.shape[1]):
        cos_a, sin_a = cos_c[:, at : at + 1], sin_c[:, at : at + 1]
        columns = slice(at * width, (at + 1) * width)
        even[:, columns] = (cos_a * cos_b - sin_a * sin_b).astype(even.dtype)
        odd[:, columns] = (sin_a * cos_b + cos_a * sin_b).astype(odd.dtype)


def meridional_tables(truncation, latitudes, starts, width):
    factors = meridional_factors(truncation, latitudes, starts, width)
    shape = pltpu.VMEM((truncation, starts.shape[0] * width), jnp.bfloat16)
    return pl.pallas_call(
        tables_kernel,
        out_shape=[shape, shape],
        compiler_params=pltpu.CompilerParams(vmem_limit_bytes=VMEM_BYTES),
        cost_estimate=pl.CostEstimate(
            flops=6 * truncation * latitudes, bytes_accessed=4 * truncation * latitudes,
            transcendentals=0,
        ),
        name="tables",
    )(*factors)


def zonal_kernel(truncation, tokens, waves, velocity, tracer, *rest):
    out, table, total, turned, velocity_here, tracer_here, sems, out_sems = rest[tokens:]
    members, fields, lat_local, longitudes = velocity.shape
    rows = waves.shape[0]
    groups = velocity_here.shape[0]
    step_fields = velocity_here.shape[1]
    steps = fields // step_fields

    def copies(step):
        part = (step // steps, pl.ds(step % steps * step_fields, step_fields))
        return [
            pltpu.make_async_copy(source.at[part], target.at[step], sems.at[step, at])
            for at, (source, target) in enumerate(
                ((velocity, velocity_here), (tracer, tracer_here))
            )
        ]

    for step in range(groups):
        for copy in copies(step):
            copy.start()

    wave = waves[...]
    weight = jnp.where(wave < truncation, 1.0 / math.sqrt(longitudes), 0.0)

    def cos_sin(count, stride):
        points = lax.broadcasted_iota(jnp.int32, (rows, count), 1) * stride
        phase = lax.rem(wave * points, jnp.full((), longitudes, jnp.int32))
        quarter = longitudes // 4
        turns = lax.div(phase + quarter // 2, jnp.full((), quarter, jnp.int32))
        angle = (phase - turns * quarter).astype(jnp.float32) * (2.0 * math.pi / longitudes)
        square = angle * angle
        cos, sin = 1.0 / 40320, -1.0 / 5040
        for power in (6, 4, 2, 0):
            sign = -1.0 if power % 4 else 1.0
            cos = cos * square + sign / math.factorial(power)
        for power in (5, 3, 1):
            sign = -1.0 if power % 4 == 3 else 1.0
            sin = sin * square + sign / math.factorial(power)
        sin = sin * angle
        swap = turns % 2 == 1
        cos, sin = jnp.where(swap, sin, cos), jnp.where(swap, cos, sin)
        cos = jnp.where((turns == 1) | (turns == 2), -cos, cos)
        sin = jnp.where((turns == 2) | (turns == 3), -sin, sin)
        return cos, sin

    (cos_c, sin_c), (cos_f, sin_f) = cos_sin(longitudes // LANES, LANES), cos_sin(LANES, 1)
    cos_c, sin_c = cos_c * weight, sin_c * weight
    for at in range(longitudes // LANES):
        cos_a, sin_a = cos_c[:, at : at + 1], sin_c[:, at : at + 1]
        columns = slice(at * LANES, (at + 1) * LANES)
        table[:rows, columns] = (cos_a * cos_f - sin_a * sin_f).astype(table.dtype)
        table[rows:, columns] = (-sin_a * cos_f - cos_a * sin_f).astype(table.dtype)

    def body(step, carry):
        for copy in copies(step):
            copy.wait()
        product = velocity_here[step].astype(jnp.float32) * tracer_here[step].astype(jnp.float32)
        product = product.astype(jnp.bfloat16).reshape(step_fields * lat_local, longitudes)
        sums = lax.dot_general(
            table[...], product, (((1,), (1,)), ((), ())), preferred_element_type=jnp.float32
        )
        first = step // steps * 2 * fields + step % steps * step_fields
        for part in range(2):
            for field in range(step_fields):
                block = sums[
                    part * rows : (part + 1) * rows, field * lat_local : (field + 1) * lat_local
                ]
                total[:, first + part * fields + field] = block.reshape(
                    rows // SUBLANES, SUBLANES, lat_local
                )
        return carry

    lax.fori_loop(0, groups, body, 0)

    tiles = rows // SUBLANES
    batch = math.gcd(tiles, 4)

    def leave(at):
        part = pl.ds(pl.multiple_of(at * batch * SUBLANES, SUBLANES), batch * SUBLANES)
        return pltpu.make_async_copy(turned.at[part], out.at[part], out_sems.at[at])

    def turn(at, carry):
        for tile in range(batch):
            first = pl.multiple_of((at * batch + tile) * SUBLANES, SUBLANES)
            tiles_here = jnp.swapaxes(total[at * batch + tile], 0, 1)
            turned[pl.ds(first, SUBLANES)] = tiles_here.astype(out.dtype)
        leave(at).start()
        return carry

    def end(at, carry):
        leave(at).wait()
        return carry

    lax.fori_loop(0, tiles // batch, turn, 0)
    lax.fori_loop(0, tiles // batch, end, 0)


def zonal_transform(waves, truncation, velocity, tracer, tokens):
    mem_local, fields, lat_local, longitudes = velocity.shape
    rows = waves.shape[0]
    fields_step = min(fields, max(1, 512 // lat_local))
    groups = mem_local * (fields // fields_step)
    out_rows = mem_local * 2 * fields
    grid_part = pltpu.VMEM((groups, fields_step, lat_local, longitudes), velocity.dtype)
    flops = 2 * 2 * rows * longitudes * mem_local * fields * lat_local
    moved = 2 * velocity.size * 2 + rows * out_rows * lat_local * 2
    return pl.pallas_call(
        functools.partial(zonal_kernel, truncation, len(tokens)),
        in_specs=[pl.BlockSpec(memory_space=pltpu.VMEM)]
        + [pl.BlockSpec(memory_space=pl.ANY)] * (2 + len(tokens)),
        out_specs=pl.BlockSpec(memory_space=pl.ANY),
        out_shape=pltpu.HBM((rows, out_rows, lat_local), jnp.bfloat16),
        scratch_shapes=[
            pltpu.VMEM((2 * rows, longitudes), jnp.bfloat16),
            pltpu.VMEM((rows // SUBLANES, out_rows, SUBLANES, lat_local), jnp.float32),
            pltpu.VMEM((rows, out_rows, lat_local), jnp.bfloat16),
            grid_part,
            grid_part,
            pltpu.SemaphoreType.DMA((groups, 2)),
            pltpu.SemaphoreType.DMA((rows // SUBLANES,)),
        ],
        compiler_params=pltpu.CompilerParams(vmem_limit_bytes=ZONAL_BYTES),
        cost_estimate=pl.CostEstimate(flops=flops, bytes_accessed=moved, transcendentals=0),
        name="zonal",
    )(waves, *in_hbm(velocity, tracer), *tokens)


def forward_kernel(first, block, waves, received, even, odd, *rest):
    out, token = rest[-2:]
    truncation = even.shape[0]
    step = pl.program_id(0)
    per_slot = received.shape[1] // block
    rows = jnp.concatenate([received[g] for g in range(received.shape[0])], axis=-1)
    contract = (((1,), (1,)), ((), ()))
    by_even = lax.dot_general(rows, even[...], contract, preferred_element_type=jnp.float32)
    by_odd = lax.dot_general(rows, odd[...], contract, preferred_element_type=jnp.float32)
    degree = lax.broadcasted_iota(jnp.int32, (per_slot, truncation), 1)
    for slot in range(block):
        wave = waves[first + step * block + slot]
        least = jnp.where(wave < truncation, wave, truncation)
        here = slice(slot * per_slot, (slot + 1) * per_slot)
        chosen = jnp.where(wave % 2 == 1, by_odd[here], by_even[here])
        chosen = jnp.where(degree >= least, chosen, 0.0)
        out[slot] = chosen.astype(out.dtype).reshape(out.shape[1:])
    token[...] = jnp.zeros_like(token)


def forward_transform(waves, first, block, received, even, odd, mem_local, tokens):
    groups, all_rows, lat_local = received.shape
    truncation, latitudes = even.shape
    slots = all_rows // (waves[1] * mem_local)
    out_shape = (slots, mem_local, waves[1], truncation)
    per_block = block * mem_local * waves[1]
    table = pl.BlockSpec(even.shape, lambda step, w: (0, 0))
    return pl.pallas_call(
        functools.partial(forward_kernel, first, block),
        grid_spec=pltpu.PrefetchScalarGridSpec(
            num_scalar_prefetch=1,
            grid=(slots // block,),
            in_specs=[
                pl.BlockSpec((groups, per_block, lat_local), lambda step, w: (0, step, 0)),
                table,
                table,
            ]
            + [pl.BlockSpec(memory_space=pl.ANY)] * len(tokens),
            out_specs=[
                pl.BlockSpec((block,) + out_shape[1:], lambda step, w: (step, 0, 0, 0)),
                pl.BlockSpec(TOKEN, lambda step, w: (0, 0)),
            ],
        ),
        out_shape=[
            pltpu.HBM(out_shape, jnp.bfloat16),
            jax.ShapeDtypeStruct(TOKEN, jnp.float32),
        ],
        compiler_params=pltpu.CompilerParams(vmem_limit_bytes=VMEM_BYTES),
        cost_estimate=pl.CostEstimate(
            flops=4 * all_rows * truncation * latitudes,
            bytes_accessed=2 * (all_rows * latitudes + 2 * even.size + all_rows * truncation),
            transcendentals=0,
        ),
        name="forward",
    )(waves[0], *in_hbm(received), *in_vmem(even, odd), *tokens)


def inverse_kernel(first, block, waves, offsets, low, own, high, noise, even, odd, *rest):
    spectra_out, fourier_out, token = rest[-3:]
    token[...] = jnp.zeros_like(token)
    truncation, latitudes = even.shape
    step = pl.program_id(0)
    mem_local, parts, fields = noise.shape[1:4]
    degree = lax.broadcasted_iota(jnp.int32, (fields, truncation), 1)
    sources = [low[:, m] for m in range(low.shape[1])]
    sources += [own[:, m] for m in range(own.shape[1])]
    sources += [high[:, m] for m in range(high.shape[1])]
    even_rows, odd_rows = [], []
    parents = []
    for child in range(mem_local):
        parent = sources[0]
        for at in range(1, len(sources)):
            parent = jnp.where(offsets[child] == at, sources[at], parent)
        parents.append(parent)
    for slot in range(block):
        wave = waves[first + step * block + slot]
        least = jnp.where(wave < truncation, wave, truncation)
        is_odd = wave % 2 == 1
        active = degree >= least
        for child in range(mem_local):
            parent = parents[child][slot].astype(jnp.float32)
            parent = parent.reshape(parts, fields, truncation)
            added = jnp.where(active[None], noise[slot, child].astype(jnp.float32), 0.0)
            total = parent + added
            spectra_out[slot, child] = total.astype(spectra_out.dtype)
            rows = total.reshape(parts * fields, truncation)
            even_rows.append(jnp.where(is_odd, 0.0, rows).astype(jnp.bfloat16))
            odd_rows.append(jnp.where(is_odd, rows, 0.0).astype(jnp.bfloat16))
    result = jnp.dot(
        jnp.concatenate(even_rows, axis=0), even[...], preferred_element_type=jnp.float32
    )
    result += jnp.dot(
        jnp.concatenate(odd_rows, axis=0), odd[...], preferred_element_type=jnp.float32
    )
    fourier_out[...] = result.reshape(fourier_out.shape).astype(fourier_out.dtype)


def inverse_transform(waves, offsets, first, block, low, own, high, noise, even, odd, outs):
    slots_all, mem_local, parts, fields, truncation = noise.shape
    latitudes = even.shape[1]
    slots = own.shape[0]
    at = first // block
    near = lambda step, w, o: (step, 0, 0, 0)
    far = lambda step, w, o: (at + step, 0, 0, 0, 0)
    table = pl.BlockSpec(even.shape, lambda step, w, o: (0, 0))
    noise_block = pl.BlockSpec((block,) + noise.shape[1:], far)
    fourier_shape = noise.shape[:4] + (latitudes,)
    fourier_block = pl.BlockSpec((block,) + fourier_shape[1:], far)
    operands = [low, *in_hbm(own), high, *in_hbm(noise), *in_vmem(even, odd)]
    in_specs = [pl.BlockSpec((block,) + a.shape[1:], near) for a in operands[:3]]
    in_specs += [noise_block, table, table]
    aliases = {}
    if outs is not None:
        aliases = {8: 0, 9: 1}
        operands += in_hbm(*outs)
        in_specs += [pl.BlockSpec(memory_space=pl.ANY)] * 2
    rows = slots * mem_local * parts * fields
    return pl.pallas_call(
        functools.partial(inverse_kernel, first, block),
        grid_spec=pltpu.PrefetchScalarGridSpec(
            num_scalar_prefetch=2,
            grid=(slots // block,),
            in_specs=in_specs,
            out_specs=[
                noise_block,
                fourier_block,
                pl.BlockSpec(TOKEN, lambda step, w, o: (0, 0)),
            ],
        ),
        out_shape=[
            jax.ShapeDtypeStruct(noise.shape, jnp.bfloat16),
            jax.ShapeDtypeStruct(fourier_shape, jnp.bfloat16),
            jax.ShapeDtypeStruct(TOKEN, jnp.float32),
        ],
        input_output_aliases=aliases,
        compiler_params=pltpu.CompilerParams(vmem_limit_bytes=VMEM_BYTES),
        cost_estimate=pl.CostEstimate(
            flops=4 * rows * truncation * latitudes,
            bytes_accessed=2 * rows * (5 * truncation + latitudes) + 4 * even.size,
            transcendentals=0,
        ),
        name="inverse",
    )(waves, offsets, *operands)


def copy_kernel(offsets, low, own, high, *rest):
    out = rest[-1]
    rows = out.shape[1] // offsets.shape[0]
    for child in range(offsets.shape[0]):
        index, chosen = 0, None
        for source in (low, own, high):
            for at in range(source.shape[1] // rows):
                value = source[:, at * rows : (at + 1) * rows]
                chosen = value if index == 0 else jnp.where(offsets[child] == index, value, chosen)
                index += 1
        out[:, child * rows : (child + 1) * rows] = chosen


def copy_parents(offsets, low, own, high, tokens):
    steps = math.gcd(own.shape[0], 8)
    block = lambda array: pl.BlockSpec(
        (array.shape[0] // steps,) + array.shape[1:], lambda step, o: (step, 0, 0)
    )
    return pl.pallas_call(
        copy_kernel,
        grid_spec=pltpu.PrefetchScalarGridSpec(
            num_scalar_prefetch=1,
            grid=(steps,),
            in_specs=[block(low), block(own), block(high)]
            + [pl.BlockSpec(memory_space=pl.ANY)] * len(tokens),
            out_specs=block(own),
        ),
        out_shape=pltpu.HBM(own.shape, own.dtype),
        compiler_params=pltpu.CompilerParams(vmem_limit_bytes=VMEM_BYTES),
        cost_estimate=pl.CostEstimate(flops=0, bytes_accessed=8 * own.size, transcendentals=0),
        name="parents",
    )(offsets, low, *in_hbm(own), high, *tokens)


def finish_block(first, waves, received, noise, even, odd, spectra_out, fourier_out, ready, store):
    truncation = even.shape[0]
    block, mem_local, parts, fields = noise.shape[:4]
    per_slot = received.shape[1] // block
    rows = jnp.concatenate([received[g] for g in range(received.shape[0])], axis=-1)
    contract = (((1,), (1,)), ((), ()))
    by_even = lax.dot_general(rows, even[...], contract, preferred_element_type=jnp.float32)
    by_odd = lax.dot_general(rows, odd[...], contract, preferred_element_type=jnp.float32)
    degree = lax.broadcasted_iota(jnp.int32, (per_slot, truncation), 1)
    even_rows, odd_rows = [], []
    ready()
    for slot in range(block):
        wave = waves[first + slot]
        least = jnp.where(wave < truncation, wave, truncation)
        is_odd = wave % 2 == 1
        active = degree >= least
        here = slice(slot * per_slot, (slot + 1) * per_slot)
        spectra = jnp.where(is_odd, by_odd[here], by_even[here])
        spectra = spectra.astype(jnp.bfloat16).astype(jnp.float32)
        added = noise[slot].astype(jnp.float32).reshape(per_slot, truncation)
        child = jnp.where(active, spectra + added, 0.0)
        spectra_out[slot] = child.reshape(noise.shape[1:]).astype(spectra_out.dtype)
        even_rows.append(jnp.where(is_odd, 0.0, child).astype(jnp.bfloat16))
        odd_rows.append(jnp.where(is_odd, child, 0.0).astype(jnp.bfloat16))
    store()
    result = jnp.dot(
        jnp.concatenate(even_rows, axis=0), even[...], preferred_element_type=jnp.float32
    )
    result += jnp.dot(
        jnp.concatenate(odd_rows, axis=0), odd[...], preferred_element_type=jnp.float32
    )
    fourier_out[...] = result.reshape(fourier_out.shape).astype(fourier_out.dtype)


def finish_kernel(first, block, waves, received, noise, even, odd, *rest):
    start = first + pl.program_id(0) * block
    nothing = lambda: None
    finish_block(start, waves, received, noise, even, odd, *rest[-2:], nothing, nothing)


def last_kernel(first, waves, received, noise, even, odd, *rest):
    spectra_out, fourier_out, noise_here, spectra_here, fourier_here, sems = rest[-6:]
    part = pl.ds(first, noise_here.shape[0])
    fetch = pltpu.make_async_copy(noise.at[part], noise_here, sems.at[0])
    leave = pltpu.make_async_copy(spectra_here, spectra_out.at[part], sems.at[1])
    leave_too = pltpu.make_async_copy(fourier_here, fourier_out.at[part], sems.at[2])
    fetch.start()
    finish_block(
        first,
        waves,
        received,
        noise_here,
        even,
        odd,
        spectra_here,
        fourier_here,
        fetch.wait,
        leave.start,
    )
    leave_too.start()
    leave.wait()
    leave_too.wait()


def last_transform(waves, first, received, noise, even, odd, outs):
    slots_all, mem_local, parts, fields, truncation = noise.shape
    latitudes = even.shape[1]
    all_rows = received.shape[1]
    block = all_rows // (mem_local * parts * fields)
    fourier_shape = noise.shape[:4] + (latitudes,)
    here = pl.BlockSpec(memory_space=pltpu.VMEM)
    anywhere = pl.BlockSpec(memory_space=pl.ANY)
    return pl.pallas_call(
        functools.partial(last_kernel, first),
        in_specs=[pl.BlockSpec(memory_space=pltpu.SMEM), here, anywhere, here, here]
        + [anywhere] * 2,
        out_specs=[anywhere, anywhere],
        out_shape=[
            jax.ShapeDtypeStruct(noise.shape, jnp.bfloat16),
            jax.ShapeDtypeStruct(fourier_shape, jnp.bfloat16),
        ],
        scratch_shapes=[
            pltpu.VMEM((block,) + noise.shape[1:], jnp.bfloat16),
            pltpu.VMEM((block,) + noise.shape[1:], jnp.bfloat16),
            pltpu.VMEM((block,) + fourier_shape[1:], jnp.bfloat16),
            pltpu.SemaphoreType.DMA((3,)),
        ],
        input_output_aliases={5: 0, 6: 1},
        compiler_params=pltpu.CompilerParams(vmem_limit_bytes=VMEM_BYTES),
        cost_estimate=pl.CostEstimate(
            flops=8 * all_rows * truncation * latitudes,
            bytes_accessed=2 * all_rows * (2 * truncation + 2 * latitudes) + 4 * even.size,
            transcendentals=0,
        ),
        name="last",
    )(waves, received, *in_hbm(noise), *in_vmem(even, odd), *in_hbm(*outs))


def finish_transform(waves, first, block, received, noise, even, odd, outs):
    slots_all, mem_local, parts, fields, truncation = noise.shape
    latitudes = even.shape[1]
    groups, all_rows, lat_local = received.shape
    per_slot = mem_local * parts * fields
    at = first // block
    far = lambda step, w: (at + step, 0, 0, 0, 0)
    table = pl.BlockSpec(even.shape, lambda step, w: (0, 0))
    noise_block = pl.BlockSpec((block,) + noise.shape[1:], far)
    fourier_shape = noise.shape[:4] + (latitudes,)
    fourier_block = pl.BlockSpec((block,) + fourier_shape[1:], far)
    received_block = pl.BlockSpec(
        (groups, block * per_slot, lat_local), lambda step, w: (0, step, 0)
    )
    return pl.pallas_call(
        functools.partial(finish_kernel, first, block),
        grid_spec=pltpu.PrefetchScalarGridSpec(
            num_scalar_prefetch=1,
            grid=(all_rows // (block * per_slot),),
            in_specs=[received_block, noise_block, table, table]
            + [pl.BlockSpec(memory_space=pl.ANY)] * 2,
            out_specs=[noise_block, fourier_block],
        ),
        out_shape=[
            jax.ShapeDtypeStruct(noise.shape, jnp.bfloat16),
            jax.ShapeDtypeStruct(fourier_shape, jnp.bfloat16),
        ],
        input_output_aliases={5: 0, 6: 1},
        compiler_params=pltpu.CompilerParams(vmem_limit_bytes=VMEM_BYTES),
        cost_estimate=pl.CostEstimate(
            flops=8 * all_rows * truncation * latitudes,
            bytes_accessed=2 * all_rows * (2 * truncation + 2 * latitudes) + 4 * even.size,
            transcendentals=0,
        ),
        name="finish",
    )(waves, *in_hbm(received, noise), *in_vmem(even, odd), *in_hbm(*outs))


def chunk_bounds(slots_here, block):
    blocks = slots_here // block
    edges = [0, (blocks * 5 + 10) // 11, (blocks * 10 + 10) // 11, blocks]
    edges = [edge * block for edge in edges]
    return [(start, stop) for start, stop in zip(edges[:-1], edges[1:]) if stop > start]


def per_device(velocity, tracer, wave_slots, parents, noise):
    lat_count = lax.axis_size("lat")
    lat_index = lax.axis_index("lat")
    mem_count = lax.axis_size("member")
    group_index = lax.axis_index("member")
    mem_local, fields, lat_local, longitudes = velocity.shape
    slots_here, truncation = noise.shape[0], noise.shape[-1]
    block = math.gcd(slots_here, 8)
    per_member = 2 * fields
    per_slot = mem_local * per_member
    latitudes = lat_count * lat_local
    own_waves = lax.dynamic_slice_in_dim(wave_slots, lat_index * slots_here, slots_here)
    first_member = group_index * mem_local
    own_parents = lax.dynamic_slice_in_dim(parents, first_member, mem_local)
    offsets = own_parents - first_member + SPREAD
    upward = [(i, i + 1) for i in range(mem_count - 1)]
    downward = [(target, source) for source, target in upward]
    slot_grid = wave_slots.reshape(lat_count, slots_here)
    bounds = chunk_bounds(slots_here, block)
    inner = min(lat_local, LANES)
    starts = jnp.arange(latitudes // inner, dtype=jnp.int32) * inner

    def zonal(at):
        start, stop = bounds[at]
        waves = slot_grid[:, start:stop].reshape(-1, 1)
        return zonal_transform(waves, truncation, velocity, tracer, [])

    def neighbours(rows, per_member):
        low = lax.ppermute(rows[:, rows.shape[1] - SPREAD * per_member :], "member", upward)
        high = lax.ppermute(rows[:, : SPREAD * per_member], "member", downward)
        return low, rows, high

    def exchanged(outgoing):
        outgoing = outgoing.reshape(lat_count, -1, lat_local)
        moved = lax.all_to_all(outgoing, "lat", split_axis=0, concat_axis=0, tiled=True)
        if lat_local % LANES != 0:
            moved = jnp.swapaxes(moved, 0, 1).reshape(1, -1, latitudes)
        return moved

    def copied(at, tokens):
        return copy_parents(offsets, *neighbours(zonal(at), per_member), tokens)

    received = exchanged(zonal(0))
    even, odd = meridional_tables(truncation, latitudes, starts, inner)
    later = [exchanged(copied(1, []))] if len(bounds) > 1 else []
    spectra, _ = forward_transform(
        (own_waves, per_member), 0, block, received, even, odd, mem_local, []
    )
    *outs, token = inverse_transform(
        own_waves, offsets, 0, block, *neighbours(spectra, 1), noise, even, odd, None
    )
    later += [exchanged(copied(at, [token])) for at in range(2, len(bounds))]
    for (start, stop), received in zip(bounds[1:], later):
        if stop - start == block:
            outs = last_transform(own_waves, start, received, noise, even, odd, outs)
        else:
            outs = finish_transform(own_waves, start, block, received, noise, even, odd, outs)
    return tuple(outs)


def solution(mesh):
    in_specs = (
        P("member", None, "lat", None),
        P("member", None, "lat", None),
        P(),
        P(),
        P("lat", "member", None, None, None),
    )
    out_specs = (P("lat", "member", None, None, None), P("lat", "member", None, None, None))
    return jax.shard_map(
        per_device, mesh=mesh, in_specs=in_specs, out_specs=out_specs, check_vma=False
    )
```
